32 devices in a mesh: dp: 16 (over z, y, x), mp: 2 (over core).
Axes of the slice: x: 2, y: 2, z: 4, core: 2. Of those that a mesh axis runs over, the one named last changes fastest.
Arguments:
- text: bfloat16 [192, 61, 768], P('dp'), may hold values from -6 to 6
- patches: bfloat16 [192, 145, 1024], P(('dp', 'mp')), may hold values from -6 to 6
- cotangent: bfloat16 [192, 61, 768], P('dp'), may hold values from -6 to 6
- region_counts: int32 [192], P('dp'), may hold values from 0 to 6, as said below
- phrase_starts: int32 [192, 6], P('dp'), may hold values from 0 to 60, as said below
- phrase_lengths: int32 [192, 6], P('dp'), may hold values from 1 to 8
- box_patches: int32 [192, 6, 16], P('dp'), may hold values from 0 to 144
- query_weight: bfloat16 [768, 768], P('dp', 'mp'), may hold values from -0.21875 to 0.21875
- key_weight: bfloat16 [768, 768], P('dp', 'mp'), may hold values from -0.21875 to 0.21875
- value_weight: bfloat16 [768, 768], P('dp', 'mp'), may hold values from -0.21875 to 0.21875
- attn_out_weight: bfloat16 [768, 768], P('mp', 'dp'), may hold values from -1.75 to 1.75
- cross_query_weight: bfloat16 [768, 768], P('dp', 'mp'), may hold values from -0.21875 to 0.21875
- cross_key_weight: bfloat16 [768, 768], P('dp', 'mp'), may hold values from -0.21875 to 0.21875
- cross_value_weight: bfloat16 [768, 768], P('dp', 'mp'), may hold values from -0.21875 to 0.21875
- cross_out_weight: bfloat16 [768, 768], P('mp', 'dp'), may hold values from -2.5 to 2.5
- image_weight: bfloat16 [1024, 768], P('dp'), may hold values from -0.1875 to 0.1875
- ffn_in_weight: bfloat16 [768, 3072], P('dp', 'mp'), may hold values from -0.21875 to 0.21875
- ffn_out_weight: bfloat16 [3072, 768], P('mp', 'dp'), may hold values from -0.109375 to 0.109375
- text_embed_weight: bfloat16 [768, 256], P('dp'), may hold values from -0.21875 to 0.21875
- image_embed_weight: bfloat16 [768, 256], P('dp'), may hold values from -0.21875 to 0.21875
- ln_attn_gain: bfloat16 [768], P('dp'), may hold values from 0.5 to 1.5
- ln_attn_bias: bfloat16 [768], P('dp'), may hold values from -1.1953125 to 1.1953125
- ln_cross_gain: bfloat16 [768], P('dp'), may hold values from 0.5 to 1.5
- ln_cross_bias: bfloat16 [768], P('dp'), may hold values from -1.1953125 to 1.1953125
- ln_ffn_gain: bfloat16 [768], P('dp'), may hold values from 0.5 to 1.5
- ln_ffn_bias: bfloat16 [768], P('dp'), may hold values from -1.1953125 to 1.1953125
Outputs:
- joined: bfloat16 [192, 61, 768], P('dp')
- text_grad: float32 [192, 61, 768], P('dp')
- patch_grad: float32 [192, 145, 1024], P(('dp', 'mp'))
- grad_query: float32 [768, 768], P('dp', 'mp')
- grad_key: float32 [768, 768], P('dp', 'mp')
- grad_value: float32 [768, 768], P('dp', 'mp')
- grad_attn_out: float32 [768, 768], P('mp', 'dp')
- grad_cross_query: float32 [768, 768], P('dp', 'mp')
- grad_cross_key: float32 [768, 768], P('dp', 'mp')
- grad_cross_value: float32 [768, 768], P('dp', 'mp')
- grad_cross_out: float32 [768, 768], P('mp', 'dp')
- grad_image: float32 [1024, 768], P('dp')
- grad_ffn_in: float32 [768, 3072], P('dp', 'mp')
- grad_ffn_out: float32 [3072, 768], P('mp', 'dp')
- grad_text_embed: float32 [768, 256], P('dp')
- grad_image_embed: float32 [768, 256], P('dp')
- grad_attn_gain: float32 [768], P('dp')
- grad_attn_bias: float32 [768], P('dp')
- grad_cross_gain: float32 [768], P('dp')
- grad_cross_bias: float32 [768], P('dp')
- grad_ffn_gain: float32 [768], P('dp')
- grad_ffn_bias: float32 [768], P('dp')
The draws below stay inside these ranges and needn't reach their ends.
Inputs may be any that keep to these rules, and one draw needn't show every extreme that they name: `region_counts`: some image has 6 boxed phrases and some has none. `phrase_starts`: each box's phrase ends within its caption: start + length <= 61.
All inputs are finite; a program needn't handle non-finite values.
Results may differ from the reference program's by a relative error of at most 0.022.
Values may be sent and summed in bfloat16 or wider, within the bound.
A program may use at most 192 MiB of HBM per device.

```python
import math
import jax
import jax.numpy as jnp
from jax import lax

D = 768
HEADS = 12
HEAD_DIM = 64
FF = 3072
DI = 1024
EMB = 256
PATCHES = 145
TEXT_LEN = 61
BOXES = 6
BOX_PATCHES = 16
SPAN_MOST = 8
PAIRS = 192


def span_table(key):
    base = jax.random.fold_in(key, 7)
    key_len, key_start, key_first, key_second = jax.random.split(base, 4)
    total = PAIRS * BOXES
    lengths = jax.random.randint(key_len, (total,), 1, SPAN_MOST + 1)
    first = jax.random.randint(key_first, (), 0, total)
    second = jax.random.randint(key_second, (), 0, total - 1)
    second = second + (second >= first).astype(jnp.int32)
    lengths = lengths.at[first].set(SPAN_MOST).at[second].set(1)
    starts = jax.random.randint(key_start, (total,), 0, TEXT_LEN - lengths + 1)
    starts = starts.at[second].set(TEXT_LEN - 1)
    return (starts.reshape(PAIRS, BOXES), lengths.reshape(PAIRS, BOXES))


def draw_phrase_starts(key, part):
    return span_table(key)[0]


def draw_phrase_lengths(key, part):
    return span_table(key)[1]


def draw_region_counts(key, part):
    key = jax.random.fold_in(key, 3)
    key_draw, key_full, key_empty = jax.random.split(key, 3)
    levels = jax.random.randint(key_draw, (PAIRS,), 0, 64)
    counts = jnp.zeros((PAIRS,), jnp.int32)
    for bound in (20, 36, 46, 53, 58, 62):
        counts = counts + (levels >= bound).astype(jnp.int32)
    counts = jnp.minimum(counts, BOXES)
    full_at = jax.random.randint(key_full, (), 0, PAIRS)
    empty_at = jax.random.randint(key_empty, (), 0, PAIRS - 1)
    empty_at = empty_at + (empty_at >= full_at).astype(jnp.int32)
    return counts.at[full_at].set(BOXES).at[empty_at].set(0)


def with_ends(entries, stream_key, smallest, top_value):
    longest = entries.shape.index(max(entries.shape))
    spots = []
    for shift in (0, 1):
        where = [jax.random.randint(jax.random.fold_in(stream_key, axis), (), 0, length) for axis, length in enumerate(entries.shape)]
        where[longest] = (where[longest] + shift) % entries.shape[longest]
        spots.append(tuple(where))
    return entries.at[spots[0]].set(smallest).at[spots[1]].set(top_value)


def block_levels(key, shape, shards, low, top_value):
    level, own = 1.0, jax.random.fold_in(key, 6)
    for dim, shards_of in shards:
        draws = jnp.exp(jax.random.uniform(jax.random.fold_in(own, dim), (shards_of,), jnp.float32, low / len(shards), top_value / len(shards)))
        level = level * jnp.repeat(draws, shape[dim] // shards_of).reshape([-1 if axis == dim else 1 for axis in range(len(shape))])
    return level


def noise(stream_key, extent, deviation, most, cuts=(), held_as=jnp.bfloat16):
    values = jax.random.normal(stream_key, extent, jnp.float32) * deviation
    if len(cuts) > 0:
        values = block_levels(stream_key, extent, cuts, -0.22, 0.18) * values
    return jnp.clip(values, min=-most, max=most).astype(held_as)


def setup_inputs(seed: int = 0) -> dict:
    key_list = jax.random.split(jax.random.key(seed), 27)
    text = noise(key_list[0], (PAIRS, TEXT_LEN, D), 1.0, 6.0, ((0, 16),))
    patches = noise(key_list[1], (PAIRS, PATCHES, DI), 1.0, 6.0, ((0, 32),))
    cotangent = noise(key_list[2], (PAIRS, TEXT_LEN, D), 1.0, 6.0, ((0, 16),))
    region_counts = draw_region_counts(jax.random.fold_in(key_list[26], 71), 0)
    phrase_starts = draw_phrase_starts(jax.random.fold_in(key_list[26], 71), 0)
    phrase_lengths = draw_phrase_lengths(jax.random.fold_in(key_list[26], 71), 0)
    box_patches = with_ends(jax.random.randint(key_list[6], (PAIRS, BOXES, BOX_PATCHES), 0, PATCHES), jax.random.fold_in(key_list[6], 1), 0, PATCHES - 1).astype(jnp.int32)
    query_weight = noise(key_list[7], (D, D), D ** -0.5, 0.21875, ((0, 16), (1, 2)))
    key_weight = noise(key_list[8], (D, D), D ** -0.5, 0.21875, ((0, 16), (1, 2)))
    value_weight = noise(key_list[9], (D, D), D ** -0.5, 0.21875, ((0, 16), (1, 2)))
    attn_out_weight = noise(key_list[10], (D, D), (D // TEXT_LEN) ** -0.5, 1.75, ((0, 2), (1, 16)))
    cross_query_weight = noise(key_list[11], (D, D), D ** -0.5, 0.21875, ((0, 16), (1, 2)))
    cross_key_weight = noise(key_list[12], (D, D), D ** -0.5, 0.21875, ((0, 16), (1, 2)))
    cross_value_weight = noise(key_list[13], (D, D), D ** -0.5, 0.21875, ((0, 16), (1, 2)))
    cross_out_weight = noise(key_list[14], (D, D), (D // PATCHES) ** -0.5, 2.5, ((0, 2), (1, 16)))
    image_weight = noise(key_list[15], (DI, D), DI ** -0.5, 0.1875, ((0, 16),))
    ffn_in_weight = noise(key_list[16], (D, FF), D ** -0.5, 0.21875, ((0, 16), (1, 2)))
    ffn_out_weight = noise(key_list[17], (FF, D), FF ** -0.5, 0.109375, ((0, 2), (1, 16)))
    text_embed_weight = noise(key_list[18], (D, EMB), D ** -0.5, 0.21875, ((0, 16),))
    image_embed_weight = noise(key_list[19], (D, EMB), D ** -0.5, 0.21875, ((0, 16),))
    ln_attn_gain = jnp.clip(1.0 + 0.1 * jax.random.normal(key_list[20], (D,), jnp.float32), 0.5, 1.5).astype(jnp.bfloat16)
    ln_attn_bias = noise(key_list[21], (D,), 0.3, 1.1953125, ((0, 16),))
    ln_cross_gain = jnp.clip(1.0 + 0.1 * jax.random.normal(key_list[22], (D,), jnp.float32), 0.5, 1.5).astype(jnp.bfloat16)
    ln_cross_bias = noise(key_list[23], (D,), 0.3, 1.1953125, ((0, 16),))
    ln_ffn_gain = jnp.clip(1.0 + 0.1 * jax.random.normal(key_list[24], (D,), jnp.float32), 0.5, 1.5).astype(jnp.bfloat16)
    ln_ffn_bias = noise(key_list[25], (D,), 0.3, 1.1953125, ((0, 16),))
    return {"text": text, "patches": patches, "cotangent": cotangent, "region_counts": region_counts, "phrase_starts": phrase_starts, "phrase_lengths": phrase_lengths, "box_patches": box_patches, "query_weight": query_weight, "key_weight": key_weight, "value_weight": value_weight, "attn_out_weight": attn_out_weight, "cross_query_weight": cross_query_weight, "cross_key_weight": cross_key_weight, "cross_value_weight": cross_value_weight, "cross_out_weight": cross_out_weight, "image_weight": image_weight, "ffn_in_weight": ffn_in_weight, "ffn_out_weight": ffn_out_weight, "text_embed_weight": text_embed_weight, "image_embed_weight": image_embed_weight, "ln_attn_gain": ln_attn_gain, "ln_attn_bias": ln_attn_bias, "ln_cross_gain": ln_cross_gain, "ln_cross_bias": ln_cross_bias, "ln_ffn_gain": ln_ffn_gain, "ln_ffn_bias": ln_ffn_bias}


EPS = 1e-06
TEMP_INVERSE = 20.0
HIGHEST = lax.Precision.HIGHEST

@jax.custom_vjp
def low(v):
    return lax.optimization_barrier(v.astype(jnp.bfloat16)).astype(jnp.float32)

@jax.custom_vjp
def low_back(v):
    return v

def low_keep(v):
    return (low(v), None)

def low_pass(kept, grad):
    return (grad,)

def back_keep(v):
    return (v, None)

def back_low(kept, grad):
    return (low(grad),)
low.defvjp(low_keep, low_pass)
low_back.defvjp(back_keep, back_low)

def project(inputs, weight):
    flat = inputs.reshape(-1, inputs.shape[-1])
    result = jnp.dot(flat, weight, precision=HIGHEST)
    return result.reshape(inputs.shape[:-1] + (weight.shape[1],))

def rounded(inputs, weight):
    return low_back(low(project(inputs, weight)))

def split_heads(flat):
    return flat.reshape(flat.shape[0], flat.shape[1], HEADS, HEAD_DIM)

def layer_norm(inputs, gain, shift):
    centred = inputs - lax.optimization_barrier(jnp.mean(inputs, -1, keepdims=True))
    inv_std = lax.rsqrt(lax.optimization_barrier(jnp.mean(centred * centred, -1, keepdims=True)) + EPS)
    return centred * inv_std * gain + shift

def attention(queries, key_heads, value_heads):
    factor = 1.0 / math.sqrt(HEAD_DIM)
    scores = low_back(jnp.einsum('gqhd,gkhd->ghqk', queries, key_heads, precision=HIGHEST) * factor)
    probs = low(jax.nn.softmax(scores, axis=-1))
    mixed = jnp.einsum('ghqk,gkhd->gqhd', probs, value_heads, precision=HIGHEST)
    mixed = low_back(low(mixed))
    return mixed.reshape(mixed.shape[0], mixed.shape[1], HEADS * HEAD_DIM)

def unit_rows(raw):
    return raw * lax.rsqrt(lax.optimization_barrier(jnp.sum(raw * raw, -1, keepdims=True)) + EPS)

def group_forward(params, text, patches, counts, starts, lengths, picks):
    query_w, key_w, value_w, attn_out_w, cross_query_w, cross_key_w, cross_value_w, cross_out_w, image_w, ffn_in_w, ffn_out_w, text_embed_w, image_embed_w, gain_one, bias_one, gain_two, bias_two, gain_three, bias_three = params
    image_feats = rounded(patches, image_w)
    queries = split_heads(rounded(text, query_w))
    key_heads = split_heads(rounded(text, key_w))
    value_heads = split_heads(rounded(text, value_w))
    first = text + low_back(project(attention(queries, key_heads, value_heads), attn_out_w))
    hidden_one = layer_norm(first, gain_one, bias_one)
    low_one = low(hidden_one)
    cross_queries = split_heads(rounded(low_one, cross_query_w))
    cross_keys = split_heads(rounded(image_feats, cross_key_w))
    cross_values = split_heads(rounded(image_feats, cross_value_w))
    second = hidden_one + low_back(project(attention(cross_queries, cross_keys, cross_values), cross_out_w))
    hidden_two = layer_norm(second, gain_two, bias_two)
    inner = low_back(project(low(hidden_two), ffn_in_w))
    active = low(jax.nn.gelu(inner, approximate=False))
    third = hidden_two + low_back(project(active, ffn_out_w))
    output = layer_norm(third, gain_three, bias_three)
    positions = jnp.arange(TEXT_LEN, dtype=jnp.int32)
    slots = jnp.arange(BOXES, dtype=jnp.int32)
    valid = (slots[None, :] < counts[:, None]).astype(jnp.float32)
    ends = starts + lengths
    inside = ((positions >= starts[..., None]) & (positions < ends[..., None])).astype(jnp.float32) * valid[..., None]
    span_weight = inside / lengths[..., None].astype(jnp.float32)
    chosen = lax.optimization_barrier(jnp.sum((picks[..., None] == jnp.arange(PATCHES, dtype=jnp.int32)).astype(jnp.float32), axis=2)) / BOX_PATCHES
    phrase = jnp.einsum('gbt,gtd->gbd', span_weight, output, precision=HIGHEST)
    region = jnp.einsum('gbn,gnd->gbd', chosen, image_feats, precision=HIGHEST)
    mismatch = (phrase - region) * valid[..., None]
    box_loss = 0.5 * jnp.sum(mismatch * mismatch)
    text_emb = low(unit_rows(jnp.dot(lax.optimization_barrier(jnp.mean(text, 1)), text_embed_w, precision=HIGHEST)))
    image_emb = low(unit_rows(jnp.dot(lax.optimization_barrier(jnp.mean(image_feats, 1)), image_embed_w, precision=HIGHEST)))
    return (output, box_loss, text_emb, image_emb)

def forward(params, text, patches, counts, starts, lengths, picks):
    group = math.gcd(PAIRS, 64)

    def split_groups(array):
        return array.reshape((PAIRS // group, group) + array.shape[1:])
    block = jax.checkpoint(lambda pieces: group_forward(params, *pieces))

    def scan_step(running, pieces):
        output, box_loss, text_emb, image_emb = block(pieces)
        return (running + box_loss, (output, text_emb, image_emb))
    inputs = tuple((split_groups(array) for array in (text, patches, counts, starts, lengths, picks)))
    box_total, (outputs, text_embs, image_embs) = lax.scan(scan_step, jnp.zeros((), jnp.float32), inputs)
    outputs = outputs.reshape(PAIRS, TEXT_LEN, D)
    text_embs = text_embs.reshape(PAIRS, EMB)
    image_embs = image_embs.reshape(PAIRS, EMB)
    logits = jnp.dot(text_embs, image_embs.T, precision=HIGHEST) * TEMP_INVERSE
    diagonal = jnp.diagonal(logits)
    contrast = 0.5 * (jnp.sum(jax.nn.logsumexp(logits, axis=1) - diagonal) + jnp.sum(jax.nn.logsumexp(logits, axis=0) - diagonal))
    return (outputs, box_total + contrast)

def reference(text, patches, cotangent, region_counts, phrase_starts, phrase_lengths, box_patches, query_weight, key_weight, value_weight, attn_out_weight, cross_query_weight, cross_key_weight, cross_value_weight, cross_out_weight, image_weight, ffn_in_weight, ffn_out_weight, text_embed_weight, image_embed_weight, ln_attn_gain, ln_attn_bias, ln_cross_gain, ln_cross_bias, ln_ffn_gain, ln_ffn_bias):
    params = tuple((weight.astype(jnp.float32) for weight in (query_weight, key_weight, value_weight, attn_out_weight, cross_query_weight, cross_key_weight, cross_value_weight, cross_out_weight, image_weight, ffn_in_weight, ffn_out_weight, text_embed_weight, image_embed_weight, ln_attn_gain, ln_attn_bias, ln_cross_gain, ln_cross_bias, ln_ffn_gain, ln_ffn_bias)))

    def objective(weights, text_vals, patch_vals):
        return forward(weights, text_vals, patch_vals, region_counts, phrase_starts, phrase_lengths, box_patches)
    (outputs, total), pullback = jax.vjp(objective, params, text.astype(jnp.float32), patches.astype(jnp.float32))
    grads, grad_text, grad_patches = pullback((cotangent.astype(jnp.float32), jnp.ones((), jnp.float32)))
    return (outputs.astype(jnp.bfloat16), grad_text, grad_patches, grads[0], grads[1], grads[2], grads[3], grads[4], grads[5], grads[6], grads[7], grads[8], grads[9], grads[10], grads[11], grads[12], grads[13], grads[14], grads[15], grads[16], grads[17], grads[18])
```

```python
import functools
import math

import jax
import jax.numpy as jnp
from jax import lax
from jax.experimental import pallas as pl
from jax.experimental.pallas import tpu as pltpu
from jax.sharding import PartitionSpec as P

HEAD_DIM = 64
EPS = 1e-06
TEMP_INVERSE = 20.0
GRAD_SCALE = 10.0
HIGHEST = lax.Precision.HIGHEST
MESH = pl.DeviceIdType.MESH
BF16 = jnp.bfloat16
F32 = jnp.float32


def split_dims(count):
    side = math.isqrt(count // 4) if count % 4 == 0 else 0
    if side and 4 * side * side == count:
        return (4, side, side)
    return (count, 1, 1)


class Place:
    def __init__(self, dims):
        self.dims = dims
        dp = lax.axis_index("dp")
        self.mp = lax.axis_index("mp")
        self.pos = (dp // (dims[1] * dims[2]), (dp // dims[2]) % dims[1], dp % dims[2])

    def at(self, axis, coord):
        spot = list(self.pos)
        spot[axis] = coord
        return ((spot[0] * self.dims[1] + spot[1]) * self.dims[2] + spot[2], self.mp)

    def peer(self):
        return (lax.axis_index("dp"), 1 - self.mp)


def block_of(place, order, stage, coord):
    index = [None] * 3
    for rank, axis in enumerate(order):
        index[axis] = slice(None) if rank < stage else (coord if rank == stage else place.pos[axis])
    return tuple(index)


def remote(src, dst, send_sem, recv_sem, device):
    return pltpu.make_async_remote_copy(
        src_ref=src,
        dst_ref=dst,
        send_sem=send_sem,
        recv_sem=recv_sem,
        device_id=device,
        device_id_type=MESH,
    )


def greet_lines(place):
    sem = pltpu.get_barrier_semaphore()

    def greet(device):
        pl.semaphore_signal(sem, inc=1, device_id=device, device_id_type=MESH)

    greet(place.peer())
    count = 1
    for axis in range(3):
        for away in range(1, place.dims[axis]):
            greet(place.at(axis, lax.rem(place.pos[axis] + away, place.dims[axis])))
            count += 1
    pl.semaphore_wait(sem, count)


def gather_steps(place, order, buf, send_sem, recv_sem):
    sent = []
    for stage, axis in enumerate(order):
        length, pos = place.dims[axis], place.pos[axis]
        if length == 1:
            continue

        def copy(way, step, coord, stage=stage, axis=axis, pos=pos):
            ref = buf.at[block_of(place, order, stage, coord)]
            device = place.at(axis, pos + 1 if way == 0 else pos - 1)
            return remote(ref, ref, send_sem.at[axis, way, step - 1], recv_sem.at[axis, way, step - 1], device)

        for step in range(1, length + 1):
            for way in (0, 1):
                coord = pos - (step - 1) if way == 0 else pos + (step - 1)
                here = (coord >= 0) if way == 0 else (coord < length)
                if step > 1:
                    pl.when(here)(lambda: copy(way, step - 1, coord).wait_recv())
                if step < length:
                    more = jnp.logical_and(here, (pos + 1 < length) if way == 0 else (pos > 0))
                    pl.when(more)(lambda: copy(way, step, coord).start())
                    sent.append((more, functools.partial(copy, way, step, coord)))
            if step < length:
                yield
    return sent


def scatter_steps(place, order, acc, arrive, send_sem, recv_sem, result):
    sent = []
    last = [axis for axis in order if place.dims[axis] > 1][0]
    at = 0
    for stage in reversed(range(3)):
        axis = order[stage]
        length, pos = place.dims[axis], place.pos[axis]
        if length == 1:
            continue
        units = math.prod(place.dims[a] for a in order[:stage])
        shape = tuple(place.dims[a] for a in sorted(order[:stage]))

        def copy(way, step, coord, stage=stage, axis=axis, pos=pos, at=at, units=units, length=length, shape=shape):
            src = acc.at[block_of(place, order, stage, coord)]
            slot = at + (way * (length - 1) + step - 1) * units
            dst = arrive.at[pl.ds(slot, units)].reshape(*shape, *arrive.shape[1:])
            device = place.at(axis, pos + 1 if way == 0 else pos - 1)
            return (
                remote(src, dst, send_sem.at[axis, way, step - 1], recv_sem.at[axis, way, step - 1], device),
                dst,
            )

        for step in range(length - 1, 0, -1):
            for way in (0, 1):
                coord = pos + step if way == 0 else pos - step
                has = (coord < length) if way == 0 else (coord >= 0)
                pl.when(has)(lambda: copy(way, step, coord)[0].start())
                sent.append((has, functools.partial(lambda move, *a: move(*a)[0], copy, way, step, coord)))
            yield
            for way in (0, 1):
                coord = pos - 1 + step if way == 0 else pos + 1 - step
                comes = jnp.logical_and(pos > 0, coord < length) if way == 0 else jnp.logical_and(pos < length - 1, coord >= 0)

                def take():
                    move, ref = copy(way, step, coord)
                    move.wait_recv()
                    index = block_of(place, order, stage, coord)
                    total = acc[index].astype(F32) + ref[...].astype(F32)
                    if axis == last and step == 1:
                        result[...] = total
                    acc[index] = total.astype(BF16)

                pl.when(comes)(take)
        at += 2 * (length - 1) * units
    return sent


def arrive_units(dims, order):
    units = 0
    for stage in range(3):
        if dims[order[stage]] > 1:
            units += 2 * (dims[order[stage]] - 1) * math.prod(dims[a] for a in order[:stage])
    return units


def in_turn(plan):
    events = sorted((time, which, step) for which, (times, _) in enumerate(plan) for step, time in enumerate(times))
    results = [None] * len(plan)
    for _, which, _ in events:
        if results[which] is None:
            try:
                next(plan[which][1])
            except StopIteration as stop:
                results[which] = stop.value
    assert all(r is not None for r in results)
    return results


def wait_sent(sent):
    for cond, make in sent:
        if cond is None:
            make().wait_send()
        else:
            pl.when(cond)(lambda: make().wait_send())


ORDERS = ((2, 0, 1), (1, 0, 2), (0, 2, 1), (2, 0, 1), (1, 0, 2), (0, 1, 2))


def step_times(dims, order, start, back=False):
    times = [0.0]
    units = 1
    for axis in order:
        for _ in range(dims[axis] - 1):
            times.append(times[-1] + 1.6 * units + 3.0)
        units *= dims[axis]
    times.append(times[-1] + 4.0)
    if back:
        times = [times[-1] - t for t in reversed(times)]
    return [start + t for t in times] + [start + times[-1] + 4.0, start + times[-1] + 8.0]


def gather_kernel(dims, count, *refs):
    ins, outs = refs[:count], refs[count : 2 * count]
    send_sem, recv_sem, own_sem, peer_send, peer_recv = refs[2 * count :]
    place = Place(dims)
    own = [
        pltpu.make_async_copy(ins[c], outs[c].at[(place.mp,) + place.pos], own_sem.at[c]) for c in range(count)
    ]
    for copy in own:
        copy.start()
    greet_lines(place)

    def chunk(c, order):
        own[c].wait()
        mine, other = outs[c].at[place.mp], outs[c].at[1 - place.mp]
        sent = yield from gather_steps(place, order, mine, send_sem.at[c], recv_sem.at[c])

        def copy(ref):
            return remote(ref, ref, peer_send.at[c], peer_recv.at[c], place.peer())

        copy(mine).start()
        yield
        copy(other).wait_recv()
        return sent + [(None, lambda: copy(mine))]

    plan = []
    for c in range(count):
        order = ORDERS[c % len(ORDERS)]
        plan.append((step_times(dims, order, 3.9 * c), chunk(c, order)))
    for sent in in_turn(plan):
        wait_sent(sent)


def gather(shards, dims):
    count = len(shards)
    longest = max(max(dims) - 1, 1)
    return pl.pallas_call(
        functools.partial(gather_kernel, dims, count),
        out_shape=[jax.ShapeDtypeStruct((2,) + dims + s.shape, BF16) for s in shards],
        in_specs=[pl.BlockSpec(memory_space=pl.ANY)] * count,
        out_specs=[pl.BlockSpec(memory_space=pl.ANY)] * count,
        scratch_shapes=[pltpu.SemaphoreType.DMA((count, 3, 2, longest))] * 2 + [pltpu.SemaphoreType.DMA((count,))] * 3,
        compiler_params=pltpu.CompilerParams(collective_id=0, has_side_effects=True),
        name="gather_weights",
    )(*shards)


def scatter_kernel(dims, count, shared, extra, *refs):
    ins, pieces = refs[:count], refs[count : count + extra]
    refs = refs[count + extra :]
    outs, wholes = refs[:count], refs[count : count + extra]
    refs = refs[count + extra :]
    acc, peer_in, arrive = refs[:count], refs[count : 2 * count], refs[2 * count : 3 * count]
    send_sem, recv_sem, own_sem, peer_send, peer_recv, end_send, end_recv, ex_own, ex_send, ex_recv = refs[3 * count :]
    place = Place(dims)
    own = [pltpu.make_async_copy(ins[c].at[place.mp], acc[c], own_sem.at[c]) for c in range(count)]
    for copy in own:
        copy.start()
    keep = [pltpu.make_async_copy(pieces[e], wholes[e].at[place.mp], ex_own.at[e]) for e in range(extra)]
    for copy in keep:
        copy.start()
    greet_lines(place)
    give = [
        remote(pieces[e], wholes[e].at[place.mp], ex_send.at[e], ex_recv.at[e], place.peer()) for e in range(extra)
    ]

    def chunk(c, order):
        def copy():
            return remote(ins[c].at[1 - place.mp], peer_in[c], peer_send.at[c], peer_recv.at[c], place.peer())

        copy().start()
        yield
        own[c].wait()
        copy().wait_recv()
        acc[c][...] = (acc[c][...].astype(F32) + peer_in[c][...].astype(F32)).astype(BF16)
        result = outs[c].at[place.mp] if c in shared else outs[c]
        sent = yield from scatter_steps(
            place, order, acc[c], arrive[c], send_sem.at[c], recv_sem.at[c], result
        )
        sent.append((None, copy))
        if c in shared:

            def hand(half):
                ref = outs[c].at[half]
                return remote(ref, ref, end_send.at[c], end_recv.at[c], place.peer())

            hand(place.mp).start()
            yield
            hand(1 - place.mp).wait_recv()
            sent.append((None, lambda: hand(place.mp)))
        return sent

    plan = []
    for c in range(count):
        order = ORDERS[c % len(ORDERS)]
        plan.append((step_times(dims, order, 3.9 * c, True), chunk(c, order)))
    for copy in give:
        copy.start()
    for sent in in_turn(plan):
        wait_sent(sent)
    for copy in keep:
        copy.wait()
    for copy in give:
        copy.wait()


def scatter(grads, shared, pieces, dims):
    count, extra = len(grads), len(pieces)
    longest = max(max(dims) - 1, 1)
    shapes = [
        jax.ShapeDtypeStruct(((2,) if c in shared else ()) + g.shape[-2:], F32) for c, g in enumerate(grads)
    ]
    wholes = [jax.ShapeDtypeStruct((2,) + p.shape, p.dtype) for p in pieces]
    return pl.pallas_call(
        functools.partial(scatter_kernel, dims, count, shared, extra),
        out_shape=shapes + wholes,
        in_specs=[pl.BlockSpec(memory_space=pl.ANY)] * (count + extra),
        out_specs=[pl.BlockSpec(memory_space=pltpu.VMEM)] * count + [pl.BlockSpec(memory_space=pl.ANY)] * extra,
        scratch_shapes=[pltpu.VMEM(g.shape[1:], BF16) for g in grads] * 2
        + [
            pltpu.VMEM((arrive_units(dims, ORDERS[c % len(ORDERS)]),) + g.shape[-2:], BF16)
            for c, g in enumerate(grads)
        ]
        + [pltpu.SemaphoreType.DMA((count, 3, 2, longest))] * 2
        + [pltpu.SemaphoreType.DMA((count,))] * 5
        + [pltpu.SemaphoreType.DMA((extra,))] * 3,
        compiler_params=pltpu.CompilerParams(
            collective_id=1, has_side_effects=True, vmem_limit_bytes=60 * 2**20
        ),
        name="scatter_gradients",
    )(*grads, *pieces)


def matmul(left, right):
    return jnp.dot(left, right, preferred_element_type=F32)


def contract_rows(left, right):
    return lax.dot_general(left, right, (((0,), (0,)), ((), ())), preferred_element_type=F32)


def contract_cols(left, right):
    return lax.dot_general(left, right, (((1,), (1,)), ((), ())), preferred_element_type=F32)


def layer_norm(inputs, gain, shift):
    centred = inputs - jnp.mean(inputs, -1, keepdims=True)
    inv_std = lax.rsqrt(jnp.mean(centred * centred, -1, keepdims=True) + EPS)
    normed = centred * inv_std
    return (normed * gain + shift, normed, inv_std)


def norm_back(upstream, normed, inv_std, gain):
    scaled = upstream * gain
    inner_mean = jnp.mean(scaled * normed, -1, keepdims=True)
    result = inv_std * (scaled - jnp.mean(scaled, -1, keepdims=True) - normed * inner_mean)
    return (result, jnp.sum(upstream * normed, 0), jnp.sum(upstream, 0))


def split_heads(flat, pair_count):
    return flat.reshape(pair_count, -1, flat.shape[-1] // HEAD_DIM, HEAD_DIM)


def attend(queries, key_heads, value_heads):
    factor = 1.0 / math.sqrt(HEAD_DIM)
    scores = jnp.einsum("pqhd,pkhd->phqk", queries, key_heads, preferred_element_type=F32) * factor
    row_max = jnp.max(scores, -1, keepdims=True)
    expd = jnp.exp(scores - row_max)
    row_sum = jnp.sum(expd, -1, keepdims=True)
    probs = (expd / row_sum).astype(BF16)
    mixed = jnp.einsum("phqk,pkhd->pqhd", probs, value_heads, preferred_element_type=F32)
    flat_rows = queries.shape[0] * queries.shape[1]
    return (mixed.astype(BF16).reshape(flat_rows, -1), row_max + jnp.log(row_sum))


def attend_back(queries, key_heads, value_heads, log_total, upstream):
    factor = 1.0 / math.sqrt(HEAD_DIM)
    scores = jnp.einsum("pqhd,pkhd->phqk", queries, key_heads, preferred_element_type=F32) * factor
    probs = jnp.exp(scores - log_total)
    dprobs = jnp.einsum("pqhd,pkhd->phqk", upstream, value_heads, preferred_element_type=F32)
    dscores = (probs * (dprobs - jnp.sum(dprobs * probs, -1, keepdims=True))).astype(BF16)
    dqueries = jnp.einsum("phqk,pkhd->pqhd", dscores, key_heads, preferred_element_type=F32) * factor
    dkeys = jnp.einsum("phqk,pqhd->pkhd", dscores, queries, preferred_element_type=F32) * factor
    dvalues = jnp.einsum("phqk,pqhd->pkhd", probs.astype(BF16), upstream, preferred_element_type=F32)
    return tuple(t.astype(BF16).reshape(-1, t.shape[2] * t.shape[3]) for t in (dqueries, dkeys, dvalues))


def unit_back(raw, inv_norm, upstream):
    cubed = inv_norm * inv_norm * inv_norm
    return inv_norm * upstream - raw * cubed * jnp.sum(raw * upstream, -1, keepdims=True)


def contrast(text_pool, image_pool, text_embed32, image_embed32):
    text_raw = jnp.dot(text_pool, text_embed32, precision=HIGHEST)
    text_inv = lax.rsqrt(jnp.sum(text_raw * text_raw, -1, keepdims=True) + EPS)
    image_raw = jnp.dot(image_pool, image_embed32, precision=HIGHEST)
    image_inv = lax.rsqrt(jnp.sum(image_raw * image_raw, -1, keepdims=True) + EPS)
    both = jnp.concatenate([(text_raw * text_inv).astype(BF16), (image_raw * image_inv).astype(BF16)], 1)
    width = text_raw.shape[1]
    everyone = lax.all_gather(both, ("dp", "mp"), axis=0, tiled=True)
    text_all, image_all = everyone[:, :width], everyone[:, width:]
    logits = contract_cols(text_all, image_all) * TEMP_INVERSE
    weights = jnp.exp(logits - jax.nn.logsumexp(logits, axis=1, keepdims=True)) + jnp.exp(
        logits - jax.nn.logsumexp(logits, axis=0, keepdims=True)
    )
    weights = weights - 2.0 * jnp.eye(logits.shape[0], dtype=F32)
    count = text_pool.shape[0]
    start = (lax.axis_index("dp") * 2 + lax.axis_index("mp")) * count
    rows = lax.dynamic_slice_in_dim(weights, start, count, 0)
    columns = lax.dynamic_slice_in_dim(weights, start, count, 1)
    dtext = GRAD_SCALE * jnp.dot(rows, image_all.astype(F32), precision=HIGHEST)
    dimage = GRAD_SCALE * jnp.dot(columns.T, text_all.astype(F32), precision=HIGHEST)
    dtext_raw = unit_back(text_raw, text_inv, dtext)
    dimage_raw = unit_back(image_raw, image_inv, dimage)
    return (
        jnp.dot(text_pool.T, dtext_raw, precision=HIGHEST),
        jnp.dot(image_pool.T, dimage_raw, precision=HIGHEST),
        jnp.dot(dtext_raw, text_embed32.T, precision=HIGHEST),
        jnp.dot(dimage_raw, image_embed32.T, precision=HIGHEST),
    )


def pad_rows(x, rows):
    return jnp.pad(x, ((0, rows - x.shape[0]), (0, 0)))


def body(
    text,
    patches,
    cotangent,
    region_counts,
    phrase_starts,
    phrase_lengths,
    box_patches,
    query_weight,
    key_weight,
    value_weight,
    attn_out_weight,
    cross_query_weight,
    cross_key_weight,
    cross_value_weight,
    cross_out_weight,
    image_weight,
    ffn_in_weight,
    ffn_out_weight,
    text_embed_weight,
    image_embed_weight,
    *norm_shards,
):
    dp = lax.axis_size("dp")
    dims = split_dims(dp)
    mp = lax.axis_index("mp")
    half_pairs, patch_count, _ = patches.shape
    length, model_width = text.shape[1:]
    half = query_weight.shape[1]
    rows = query_weight.shape[0]
    hidden_blocks = ffn_in_weight.shape[1] // half
    embed_half = text_embed_weight.shape[1] // 2
    image_rows_own = image_weight.shape[0]

    def own_half(x, size, dim):
        return lax.dynamic_slice_in_dim(x, mp * size, size, dim)

    text, cotangent = own_half(text, half_pairs, 0), own_half(cotangent, half_pairs, 0)
    region_counts, phrase_starts = own_half(region_counts, half_pairs, 0), own_half(phrase_starts, half_pairs, 0)
    phrase_lengths, box_patches = own_half(phrase_lengths, half_pairs, 0), own_half(box_patches, half_pairs, 0)

    padded = -(-rows // 16) * 16
    small = jnp.concatenate(
        [own_half(text_embed_weight, embed_half, 1), own_half(image_embed_weight, embed_half, 1)]
        + [jnp.pad(jnp.stack(norm_shards, 1), ((0, 0), (0, half - 2 * embed_half - len(norm_shards))))],
        1,
    )
    ffn_out_t = ffn_out_weight.T
    shards = [
        own_half(image_weight, half, 1),
        query_weight,
        key_weight,
        value_weight,
        attn_out_weight.T,
        small,
        cross_key_weight,
        cross_value_weight,
        cross_query_weight,
        cross_out_weight.T,
        *(ffn_in_weight[:, k * half : (k + 1) * half] for k in range(hidden_blocks)),
        *(ffn_out_t[:, k * half : (k + 1) * half] for k in range(hidden_blocks)),
    ]
    real = [s.shape[0] for s in shards]
    shards = [pad_rows(s, -(-s.shape[0] // 16) * 16) for s in shards]
    gathered = gather(shards, dims)

    def merge(g, n):
        g = g.reshape(2, dp, *g.shape[-2:])[:, :, :n]
        return g.reshape(2, dp * n, g.shape[-1])

    gathered = [merge(g, n) for g, n in zip(gathered, real)]

    def columns(g):
        return jnp.concatenate([g[0], g[1]], 1)

    def blocks(gs):
        return jnp.concatenate([g[0] for g in gs] + [g[1] for g in gs], 1)

    image_w, query_w, key_w, value_w, attn_out_t = (columns(g) for g in gathered[:5])
    embeds = gathered[5]
    text_embed32 = columns(embeds[:, :, :embed_half]).astype(F32)
    image_embed32 = columns(embeds[:, :, embed_half : 2 * embed_half]).astype(F32)
    norms = embeds[0, :, 2 * embed_half : 2 * embed_half + len(norm_shards)].astype(F32).T
    gain_one, bias_one, gain_two, bias_two, gain_three, bias_three = (norms[k] for k in range(6))
    cross_key_w, cross_value_w, cross_query_w, cross_out_t = (columns(g) for g in gathered[6:10])
    ffn_in_w = blocks(gathered[10 : 10 + hidden_blocks])
    ffn_out_tw = blocks(gathered[10 + hidden_blocks :])

    text_rows = text.reshape(half_pairs * length, model_width)
    patch_rows = patches.reshape(half_pairs * patch_count, -1)
    image_rows = matmul(patch_rows, image_w).astype(BF16)
    image32 = image_rows.astype(F32).reshape(half_pairs, patch_count, model_width)
    queries = split_heads(matmul(text_rows, query_w).astype(BF16), half_pairs)
    key_heads = split_heads(matmul(text_rows, key_w).astype(BF16), half_pairs)
    value_heads = split_heads(matmul(text_rows, value_w).astype(BF16), half_pairs)
    self_mixed, self_total = attend(queries, key_heads, value_heads)
    first = text_rows.astype(F32) + contract_cols(self_mixed, attn_out_t)
    hidden_one, normed_one, inv_one = layer_norm(first, gain_one, bias_one)
    low_one = hidden_one.astype(BF16)
    cross_queries = split_heads(matmul(low_one, cross_query_w).astype(BF16), half_pairs)
    cross_keys = split_heads(matmul(image_rows, cross_key_w).astype(BF16), half_pairs)
    cross_values = split_heads(matmul(image_rows, cross_value_w).astype(BF16), half_pairs)
    cross_mixed, cross_total = attend(cross_queries, cross_keys, cross_values)
    second = hidden_one + contract_cols(cross_mixed, cross_out_t)
    hidden_two, normed_two, inv_two = layer_norm(second, gain_two, bias_two)
    low_two = hidden_two.astype(BF16)
    inner = matmul(low_two, ffn_in_w)
    active = jax.nn.gelu(inner, approximate=False).astype(BF16)
    third = hidden_two + contract_cols(active, ffn_out_tw)
    output, normed_three, inv_three = layer_norm(third, gain_three, bias_three)
    output3 = output.reshape(half_pairs, length, model_width)
    joined = output3.astype(BF16)

    text_pool = jnp.mean(text.astype(F32), 1)
    image_pool = jnp.mean(image32, 1)
    grad_text_embed, grad_image_embed, text_extra, image_pool_grad = contrast(
        text_pool, image_pool, text_embed32, image_embed32
    )
    text_extra = (text_extra / length)[:, None, :]
    image_pool_grad = image_pool_grad / patch_count
    positions = jnp.arange(length, dtype=jnp.int32)
    slots = jnp.arange(phrase_starts.shape[1], dtype=jnp.int32)
    valid = (slots[None, :] < region_counts[:, None]).astype(F32)
    ends = phrase_starts + phrase_lengths
    inside = ((positions >= phrase_starts[..., None]) & (positions < ends[..., None])).astype(F32) * valid[..., None]
    span_weight = inside / phrase_lengths[..., None].astype(F32)
    chosen = (
        jnp.sum((box_patches[..., None] == jnp.arange(patch_count, dtype=jnp.int32)).astype(F32), axis=2)
        / box_patches.shape[2]
    )
    phrase = jnp.einsum("pbt,ptd->pbd", span_weight, output3, precision=HIGHEST)
    region = jnp.einsum("pbn,pnd->pbd", chosen, image32, precision=HIGHEST)
    mismatch = (phrase - region) * valid[..., None]
    box_text = jnp.einsum("pbt,pbd->ptd", span_weight, mismatch, precision=HIGHEST)
    box_image = -jnp.einsum("pbn,pbd->pnd", chosen, mismatch, precision=HIGHEST)
    image_extra = (box_image + image_pool_grad[:, None, :]).reshape(-1, model_width)

    upstream = cotangent.astype(F32).reshape(-1, model_width) + box_text.reshape(-1, model_width)
    grad_third, gain_three_grad, bias_three_grad = norm_back(upstream, normed_three, inv_three, gain_three)
    low_third = grad_third.astype(BF16)
    grad_ffn_out_t = contract_rows(low_third, active)
    dactive = matmul(low_third, ffn_out_tw)
    gelu_pull = jax.vjp(lambda values: jax.nn.gelu(values, approximate=False), inner)[1]
    dinner = gelu_pull(dactive)[0].astype(BF16)
    grad_ffn_in = contract_rows(low_two, dinner)
    grad_second = grad_third + contract_cols(dinner, ffn_in_w)
    grad_second, gain_two_grad, bias_two_grad = norm_back(grad_second, normed_two, inv_two, gain_two)
    low_second = grad_second.astype(BF16)
    grad_cross_out_t = contract_rows(low_second, cross_mixed)
    dcross = split_heads(matmul(low_second, cross_out_t).astype(BF16), half_pairs)
    dqueries, dkeys, dvalues = attend_back(cross_queries, cross_keys, cross_values, cross_total, dcross)
    grad_cross_query = contract_rows(low_one, dqueries)
    grad_first = grad_second + contract_cols(dqueries, cross_query_w)
    grad_cross_key = contract_rows(image_rows, dkeys)
    grad_cross_value = contract_rows(image_rows, dvalues)
    dimage = contract_cols(dkeys, cross_key_w) + contract_cols(dvalues, cross_value_w) + image_extra
    low_image = dimage.astype(BF16)
    grad_image = contract_rows(patch_rows, low_image)
    patch_grad = contract_cols(low_image, image_w).reshape(patches.shape)
    grad_first, gain_one_grad, bias_one_grad = norm_back(grad_first, normed_one, inv_one, gain_one)
    low_first = grad_first.astype(BF16)
    grad_attn_out_t = contract_rows(low_first, self_mixed)
    dself = split_heads(matmul(low_first, attn_out_t).astype(BF16), half_pairs)
    dqueries, dkeys, dvalues = attend_back(queries, key_heads, value_heads, self_total, dself)
    grad_query = contract_rows(text_rows, dqueries)
    grad_key = contract_rows(text_rows, dkeys)
    grad_value = contract_rows(text_rows, dvalues)
    dtext = contract_cols(dqueries, query_w) + contract_cols(dkeys, key_w) + contract_cols(dvalues, value_w)
    text_grad = (grad_first + dtext).reshape(half_pairs, length, model_width) + text_extra

    def halves(g):
        g = g.astype(BF16)
        return jnp.stack([g[:, :half], g[:, half:]], 0)

    def hidden_halves(g):
        g = g.astype(BF16)
        return [
            jnp.stack([g[:, k * half : (k + 1) * half], g[:, (hidden_blocks + k) * half : (hidden_blocks + k + 1) * half]])
            for k in range(hidden_blocks)
        ]

    norm_grads = jnp.stack(
        [gain_one_grad, bias_one_grad, gain_two_grad, bias_two_grad, gain_three_grad, bias_three_grad], 1
    ).astype(BF16)
    norm_grads = jnp.pad(norm_grads, ((0, 0), (0, half - 2 * embed_half - len(norm_shards))))
    text_half, image_half = grad_text_embed.astype(BF16), grad_image_embed.astype(BF16)
    small_grads = jnp.stack(
        [
            jnp.concatenate(
                [text_half[:, k * embed_half : (k + 1) * embed_half], image_half[:, k * embed_half : (k + 1) * embed_half], norm_grads], 1
            )
            for k in range(2)
        ]
    )
    grads = [
        *hidden_halves(grad_ffn_out_t),
        *hidden_halves(grad_ffn_in),
        halves(grad_cross_out_t),
        halves(grad_cross_query),
        halves(grad_cross_key),
        halves(grad_cross_value),
        halves(grad_image),
        halves(grad_attn_out_t),
        halves(grad_query),
        halves(grad_key),
        halves(grad_value),
        small_grads,
    ]
    shared = (2 * hidden_blocks + 4, len(grads) - 1)

    def cut(g):
        n = g.shape[1] // dp
        g = g.reshape(2, dp, n, g.shape[-1])
        g = jnp.pad(g, ((0, 0), (0, 0), (0, -(-n // 16) * 16 - n), (0, 0)))
        return g.reshape(2, *dims, *g.shape[-2:])

    results = scatter([cut(g) for g in grads], shared, (joined, text_grad), dims)
    joined_all, text_grad_all = (r.reshape(2 * half_pairs, length, model_width) for r in results[len(grads) :])
    sums = [r[..., :n, :] for r, n in zip(results, [g.shape[1] // dp for g in grads])]
    ffn_out_own = jnp.concatenate(sums[:hidden_blocks], 1).T
    ffn_in_own = jnp.concatenate(sums[hidden_blocks : 2 * hidden_blocks], 1)
    cross_out_own, cross_query_own, cross_key_own, cross_value_own, image_own, attn_out_own, query_own, key_own, value_own, small_own = sums[2 * hidden_blocks :]
    own_norm = lax.dynamic_index_in_dim(small_own, mp, 0, keepdims=False)[:, 2 * embed_half :]
    return (
        joined_all,
        text_grad_all,
        patch_grad,
        query_own,
        key_own,
        value_own,
        attn_out_own.T,
        cross_query_own,
        cross_key_own,
        cross_value_own,
        cross_out_own.T,
        jnp.concatenate([image_own[0], image_own[1]], 1),
        ffn_in_own,
        ffn_out_own,
        jnp.concatenate([small_own[0, :, :embed_half], small_own[1, :, :embed_half]], 1),
        jnp.concatenate([small_own[0, :, embed_half : 2 * embed_half], small_own[1, :, embed_half : 2 * embed_half]], 1),
        own_norm[:, 0],
        own_norm[:, 1],
        own_norm[:, 2],
        own_norm[:, 3],
        own_norm[:, 4],
        own_norm[:, 5],
    )


def solution(mesh):
    pairs, weight, turned, single = P("dp", None, None), P("dp", "mp"), P("mp", "dp"), P("dp", None)
    weights = (weight, weight, weight, turned, weight, weight, weight, turned, single, weight, turned, single, single)
    norms = (P("dp"),) * 6
    halves = P(("dp", "mp"), None, None)
    in_specs = (pairs, halves, pairs, P("dp"), single, single, pairs) + weights + norms
    out_specs = (pairs, pairs, halves) + weights + norms
    return jax.shard_map(body, mesh=mesh, in_specs=in_specs, out_specs=out_specs, check_vma=False)
```

```python
import functools
import math
import types

import jax
import jax.numpy as jnp
from jax import lax
from jax.experimental import pallas as pl
from jax.experimental.pallas import tpu as pltpu
from jax.sharding import PartitionSpec as P

HEAD_DIM = 64
EPS = 1e-06
TEMP_INVERSE = 20.0
GRAD_SCALE = 10.0
HIGHEST = lax.Precision.HIGHEST
MESH = pl.DeviceIdType.MESH
BF16 = jnp.bfloat16
F32 = jnp.float32


def split_dims(count):
    side = math.isqrt(count // 4) if count % 4 == 0 else 0
    if side and 4 * side * side == count:
        return (4, side, side)
    return (count, 1, 1)


class Place:
    def __init__(self, dims):
        self.dims = dims
        dp = lax.axis_index("dp")
        self.mp = lax.axis_index("mp")
        self.pos = (dp // (dims[1] * dims[2]), (dp // dims[2]) % dims[1], dp % dims[2])

    def at(self, axis, coord):
        spot = list(self.pos)
        spot[axis] = coord
        return ((spot[0] * self.dims[1] + spot[1]) * self.dims[2] + spot[2], self.mp)

    def peer(self):
        return (lax.axis_index("dp"), 1 - self.mp)


def block_of(place, order, stage, coord):
    index = [None] * 3
    for rank, axis in enumerate(order):
        index[axis] = slice(None) if rank < stage else (coord if rank == stage else place.pos[axis])
    return tuple(index)


def remote(src, dst, send_sem, recv_sem, device):
    return pltpu.make_async_remote_copy(
        src_ref=src,
        dst_ref=dst,
        send_sem=send_sem,
        recv_sem=recv_sem,
        device_id=device,
        device_id_type=MESH,
    )


def greet_lines(place):
    sem = pltpu.get_barrier_semaphore()

    def greet(device):
        pl.semaphore_signal(sem, inc=1, device_id=device, device_id_type=MESH)

    greet(place.peer())
    count = 1
    for axis in range(3):
        for away in range(1, place.dims[axis]):
            greet(place.at(axis, lax.rem(place.pos[axis] + away, place.dims[axis])))
            count += 1
    pl.semaphore_wait(sem, count)


def line_slots(length):
    return (2 if length > 2 else 1) * (length - 1)


def line_slot(dims, axis, way, step):
    length = dims[axis]
    return sum(line_slots(d) for d in dims[:axis]) + (way * (length - 1) if length > 2 else 0) + step - 1


def send_slots(dims):
    return sum(line_slots(d) for d in dims)


def gather_slots(dims):
    return sum(d - 1 for d in dims)


def gather_steps(place, order, buf, send_sem, recv_sem):
    sent = []
    for stage, axis in enumerate(order):
        length, pos = place.dims[axis], place.pos[axis]
        if length == 1:
            continue
        base = sum(d - 1 for d in place.dims[:axis])

        def copy(way, step, coord, to, stage=stage, axis=axis, pos=pos, base=base):
            ref = buf.at[block_of(place, order, stage, coord)]
            arrival = recv_sem.at[base + coord - (coord > to).astype(jnp.int32)]
            return remote(ref, ref, send_sem.at[line_slot(place.dims, axis, way, step)], arrival, place.at(axis, to))

        for step in range(1, length + 1):
            for way in (0, 1):
                coord = pos - (step - 1) if way == 0 else pos + (step - 1)
                to = pos + 1 if way == 0 else pos - 1
                here = (coord >= 0) if way == 0 else (coord < length)
                if step > 1:
                    pl.when(here)(lambda: copy(way, step - 1, coord, pos).wait_recv())
                if step < length:
                    more = jnp.logical_and(here, (to < length) if way == 0 else (to >= 0))
                    pl.when(more)(lambda: copy(way, step, coord, to).start())
                    sent.append((more, functools.partial(copy, way, step, coord, to)))
            if step < length:
                yield
    return sent


def scatter_steps(place, order, acc, arrive, send_sem, recv_sem, result):
    sent = []
    last = [axis for axis in order if place.dims[axis] > 1][0]
    at = 0
    for stage in reversed(range(3)):
        axis = order[stage]
        length, pos = place.dims[axis], place.pos[axis]
        if length == 1:
            continue
        units = math.prod(place.dims[a] for a in order[:stage])
        shape = tuple(place.dims[a] for a in sorted(order[:stage]))

        def copy(way, step, coord, stage=stage, axis=axis, pos=pos, at=at, units=units, length=length, shape=shape):
            src = acc.at[block_of(place, order, stage, coord)]
            slot = at + ((way * (length - 1) if length > 2 else 0) + step - 1) * units
            dst = arrive.at[pl.ds(slot, units)].reshape(*shape, *arrive.shape[1:])
            sem = line_slot(place.dims, axis, way, step)
            device = place.at(axis, pos + 1 if way == 0 else pos - 1)
            return remote(src, dst, send_sem.at[sem], recv_sem.at[sem], device), dst

        for step in range(length - 1, 0, -1):
            for way in (0, 1):
                coord = pos + step if way == 0 else pos - step
                has = (coord < length) if way == 0 else (coord >= 0)
                pl.when(has)(lambda: copy(way, step, coord)[0].start())
                sent.append((has, functools.partial(lambda move, *a: move(*a)[0], copy, way, step, coord)))
            yield
            for way in (0, 1):
                coord = pos - 1 + step if way == 0 else pos + 1 - step
                if way == 0:
                    comes = jnp.logical_and(pos > 0, coord < length)
                else:
                    comes = jnp.logical_and(pos < length - 1, coord >= 0)

                def take():
                    move, ref = copy(way, step, coord)
                    move.wait_recv()
                    index = block_of(place, order, stage, coord)
                    if axis == last and step == 1:
                        total = acc[index].astype(F32) + ref[...].astype(F32)
                        result[...] = total
                        acc[index] = total.astype(BF16)
                    else:
                        acc[index] = acc[index] + ref[...]

                pl.when(comes)(take)
        at += line_slots(length) * units
    return sent


def arrive_units(dims, order):
    units = 0
    for stage in range(3):
        if dims[order[stage]] > 1:
            length = dims[order[stage]]
            units += (2 if length > 2 else 1) * (length - 1) * math.prod(dims[a] for a in order[:stage])
    return units


def in_turn(plan):
    events = sorted((time, which, step) for which, (times, _) in enumerate(plan) for step, time in enumerate(times))
    results = [None] * len(plan)
    for _, which, _ in events:
        if results[which] is None:
            try:
                next(plan[which][1])
            except StopIteration as stop:
                results[which] = stop.value
    assert all(r is not None for r in results)
    return results


def wait_sent(sent):
    for cond, make in sent:
        if cond is None:
            make().wait_send()
        else:
            pl.when(cond)(lambda: make().wait_send())


ORDERS = ((2, 0, 1), (1, 0, 2), (0, 2, 1), (2, 0, 1), (1, 0, 2), (0, 1, 2))


def step_times(dims, order, start, back=False):
    times = [0.0]
    units = 1
    for axis in order:
        for _ in range(dims[axis] - 1):
            times.append(times[-1] + 1.6 * units + 3.0)
        units *= dims[axis]
    times.append(times[-1] + 4.0)
    if back:
        times = [times[-1] - t for t in reversed(times)]
    return [start + t for t in times] + [start + times[-1] + 4.0, start + times[-1] + 8.0]


def gather_kernel(dims, count, *refs):
    ins, outs = refs[:count], refs[count : 2 * count]
    send_sem, recv_sem, own_sem, peer_send, peer_recv = refs[2 * count :]
    place = Place(dims)
    own = [
        pltpu.make_async_copy(ins[c], outs[c].at[(place.mp,) + place.pos], own_sem.at[c]) for c in range(count)
    ]
    for copy in own:
        copy.start()
    greet_lines(place)

    def chunk(c, order):
        own[c].wait()
        mine, other = outs[c].at[place.mp], outs[c].at[1 - place.mp]
        sent = yield from gather_steps(place, order, mine, send_sem.at[c], recv_sem.at[c])

        def copy(ref):
            return remote(ref, ref, peer_send.at[c], peer_recv.at[c], place.peer())

        copy(mine).start()
        yield
        copy(other).wait_recv()
        return sent + [(None, lambda: copy(mine))]

    plan = []
    for c in range(count):
        order = ORDERS[c % len(ORDERS)]
        plan.append((step_times(dims, order, 3.9 * c), chunk(c, order)))
    for sent in in_turn(plan):
        wait_sent(sent)


def gather(shards, dims):
    count = len(shards)
    return pl.pallas_call(
        functools.partial(gather_kernel, dims, count),
        out_shape=[jax.ShapeDtypeStruct((2,) + dims + s.shape, BF16) for s in shards],
        in_specs=[pl.BlockSpec(memory_space=pl.ANY)] * count,
        out_specs=[pl.BlockSpec(memory_space=pl.ANY)] * count,
        scratch_shapes=[
            pltpu.SemaphoreType.DMA((count, send_slots(dims))),
            pltpu.SemaphoreType.DMA((count, gather_slots(dims))),
        ]
        + [pltpu.SemaphoreType.DMA((count,))] * 3,
        compiler_params=pltpu.CompilerParams(collective_id=0, has_side_effects=True),
        name="gather_weights",
    )(*shards)


def scatter_kernel(dims, count, shared, extra, *refs):
    ins, pieces = refs[:count], refs[count : count + extra]
    refs = refs[count + extra :]
    outs, wholes = refs[:count], refs[count : count + extra]
    refs = refs[count + extra :]
    acc, peer_in, arrive = refs[:count], refs[count : 2 * count], refs[2 * count : 3 * count]
    send_sem, recv_sem, own_sem, peer_send, peer_recv, end_send, end_recv, ex_own, ex_send, ex_recv = refs[3 * count :]
    place = Place(dims)
    own = [pltpu.make_async_copy(ins[c].at[place.mp], acc[c], own_sem.at[c]) for c in range(count)]
    for copy in own:
        copy.start()
    keep = [pltpu.make_async_copy(pieces[e], wholes[e].at[place.mp], ex_own.at[e]) for e in range(extra)]
    for copy in keep:
        copy.start()
    greet_lines(place)
    give = [
        remote(pieces[e], wholes[e].at[place.mp], ex_send.at[e], ex_recv.at[e], place.peer()) for e in range(extra)
    ]

    def chunk(c, order):
        def copy():
            return remote(ins[c].at[1 - place.mp], peer_in[c], peer_send.at[c], peer_recv.at[c], place.peer())

        copy().start()
        yield
        own[c].wait()
        copy().wait_recv()
        acc[c][...] = acc[c][...] + peer_in[c][...]
        result = outs[c].at[place.mp] if c in shared else outs[c]
        sent = yield from scatter_steps(
            place, order, acc[c], arrive[c], send_sem.at[c], recv_sem.at[c], result
        )
        sent.append((None, copy))
        if c in shared:

            def hand(half):
                ref = outs[c].at[half]
                return remote(ref, ref, end_send.at[c], end_recv.at[c], place.peer())

            hand(place.mp).start()
            yield
            hand(1 - place.mp).wait_recv()
            sent.append((None, lambda: hand(place.mp)))
        return sent

    plan = []
    for c in range(count):
        order = ORDERS[c % len(ORDERS)]
        plan.append((step_times(dims, order, 3.9 * c, True), chunk(c, order)))
    for copy in give:
        copy.start()
    for sent in in_turn(plan):
        wait_sent(sent)
    for copy in keep:
        copy.wait()
    for copy in give:
        copy.wait()


def scatter(grads, shared, pieces, dims):
    count, extra = len(grads), len(pieces)
    shapes = [
        jax.ShapeDtypeStruct(((2,) if c in shared else ()) + g.shape[-2:], F32) for c, g in enumerate(grads)
    ]
    wholes = [jax.ShapeDtypeStruct((2,) + p.shape, p.dtype) for p in pieces]
    return pl.pallas_call(
        functools.partial(scatter_kernel, dims, count, shared, extra),
        out_shape=shapes + wholes,
        in_specs=[pl.BlockSpec(memory_space=pl.ANY)] * (count + extra),
        out_specs=[pl.BlockSpec(memory_space=pltpu.VMEM)] * count + [pl.BlockSpec(memory_space=pl.ANY)] * extra,
        scratch_shapes=[pltpu.VMEM(g.shape[1:], BF16) for g in grads] * 2
        + [
            pltpu.VMEM((arrive_units(dims, ORDERS[c % len(ORDERS)]),) + g.shape[-2:], BF16)
            for c, g in enumerate(grads)
        ]
        + [pltpu.SemaphoreType.DMA((count, send_slots(dims)))] * 2
        + [pltpu.SemaphoreType.DMA((count,))] * 5
        + [pltpu.SemaphoreType.DMA((extra,))] * 3,
        compiler_params=pltpu.CompilerParams(
            collective_id=1, has_side_effects=True, vmem_limit_bytes=60 * 2**20
        ),
        name="scatter_gradients",
    )(*grads, *pieces)


def matmul(left, right):
    return jnp.dot(left, right, preferred_element_type=F32)


def contract_rows(left, right):
    return lax.dot_general(left, right, (((0,), (0,)), ((), ())), preferred_element_type=F32)


def contract_cols(left, right):
    return lax.dot_general(left, right, (((1,), (1,)), ((), ())), preferred_element_type=F32)


def layer_norm(inputs, gain, shift):
    centred = inputs - jnp.mean(inputs, -1, keepdims=True)
    inv_std = lax.rsqrt(jnp.mean(centred * centred, -1, keepdims=True) + EPS)
    normed = centred * inv_std
    return (normed * gain + shift, normed, inv_std)


def norm_back(upstream, normed, inv_std, gain):
    scaled = upstream * gain
    inner_mean = jnp.mean(scaled * normed, -1, keepdims=True)
    result = inv_std * (scaled - jnp.mean(scaled, -1, keepdims=True) - normed * inner_mean)
    return (result, jnp.sum(upstream * normed, 0), jnp.sum(upstream, 0))


def split_heads(flat, pair_count):
    return flat.reshape(pair_count, -1, flat.shape[-1] // HEAD_DIM, HEAD_DIM)


def attend(queries, key_heads, value_heads):
    factor = 1.0 / math.sqrt(HEAD_DIM)
    scores = jnp.einsum("pqhd,pkhd->phqk", queries, key_heads, preferred_element_type=F32) * factor
    row_max = jnp.max(scores, -1, keepdims=True)
    expd = jnp.exp(scores - row_max)
    row_sum = jnp.sum(expd, -1, keepdims=True)
    probs = (expd / row_sum).astype(BF16)
    mixed = jnp.einsum("phqk,pkhd->pqhd", probs, value_heads, preferred_element_type=F32)
    flat_rows = queries.shape[0] * queries.shape[1]
    return (mixed.astype(BF16).reshape(flat_rows, -1), row_max + jnp.log(row_sum))


def attend_back(queries, key_heads, value_heads, log_total, upstream):
    factor = 1.0 / math.sqrt(HEAD_DIM)
    scores = jnp.einsum("pqhd,pkhd->phqk", queries, key_heads, preferred_element_type=F32) * factor
    probs = jnp.exp(scores - log_total)
    dprobs = jnp.einsum("pqhd,pkhd->phqk", upstream, value_heads, preferred_element_type=F32)
    dscores = (probs * (dprobs - jnp.sum(dprobs * probs, -1, keepdims=True))).astype(BF16)
    dqueries = jnp.einsum("phqk,pkhd->pqhd", dscores, key_heads, preferred_element_type=F32) * factor
    dkeys = jnp.einsum("phqk,pqhd->pkhd", dscores, queries, preferred_element_type=F32) * factor
    dvalues = jnp.einsum("phqk,pqhd->pkhd", probs.astype(BF16), upstream, preferred_element_type=F32)
    return tuple(t.astype(BF16).reshape(-1, t.shape[2] * t.shape[3]) for t in (dqueries, dkeys, dvalues))


def unit_back(raw, inv_norm, upstream):
    cubed = inv_norm * inv_norm * inv_norm
    return inv_norm * upstream - raw * cubed * jnp.sum(raw * upstream, -1, keepdims=True)


def contrast(text_pool, image_pool, text_embed32, image_embed32):
    text_raw = jnp.dot(text_pool, text_embed32, precision=HIGHEST)
    text_inv = lax.rsqrt(jnp.sum(text_raw * text_raw, -1, keepdims=True) + EPS)
    image_raw = jnp.dot(image_pool, image_embed32, precision=HIGHEST)
    image_inv = lax.rsqrt(jnp.sum(image_raw * image_raw, -1, keepdims=True) + EPS)
    both = jnp.concatenate([(text_raw * text_inv).astype(BF16), (image_raw * image_inv).astype(BF16)], 1)
    width = text_raw.shape[1]
    everyone = lax.all_gather(both, ("dp", "mp"), axis=0, tiled=True)
    text_all, image_all = everyone[:, :width], everyone[:, width:]
    logits = contract_cols(text_all, image_all) * TEMP_INVERSE
    weights = jnp.exp(logits - jax.nn.logsumexp(logits, axis=1, keepdims=True)) + jnp.exp(
        logits - jax.nn.logsumexp(logits, axis=0, keepdims=True)
    )
    weights = weights - 2.0 * jnp.eye(logits.shape[0], dtype=F32)
    count = text_pool.shape[0]
    start = (lax.axis_index("dp") * 2 + lax.axis_index("mp")) * count
    rows = lax.dynamic_slice_in_dim(weights, start, count, 0)
    columns = lax.dynamic_slice_in_dim(weights, start, count, 1)
    dtext = GRAD_SCALE * jnp.dot(rows, image_all.astype(F32), precision=HIGHEST)
    dimage = GRAD_SCALE * jnp.dot(columns.T, text_all.astype(F32), precision=HIGHEST)
    dtext_raw = unit_back(text_raw, text_inv, dtext)
    dimage_raw = unit_back(image_raw, image_inv, dimage)
    return (
        jnp.dot(text_pool.T, dtext_raw, precision=HIGHEST),
        jnp.dot(image_pool.T, dimage_raw, precision=HIGHEST),
        jnp.dot(dtext_raw, text_embed32.T, precision=HIGHEST),
        jnp.dot(dimage_raw, image_embed32.T, precision=HIGHEST),
    )


FACTOR = 1.0 / math.sqrt(HEAD_DIM)
LOWEST = -1e30
TEXT_PAD = 64
PATCH_PAD = 160
RING = 8


def nn(a, b):
    return lax.dot_general(a, b, (((1,), (0,)), ((), ())), preferred_element_type=F32)


def nt(a, b):
    return lax.dot_general(a, b, (((1,), (1,)), ((), ())), preferred_element_type=F32)


def tn(a, b):
    return lax.dot_general(a, b, (((0,), (0,)), ((), ())), preferred_element_type=F32)


def exact(a, b, dims):
    return lax.dot_general(a, b, (dims, ((), ())), precision=HIGHEST, preferred_element_type=F32)


def terms(x):
    high = x.astype(BF16)
    return high, (x - high.astype(F32)).astype(BF16)


def near(a, b, dims):
    def dot(x, y):
        return lax.dot_general(x, y, (dims, ((), ())), preferred_element_type=F32)

    (a_high, a_low), (b_high, b_low) = terms(a), terms(b)
    return dot(a_high, b_high) + (dot(a_high, b_low) + dot(a_low, b_high))


class Blocks:
    def __init__(self):
        self.free, self.top = [], 0

    def take(self, count):
        spare = sorted(self.free)
        for at in spare:
            if all(at + k in spare for k in range(count)):
                for k in range(count):
                    self.free.remove(at + k)
                return at
        at, self.top = self.top, self.top + count
        return at

    def give(self, at, count):
        self.free += range(at, at + count)


def lane_masks(width, split):
    lane = lax.broadcasted_iota(jnp.int32, (1, width), 1)
    left = (lane < split).astype(F32)
    return left, 1.0 - left


def head_pair(x):
    left, right = lane_masks(128, 64)
    return jnp.concatenate([x * left.astype(BF16), x * right.astype(BF16)], 0)


def one_head_each(x):
    half = x.shape[0] // 2
    left = lax.broadcasted_iota(jnp.int32, (half, 128), 1) < 64
    return jnp.where(left, x[:half], x[half:])


def softmax_pair(scores, keys, real):
    lane = lax.broadcasted_iota(jnp.int32, scores.shape, 1)
    left = lane < keys
    within = jnp.where(left, lane, lane - keys)
    scores = jnp.where(within < real, scores * FACTOR, LOWEST)
    top0 = jnp.max(jnp.where(left, scores, LOWEST), 1, keepdims=True)
    top1 = jnp.max(jnp.where(left, LOWEST, scores), 1, keepdims=True)
    expd = jnp.exp(scores - jnp.where(left, top0, top1))
    sum0 = jnp.sum(jnp.where(left, expd, 0.0), 1, keepdims=True)
    sum1 = jnp.sum(jnp.where(left, 0.0, expd), 1, keepdims=True)
    return (expd * jnp.where(left, 1.0 / sum0, 1.0 / sum1)).astype(BF16)


def softmax_pair_back(probs, dprobs, keys):
    left = lax.broadcasted_iota(jnp.int32, dprobs.shape, 1) < keys
    probs = probs.astype(F32)
    both = probs * dprobs
    sum0 = jnp.sum(jnp.where(left, both, 0.0), 1, keepdims=True)
    sum1 = jnp.sum(jnp.where(left, 0.0, both), 1, keepdims=True)
    return (both - probs * jnp.where(left, sum0, sum1)).astype(BF16)


def norm_rows(x):
    centred = x - jnp.mean(x, -1, keepdims=True)
    inv_std = lax.rsqrt(jnp.mean(centred * centred, -1, keepdims=True) + EPS)
    return centred * inv_std, inv_std


class Layer:
    def __init__(self, dims, sizes, refs):
        self.dims, self.sizes = dims, sizes
        self.__dict__.update(refs)
        self.place = Place(dims)
        self.blocks, self.wide = Blocks(), Blocks()
        self.rows = sizes.pairs * TEXT_PAD
        self.patch_rows = sizes.pairs * PATCH_PAD
        self.half = sizes.half
        self.da = None


    def weight(self, slot, h):
        w = self.w[slot][h]
        return w.reshape(-1, w.shape[-1])

    def put_grad(self, slot, h, f, value):
        cut = self.dims[0] // 2
        shape = self.w[slot].shape[2:]
        self.w[slot][h, f * cut : (f + 1) * cut] = value.astype(BF16).reshape(cut, *shape)

    def project(self, at, slot, h):
        w = self.weight(slot, h)
        return nn(self.t[at], w[: self.half]) + nn(self.t[at + 1], w[self.half :])

    def two(self, fn):
        for h in range(2):
            fn(h)

    def text_loop(self, fn):
        def step(p, carry):
            fn(p, pl.ds(pl.multiple_of(p * TEXT_PAD, TEXT_PAD), TEXT_PAD))
            return carry

        lax.fori_loop(0, self.sizes.pairs, step, 0)

    def read_rows(self, at, rows):
        return jnp.concatenate([self.t[at, rows, :], self.t[at + 1, rows, :]], 1)

    def write_rows(self, at, rows, value):
        self.t[at, rows, :] = value[:, : self.half].astype(BF16)
        self.t[at + 1, rows, :] = value[:, self.half :].astype(BF16)


    def load(self):
        take = self.blocks.take
        self.x, self.cot = take(2), take(2)
        copies = [pltpu.make_async_copy(self.patches_in, self.patches, self.load_sem.at[4])]
        for h in range(2):
            cols = pl.ds(h * self.half, self.half)
            copies.append(pltpu.make_async_copy(self.text_in.at[:, cols], self.t.at[self.x + h], self.load_sem.at[h]))
            copies.append(pltpu.make_async_copy(self.cot_in.at[:, cols], self.t.at[self.cot + h], self.load_sem.at[2 + h]))
        for copy in copies:
            copy.start()
        return copies

    def image_features(self):
        self.im = self.wide.take(2)
        block = self.patch_rows // 3

        def step(i, carry):
            rows = pl.ds(pl.multiple_of(i * block, block), block)
            left = self.patches[rows, :]
            for h in range(2):
                self.u[self.im + h, rows, :] = nn(left, self.weight(IMAGE, h)).astype(BF16)
            return carry

        lax.fori_loop(0, 3, step, 0)

    def self_projections(self):
        self.q = self.blocks.take(6)
        for k, slot in enumerate((QUERY, KEY, VALUE)):
            self.two(lambda h: self.t.__setitem__(self.q + 2 * k + h, self.project(self.x, slot, h).astype(BF16)))

    def couples(self):
        return [(h, slice(128 * j, 128 * j + 128)) for h in range(2) for j in range(self.half // 128)]

    def put_couples(self, ref, at, rows, values):
        each = len(values) // 2
        for h in range(2):
            ref[at + h, rows, :] = jnp.concatenate(values[h * each : (h + 1) * each], 1)

    def attention(self, p, rows, queries, keys, values, saved, key_pad, real, out):
        scores = jnp.concatenate([nt(q, head_pair(k)) for q, k in zip(queries, keys)], 0)
        probs = softmax_pair(scores, key_pad, real)
        saved[p] = probs
        mixed = [
            nn(probs[TEXT_PAD * i : TEXT_PAD * (i + 1)], head_pair(v)).astype(BF16) for i, v in enumerate(values)
        ]
        self.put_couples(self.t, out, rows, mixed)

    def attention_back(self, p, queries, keys, values, upstream, saved, key_pad):
        probs = saved[p]
        dprobs = jnp.concatenate([nt(d, head_pair(v)) for d, v in zip(upstream, values)], 0)
        dscores = softmax_pair_back(probs, dprobs, key_pad)
        part = [slice(TEXT_PAD * i, TEXT_PAD * (i + 1)) for i in range(len(queries))]
        dqueries = [(nn(dscores[r], head_pair(k)) * FACTOR).astype(BF16) for r, k in zip(part, keys)]
        dkeys = [(one_head_each(tn(dscores[r], q)) * FACTOR).astype(BF16) for r, q in zip(part, queries)]
        dvalues = [one_head_each(tn(probs[r], d)).astype(BF16) for r, d in zip(part, upstream)]
        return dqueries, dkeys, dvalues

    def self_attention(self):
        self.a1 = self.blocks.take(2)

        def pair(p, rows):
            q, k, v = ([self.t[self.q + 2 * m + h, rows, lanes] for h, lanes in self.couples()] for m in range(3))
            self.attention(p, rows, q, k, v, self.p1, TEXT_PAD, self.sizes.length, self.a1)

        self.text_loop(pair)

    def norm_params(self):
        cols = self.weight(SMALL, 0)[:, 2 * self.sizes.embed_half :].astype(F32)
        self.norms[...] = jnp.transpose(cols)[: self.norms.shape[0]]

    def after_branch(self, at, slot, k):
        self.z[...] = nt(self.t[at], self.weight(slot, 0)) + nt(self.t[at + 1], self.weight(slot, 1))
        normed_at, low_at = self.blocks.take(2), self.blocks.take(2)

        def rows_step(p, rows):
            residual = self.read_rows(self.x, rows).astype(F32) if k == 0 else self.hid[rows, :]
            normed, inv_std = norm_rows(residual + self.z[rows, :])
            hidden = normed * self.norms[2 * k : 2 * k + 1, :] + self.norms[2 * k + 1 : 2 * k + 2, :]
            self.hid[rows, :] = hidden
            self.inv[k, rows, :] = inv_std
            self.write_rows(normed_at, rows, normed)
            self.write_rows(low_at, rows, hidden)

        self.text_loop(rows_step)
        return normed_at, low_at

    def turned(self, at):
        out = self.blocks.take(2)
        for h in range(2):
            self.t[out + h] = jnp.transpose(self.t[at + h])
        return out

    def after_self(self):
        self.n1, low = self.after_branch(self.a1, ATTN_OUT, 0)
        self.low1, self.low1_t = low, self.turned(low)

    def cross_keys(self, slot):
        at = self.wide.take(2)
        block = self.patch_rows // 3

        def step(i, carry):
            rows = pl.ds(pl.multiple_of(i * block, block), block)
            for h in range(2):
                w = self.weight(slot, h)
                self.u[at + h, rows, :] = (
                    nn(self.u[self.im, rows, :], w[: self.half]) + nn(self.u[self.im + 1, rows, :], w[self.half :])
                ).astype(BF16)
            return carry

        lax.fori_loop(0, 3, step, 0)
        return at

    def make_keys(self):
        self.k2 = self.cross_keys(CROSS_KEY)

    def make_values(self):
        self.v2 = self.cross_keys(CROSS_VALUE)

    def cross_query(self):
        self.q2 = self.blocks.take(2)
        self.two(lambda h: self.t.__setitem__(self.q2 + h, self.project(self.low1, CROSS_QUERY, h).astype(BF16)))
        self.blocks.give(self.low1, 2)

    def patch_rows_of(self, p):
        return pl.ds(pl.multiple_of(p * PATCH_PAD, PATCH_PAD), PATCH_PAD)

    def cross_attention(self):
        self.a2 = self.blocks.take(2)

        def pair(p, rows):
            keys = self.patch_rows_of(p)
            q = [self.t[self.q2 + h, rows, lanes] for h, lanes in self.couples()]
            k, v = ([self.u[at + h, keys, lanes] for h, lanes in self.couples()] for at in (self.k2, self.v2))
            self.attention(p, rows, q, k, v, self.p2, PATCH_PAD, self.sizes.patch_count, self.a2)

        self.text_loop(pair)

    def after_cross(self):
        self.n2, low = self.after_branch(self.a2, CROSS_OUT, 1)
        self.low2, self.low2_t = low, self.turned(low)
        self.g, self.dg = self.blocks.take(2 * self.sizes.hidden_blocks), self.blocks.take(2 * self.sizes.hidden_blocks)

    def ffn_in(self, k):
        def half(h, carry):
            inner = self.project(self.low2, FFN + k, h)
            cdf = 0.5 * (1.0 + lax.erf(inner * math.sqrt(0.5)))
            pdf = jnp.exp(-0.5 * inner * inner) * (1.0 / math.sqrt(2.0 * math.pi))
            self.t[self.g + 2 * k + h] = (inner * cdf).astype(BF16)
            self.t[self.dg + 2 * k + h] = (cdf + inner * pdf).astype(BF16)
            return carry

        lax.fori_loop(0, 2, half, 0)
        if k == self.sizes.hidden_blocks - 1:
            self.blocks.give(self.low2, 2)

    def ffn_out(self, k):
        def half(h, carry):
            self.hid[...] += nt(self.t[self.g + 2 * k + h], self.weight(FFN + self.sizes.hidden_blocks + k, h))
            return carry

        lax.fori_loop(0, 2, half, 0)


    def pools(self):
        pairs, length, patch_count = self.sizes.pairs, self.sizes.length, self.sizes.patch_count
        self.pool[...] = jnp.zeros_like(self.pool)
        for p in range(pairs):
            rows = pl.ds(p * TEXT_PAD, TEXT_PAD)
            self.pool[0, p : p + 1, :] = jnp.sum(self.read_rows(self.x, rows).astype(F32), 0, keepdims=True) * (1.0 / length)
            keys = pl.ds(p * PATCH_PAD, PATCH_PAD)
            for h in range(2):
                self.pool[1, p : p + 1, h * self.half : (h + 1) * self.half] = jnp.sum(
                    self.u[self.im + h, keys, :].astype(F32), 0, keepdims=True
                ) * (1.0 / patch_count)

    def embed_weight(self, which, h):
        width = self.sizes.embed_half
        return self.weight(SMALL, h)[:, which * width : (which + 1) * width].astype(F32)

    def embed(self):
        width = self.sizes.embed_half
        for which in range(2):
            for h in range(2):
                self.raw[which, :, h * width : (h + 1) * width] = exact(
                    self.pool[which], self.embed_weight(which, h), ((1,), (0,))
                )
            raw = self.raw[which]
            inv = lax.rsqrt(jnp.sum(raw * raw, -1, keepdims=True) + EPS)
            self.own_emb[:, which * 2 * width : (which + 1) * 2 * width] = (raw * inv).astype(BF16)

    def contrast(self):
        width, pairs = self.sizes.embed_half, self.sizes.pairs
        everyone = self.emb[...].reshape(-1, 4 * width)
        count = everyone.shape[0]
        both = everyone[:, : 2 * width], everyone[:, 2 * width :]
        own = self.own_emb[...][:, : 2 * width], self.own_emb[...][:, 2 * width :]
        spot = self.place.pos
        me = self.place.mp * (count // 2) + ((spot[0] * self.dims[1] + spot[1]) * self.dims[2] + spot[2]) * 16
        real_row = (lax.broadcasted_iota(jnp.int32, (1, count), 1) % 16 < pairs).astype(F32)
        real_col = (lax.broadcasted_iota(jnp.int32, (count, 1), 0) % 16 < pairs).astype(F32)
        own_row = (lax.broadcasted_iota(jnp.int32, (16, 1), 0) < pairs).astype(F32)
        match = (
            lax.broadcasted_iota(jnp.int32, (16, count), 1) == lax.broadcasted_iota(jnp.int32, (16, count), 0) + me
        ).astype(F32)
        for which in range(2):
            mine, others = own[which], both[1 - which]
            column_sum = jnp.zeros((1, count), F32)
            for at in range(0, count, 128):
                cross = nt(both[which][at : at + 128], others) * TEMP_INVERSE - TEMP_INVERSE
                column_sum = column_sum + jnp.sum(jnp.exp(cross) * real_col[at : at + 128], 0, keepdims=True)
            logits = nt(mine, others) * TEMP_INVERSE - TEMP_INVERSE
            expd = jnp.exp(logits) * (real_row * own_row)
            row_sum = jnp.sum(expd, 1, keepdims=True) + (1.0 - own_row)
            pull = expd * (1.0 / row_sum) + expd * (1.0 / column_sum) - 2.0 * match * own_row
            upstream = GRAD_SCALE * exact(pull, others.astype(F32), ((1,), (0,)))
            raw = self.raw[which]
            inv = lax.rsqrt(jnp.sum(raw * raw, -1, keepdims=True) + EPS)
            draw = unit_back(raw, inv, upstream)
            scale = 1.0 / (self.sizes.length if which == 0 else self.sizes.patch_count)
            extra = exact(draw[:, :width], self.embed_weight(which, 0), ((1,), (1,))) + exact(
                draw[:, width:], self.embed_weight(which, 1), ((1,), (1,))
            )
            self.extra[which] = extra * scale
            for h in range(2):
                value = exact(self.pool[which], draw[:, h * width : (h + 1) * width], ((0,), (0,)))
                self.put_small(h, which * width, value)


    def region(self):
        pairs, length, patch_count = self.sizes.pairs, self.sizes.length, self.sizes.patch_count
        boxes, listed = self.picks.shape[1:]
        self.chosen[...] = jnp.zeros_like(self.chosen)
        self.span[...] = jnp.zeros_like(self.span)
        for p in range(pairs):
            picks = self.picks[self.place.mp * pairs + p]
            counts = self.counts[pl.ds(self.place.mp * pairs + p, 1), :]
            spot = lax.broadcasted_iota(jnp.int32, (boxes, PATCH_PAD), 1)
            listing = jnp.zeros((boxes, PATCH_PAD), F32)
            for k in range(listed):
                listing = listing + (picks[:, k : k + 1] == spot).astype(F32)
            valid = lax.broadcasted_iota(jnp.int32, (boxes, PATCH_PAD), 0) < counts
            self.chosen[p, :boxes, :] = jnp.where(valid, listing * (1.0 / listed), 0.0)
            starts = self.starts[pl.ds(self.place.mp * pairs + p, 1), :]
            lengths = self.lengths[pl.ds(self.place.mp * pairs + p, 1), :]
            token = lax.broadcasted_iota(jnp.int32, (TEXT_PAD, boxes), 0)
            slot = lax.broadcasted_iota(jnp.int32, (TEXT_PAD, boxes), 1)
            inside = (token >= starts) & (token < starts + lengths) & (slot < counts)
            self.span[p, :, :boxes] = jnp.where(inside, 1.0 / lengths.astype(F32), 0.0)
            keys = pl.ds(p * PATCH_PAD, PATCH_PAD)
            for h in range(2):
                self.regions[p, :, h * self.half : (h + 1) * self.half] = nn(
                    self.chosen[p].astype(BF16), self.u[self.im + h, keys, :]
                )


    def norm_back(self, k, upstream, normed, inv_std, rows):
        scaled = upstream * self.norms[2 * k : 2 * k + 1, :]
        inner = jnp.mean(scaled * normed, -1, keepdims=True)
        self.norm_grad[2 * k : 2 * k + 1, :] += jnp.sum(upstream * normed, 0, keepdims=True)
        self.norm_grad[2 * k + 1 : 2 * k + 2, :] += jnp.sum(upstream, 0, keepdims=True)
        result = inv_std * (scaled - jnp.mean(scaled, -1, keepdims=True) - normed * inner)
        self.z[rows, :] = result
        self.write_rows(self.db, rows, result)

    def output_and_back(self):
        self.db = self.blocks.take(2)
        self.norm_grad[...] = jnp.zeros_like(self.norm_grad)

        def pair(p, rows):
            normed, inv_std = norm_rows(self.hid[rows, :])
            output = normed * self.norms[4:5, :] + self.norms[5:6, :]
            self.joined[p] = output[: self.sizes.length].astype(BF16)
            mismatch = near(self.span[p], output, ((0,), (0,))) - self.regions[p]
            self.regions[p] = mismatch
            upstream = self.read_rows(self.cot, rows).astype(F32) + near(self.span[p], mismatch, ((1,), (0,)))
            self.norm_back(2, upstream, normed, inv_std, rows)

        self.text_loop(pair)
        self.blocks.give(self.cot, 2)
        self.db_t = self.turned(self.db)

    def grads(self, slot, h, left_t, right):
        for f in range(2):
            self.put_grad(slot, h, f, nn(self.t[left_t + f], right))

    def ffn_out_back(self, k):
        slot = FFN + self.sizes.hidden_blocks + k

        def half(h, carry):
            at = 2 * k + h
            dactive = self.project(self.db, slot, h)
            self.t[self.dg + at] = (dactive * self.t[self.dg + at].astype(F32)).astype(BF16)
            self.grads(slot, h, self.db_t, self.t[self.g + at])
            return carry

        lax.fori_loop(0, 2, half, 0)
        self.blocks.give(self.g + 2 * k, 2)

    def ffn_in_back(self, k):
        slot = FFN + k

        def half(h, carry):
            dinner = self.t[self.dg + 2 * k + h]
            self.z[...] += nt(dinner, self.weight(slot, h))
            self.grads(slot, h, self.low2_t, dinner)
            return carry

        lax.fori_loop(0, 2, half, 0)

    def back_through_norm(self, k):
        normed_at = (self.n1, self.n2)[k]

        def step(p, rows):
            self.norm_back(k, self.z[rows, :], self.read_rows(normed_at, rows).astype(F32), self.inv[k, rows, :], rows)

        self.text_loop(step)
        for h in range(2):
            self.t[self.db_t + h] = jnp.transpose(self.t[self.db + h])

    def branch_back(self, slot, at):
        if self.da is None:
            self.da = self.blocks.take(2)

        def half(h, carry):
            self.t[self.da + h] = self.project(self.db, slot, h).astype(BF16)
            self.grads(slot, h, self.db_t, self.t[at + h])
            return carry

        lax.fori_loop(0, 2, half, 0)

    def cross_attention_back(self):
        def pair(p, rows):
            keys = self.patch_rows_of(p)
            q, d = ([self.t[at + h, rows, lanes] for h, lanes in self.couples()] for at in (self.q2, self.da))
            k, v = ([self.u[at + h, keys, lanes] for h, lanes in self.couples()] for at in (self.k2, self.v2))
            dq, dk, dv = self.attention_back(p, q, k, v, d, self.p2, PATCH_PAD)
            self.put_couples(self.t, self.q2, rows, dq)
            self.put_couples(self.u, self.k2, keys, dk)
            self.put_couples(self.u, self.v2, keys, dv)

        self.text_loop(pair)

    def cross_query_back(self):
        def half(h, carry):
            dq = self.t[self.q2 + h]
            self.z[...] += nt(dq, self.weight(CROSS_QUERY, h))
            self.grads(CROSS_QUERY, h, self.low1_t, dq)
            return carry

        lax.fori_loop(0, 2, half, 0)

    def image_back(self):
        self.dim = self.wide.take(2)
        block = 2 * PATCH_PAD

        def step(i, carry):
            rows = pl.ds(pl.multiple_of(i * block, block), block)
            parts = [self.u[at + h, rows, :] for at in (self.k2, self.v2) for h in range(2)]
            for half in range(2):
                cols = slice(half * self.half, (half + 1) * self.half)
                weights = [self.weight(slot, h)[cols] for slot in (CROSS_KEY, CROSS_VALUE) for h in range(2)]
                total = sum(nt(part, weight) for part, weight in zip(parts, weights))
                for k in range(2):
                    p = 2 * i + k
                    value = total[k * PATCH_PAD : (k + 1) * PATCH_PAD]
                    value = value - sum(tn(self.chosen[p].astype(BF16), m) for m in terms(self.regions[p, :, cols]))
                    value = value + self.extra[1, pl.ds(p, 1), cols]
                    self.u[self.dim + half, self.patch_rows_of(p), :] = value.astype(BF16)
            return carry

        lax.fori_loop(0, self.sizes.pairs // 2, step, 0)

    def cross_key_back(self, slot, at):
        for f in range(2):

            def half(h, carry):
                self.put_grad(slot, h, f, tn(self.u[self.im + f], self.u[at + h]))
                return carry

            lax.fori_loop(0, 2, half, 0)

    def patch_back(self):
        pairs, patch_count = self.sizes.pairs, self.sizes.patch_count

        def out(p):
            return pltpu.make_async_copy(self.patch_stage.at[p % 2], self.patch_grad.at[p], self.patch_sem.at[p % 2])

        for p in range(pairs):
            if p >= 2:
                out(p - 2).wait()
            keys = pl.ds(p * PATCH_PAD, PATCH_PAD)
            value = nt(self.u[self.dim, keys, :], self.weight(IMAGE, 0)) + nt(
                self.u[self.dim + 1, keys, :], self.weight(IMAGE, 1)
            )
            self.patch_stage[p % 2] = value[:patch_count]
            out(p).start()
        for p in range(max(pairs - 2, 0), pairs):
            out(p).wait()

    def image_weight_back(self):
        cut = self.dims[0] // 2
        shape = self.w[IMAGE].shape[2:]
        half_depth = self.patches.shape[1] // 2
        for f in range(2):

            def half(h, carry):
                value = tn(self.patches[:, f * half_depth : (f + 1) * half_depth], self.u[self.dim + h])
                self.w[IMAGE][h, f * cut : (f + 1) * cut] = value.astype(BF16).reshape(cut, *shape)
                return carry

            lax.fori_loop(0, 2, half, 0)

    def put_small(self, h, start, value):
        ref = self.w[SMALL]
        ref[h, :, :, :, :, start : start + value.shape[1]] = value.astype(BF16).reshape(
            *ref.shape[1:-1], value.shape[1]
        )

    def small_grads(self):
        rows = jnp.concatenate([self.norm_grad[...], jnp.zeros((128 - self.norm_grad.shape[0], 2 * self.half), F32)], 0)
        columns = jnp.transpose(rows)
        for h in range(2):
            self.put_small(h, 2 * self.sizes.embed_half, columns)

    def self_attention_back(self):
        def pair(p, rows):
            q, k, v = ([self.t[self.q + 2 * m + h, rows, lanes] for h, lanes in self.couples()] for m in range(3))
            d = [self.t[self.da + h, rows, lanes] for h, lanes in self.couples()]
            for m, values in enumerate(self.attention_back(p, q, k, v, d, self.p1, TEXT_PAD)):
                self.put_couples(self.t, self.q + 2 * m, rows, values)

        self.text_loop(pair)
        for h in range(2):
            self.t[self.db_t + h] = jnp.transpose(self.t[self.x + h])

    def self_projection_back(self, k):
        slot = (QUERY, KEY, VALUE)[k]

        def half(h, carry):
            d = self.t[self.q + 2 * k + h]
            self.z[...] += nt(d, self.weight(slot, h))
            self.grads(slot, h, self.db_t, d)
            return carry

        lax.fori_loop(0, 2, half, 0)

    def text_out(self):
        def moves(p):
            src, dst = self.text_stage.at[p % 2], self.text_out_ref.at[self.place.mp, p]
            own = pltpu.make_async_copy(src, dst, self.text_own.at[p])
            return own, remote(src, dst, self.text_send.at[p], self.text_recv.at[p], self.place.peer())

        def done(p):
            own, give = moves(p)
            own.wait()
            give.wait_send()

        pairs = self.sizes.pairs
        for p in range(pairs):
            if p >= 2:
                done(p - 2)
            rows = pl.ds(p * TEXT_PAD, TEXT_PAD)
            value = self.z[rows, :] + self.extra[0, p : p + 1, :]
            self.text_stage[p % 2] = value[: self.sizes.length]
            for move in moves(p):
                move.start()

        def end():
            for p in range(max(pairs - 2, 0), pairs):
                done(p)
            for p in range(pairs):
                moves(p)[1].wait_recv()

        self.ends.append(end)


    def gather_to_peer(self, c, name, order, buf):
        mine, other = buf.at[self.place.mp], buf.at[1 - self.place.mp]
        sent = yield from gather_steps(self.place, order, mine, self.g_send.at[c], self.g_recv.at[c])

        def copy(ref):
            return remote(ref, ref, self.gp_send.at[c], self.gp_recv.at[c], self.place.peer())

        copy(mine).start()
        yield
        copy(other).wait_recv()
        self.sending[name] = sent + [(None, lambda: copy(mine))]

    def gather(self, c, name, order):
        buf = self.w[name]
        own = pltpu.make_async_copy(self.shards[name], buf.at[(self.place.mp,) + self.place.pos], self.own_sem.at[c])
        own.start()
        yield
        own.wait()
        yield from self.gather_to_peer(c, name, order, buf)

    def gather_embeddings(self, c, order):
        self.emb[(self.place.mp,) + self.place.pos] = self.own_emb[...]
        yield from self.gather_to_peer(c, EMBEDDINGS, order, self.emb)

    def settle(self, names):
        for name in names:
            wait_sent(self.sending.pop(name))

    def credit(self, slot, give):
        place = self.place

        def act(index, device):
            sem = self.credits.at[slot, index]
            if give:
                pl.semaphore_signal(sem, inc=1, device_id=device, device_id_type=MESH)
            else:
                pl.semaphore_wait(sem, 1)

        act(6, place.peer())
        for axis in range(3):
            length, pos = place.dims[axis], place.pos[axis]
            if length > 1:
                pl.when(pos > 0)(lambda: act(2 * axis + (1 if give else 0), place.at(axis, pos - 1)))
                pl.when(pos < length - 1)(lambda: act(2 * axis + (0 if give else 1), place.at(axis, pos + 1)))

    def spare(self, at, units, rows):
        blocks = self.u.at[pl.ds(at, 2)].reshape(-1, rows, self.half)
        return blocks.at[pl.ds(0, units)]

    def scatter(self, c, turn, name, order, total):
        buf, slot = self.w[name], turn % RING
        mine, other = buf.at[self.place.mp], buf.at[1 - self.place.mp]
        if name == IMAGE:
            slot = RING
            peer_in = self.spare(0, math.prod(self.dims), buf.shape[-2]).reshape(*buf.shape[1:])
            arrive = self.spare(2, arrive_units(self.dims, order), buf.shape[-2])
        else:
            peer_in, arrive = self.peer_in.at[slot], self.arrive.at[slot]

        def copy():
            return remote(other, peer_in, self.sp_send.at[slot], self.sp_recv.at[slot], self.place.peer())

        if name == IMAGE or turn >= RING:
            self.credit(slot, False)
        if slot in self.ring_sent:
            wait_sent(self.ring_sent.pop(slot))
        copy().start()
        yield
        copy().wait_recv()
        mine[...] = mine[...] + peer_in[...]
        result = self.results[name]
        target = result.at[self.place.mp] if len(result.shape) == 3 else result
        sent = yield from scatter_steps(
            self.place, order, mine, arrive, self.s_send.at[slot], self.s_recv.at[slot], target
        )
        if name != IMAGE and turn + RING < total:
            self.credit(slot, True)
        self.ring_sent[slot] = sent + [(None, copy)]
        if len(result.shape) == 3:

            def hand(half):
                ref = result.at[half]
                return remote(ref, ref, self.h_send.at[int(name == IMAGE)], self.h_recv.at[int(name == IMAGE)], self.place.peer())

            hand(self.place.mp).start()
            yield
            hand(1 - self.place.mp).wait_recv()
            self.sent.append((None, lambda: hand(self.place.mp)))

    def joined_over(self):
        stage, whole = self.joined, self.joined_out
        own = pltpu.make_async_copy(stage, whole.at[self.place.mp], self.out_own)
        give = remote(stage, whole.at[self.place.mp], self.out_send, self.out_recv, self.place.peer())
        own.start()
        give.start()
        self.ends += [own.wait, give.wait]


IMAGE, QUERY, KEY, VALUE, SMALL, ATTN_OUT, CROSS_KEY, CROSS_VALUE, CROSS_QUERY, CROSS_OUT, FFN = range(11)
EMBEDDINGS = -1


def grad_order(hidden_blocks):
    ffn = (*range(FFN + hidden_blocks, FFN + 2 * hidden_blocks), *range(FFN, FFN + hidden_blocks))
    return ffn + (CROSS_OUT, CROSS_QUERY, CROSS_KEY, CROSS_VALUE, IMAGE, ATTN_OUT, SMALL, QUERY, KEY, VALUE)


class Timeline:
    def __init__(self):
        self.events = []

    def add(self, time, fn):
        self.events.append((time, len(self.events), fn))

    def add_steps(self, times, steps):
        last = [False]

        def advance():
            if not last[0]:
                try:
                    next(steps)
                except StopIteration:
                    last[0] = True

        for time in times:
            self.add(time, advance)

    def run(self):
        for _, _, fn in sorted(self.events, key=lambda e: e[:2]):
            fn()


CHUNK = 3.9
KINDS = ((2, 0, 1), (1, 0, 2), (0, 2, 1), (0, 1, 2))

GATHER_KINDS = (3, 2, 0, 1, 2, 1, 3, 0, 1, 2, 1, 0, 1, 2, 2, 2, 3, 2)
GATHER_START = (0.0, 0.37, 5.87, 5.87, 19.41, 25.59, 25.59, 28.48, 29.2, 36.36, 37.1, 42.44, 50.18, 51.33, 62.99, 64.25, 65.56, 71.17)
GATHER_STEPS = (
    (0.0, 5.65, 10.87, 19.52, 23.43, 32.51, 38.07),
    (0.0, 8.21, 16.58, 22.37, 26.9, 40.27, 41.69),
    (0.0, 3.91, 10.24, 12.58, 19.94, 34.91, 37.57),
    (0.0, 4.25, 7.26, 8.9, 19.7, 35.9, 41.21),
)
EMBED_STEPS = (0.0, 12.89, 18.79, 23.91, 26.27, 28.78, 29.78)
SCATTER_KINDS = (1, 1, 2, 2, 1, 2, 0, 3, 3, 1, 2, 1, 0, 2, 1, 0, 1, 2)
SCATTER_GAPS = (25.71, 3.59, 3.03, 0.0, 0.0, 6.41, 3.94, 8.09, 3.5, 6.46, 5.55, 0.81, 3.15, 14.45, 2.66, 6.8, 7.04, 4.49)
SCATTER_STEPS = (
    (0.0, 6.87, 21.13, 26.44, 40.85, 54.69, 60.91),
    (0.0, 5.03, 17.82, 22.88, 27.78, 34.13, 41.63),
    (0.0, 4.01, 18.98, 26.43, 32.91, 38.1, 43.98),
    (0.0, 1.86, 12.09, 19.21, 25.88, 31.23, 48.54),
)
PACE = 1.326


class Plan:
    def __init__(self, dims, count):
        self.dims = dims
        self.tabled = dims == (4, 2, 2) and count == len(GATHER_START)
        self.gather_kinds = GATHER_KINDS if self.tabled else [k % 2 for k in range(count)]
        self.scatter_kinds = SCATTER_KINDS if self.tabled else [k % 2 for k in range(count)]
        self.gaps = SCATTER_GAPS if self.tabled else [CHUNK] * count
        self.pace = PACE if self.tabled else 1.0

    def steps(self, order, back):
        units = [math.prod(self.dims[a] for a in order[:k]) for k in range(3) for _ in range(self.dims[order[k]] - 1)]
        times = [0.0, 3.0] if back else [0.0]
        for unit in reversed(units) if back else units:
            times.append(times[-1] + 1.6 * unit + 3.0)
        return times if back else times + [times[-1] + 4.0]

    def gather(self, c):
        kind = self.gather_kinds[c]
        if self.tabled:
            return KINDS[kind], [GATHER_START[c] + t for t in GATHER_STEPS[kind]]
        return KINDS[kind], [CHUNK * c + t for t in self.steps(KINDS[kind], False)]

    def scatter(self, c):
        kind = self.scatter_kinds[c]
        return KINDS[kind], SCATTER_STEPS[kind] if self.tabled else self.steps(KINDS[kind], True)

    def embeddings(self, start):
        order = (2, 1, 0)
        return order, [start + t for t in (EMBED_STEPS if self.tabled else self.steps(order, False))]


def fused_kernel(dims, sizes, refs):
    layer = Layer(dims, sizes, refs)
    blocks = sizes.hidden_blocks
    layer.sent, layer.ends, layer.sending, layer.ring_sent = [], [], {}, {}
    timeline = Timeline()

    loads = layer.load()
    layer.own_emb[...] = jnp.zeros_like(layer.own_emb)
    ready = {}
    plan = Plan(dims, FFN + 2 * blocks)
    for c, name in enumerate(range(FFN + 2 * blocks)):
        order, times = plan.gather(c)
        timeline.add_steps([-1.0] + times, layer.gather(c, name, order))
        ready[name] = times[-1]
    timeline.add(-0.5, lambda: greet_lines(layer.place))

    clock = [0.0]

    def compute(fn, cost, *needs):
        clock[0] = max([clock[0] + 0.001] + [ready[n] + 0.01 for n in needs])
        timeline.add(clock[0], fn)
        clock[0] += cost * plan.pace
        return clock[0]

    def arrived():
        for copy in loads:
            copy.wait()

    compute(arrived, 0.1)
    compute(layer.image_features, 1.6, IMAGE)
    compute(layer.region, 0.8)
    compute(layer.self_projections, 2.0, QUERY, KEY, VALUE)
    compute(layer.self_attention, 4.0)
    compute(layer.norm_params, 0.2, SMALL)
    compute(layer.pools, 0.3)
    start = compute(layer.embed, 0.3)
    order, times = plan.embeddings(start)
    timeline.add_steps(times, layer.gather_embeddings(len(ready), order))
    ready[EMBEDDINGS] = times[-1]
    compute(layer.after_self, 2.7, ATTN_OUT)
    compute(layer.make_keys, 2.3, CROSS_KEY)
    compute(layer.make_values, 2.3, CROSS_VALUE)
    compute(layer.cross_query, 0.6, CROSS_QUERY)
    compute(layer.cross_attention, 4.5)
    compute(layer.after_cross, 2.0, CROSS_OUT)
    compute(lambda: layer.settle([SMALL]), 0.0, EMBEDDINGS)
    compute(layer.contrast, 4.0)
    for k in range(blocks):
        compute(functools.partial(layer.ffn_in, k), 1.6, FFN + k)
    for k in range(blocks):
        compute(functools.partial(layer.ffn_out, k), 1.0, FFN + blocks + k)

    done = {}
    compute(layer.output_and_back, 4.0)
    compute(lambda: layer.settle(list(layer.sending)), 0.0)
    compute(layer.joined_over, 0.1)
    for k in range(blocks):
        done[FFN + blocks + k] = compute(functools.partial(layer.ffn_out_back, k), 2.2)
    for k in range(blocks):
        done[FFN + k] = compute(functools.partial(layer.ffn_in_back, k), 1.9)
    compute(functools.partial(layer.back_through_norm, 1), 1.8)
    done[CROSS_OUT] = compute(lambda: layer.branch_back(CROSS_OUT, layer.a2), 1.8)
    compute(layer.cross_attention_back, 5.0)
    done[CROSS_QUERY] = compute(layer.cross_query_back, 1.5)
    compute(layer.image_back, 5.0)
    done[CROSS_KEY] = compute(lambda: layer.cross_key_back(CROSS_KEY, layer.k2), 2.4)
    done[CROSS_VALUE] = compute(lambda: layer.cross_key_back(CROSS_VALUE, layer.v2), 2.4)
    compute(layer.patch_back, 5.5)
    done[IMAGE] = compute(layer.image_weight_back, 2.3)
    compute(lambda: layer.credit(RING, True), 0.1)
    compute(functools.partial(layer.back_through_norm, 0), 1.8)
    done[ATTN_OUT] = compute(lambda: layer.branch_back(ATTN_OUT, layer.a1), 1.8)
    done[SMALL] = compute(layer.small_grads, 0.5)
    compute(layer.self_attention_back, 5.0)
    for k, name in enumerate((QUERY, KEY, VALUE)):
        done[name] = compute(functools.partial(layer.self_projection_back, k), 1.5)
    compute(layer.text_out, 2.0)

    start, ends = 0.0, []
    for c, name in enumerate(grad_order(blocks)):
        order, steps = plan.scatter(c)
        start = max(start + plan.gaps[c], done[name])
        if name != IMAGE and len(ends) >= RING:
            start = max(start, ends[len(ends) - RING] + 0.1)
        times = [start + 0.02 + t for t in steps]
        if name in (IMAGE, SMALL):
            times.append(times[-1] + 3.0)
        timeline.add_steps(times, layer.scatter(c, len(ends), name, order, sizes.ring_total))
        if name != IMAGE:
            ends.append(times[len(steps) - 1])
    timeline.run()
    assert not layer.sending
    for end in layer.ends:
        end()
    for sent in (layer.sent, *layer.ring_sent.values()):
        wait_sent(sent)
    assert layer.blocks.top <= layer.t.shape[0], layer.blocks.top
    assert layer.wide.top <= layer.u.shape[0], layer.wide.top


def fused_body(
    text,
    patches,
    cotangent,
    region_counts,
    phrase_starts,
    phrase_lengths,
    box_patches,
    query_weight,
    key_weight,
    value_weight,
    attn_out_weight,
    cross_query_weight,
    cross_key_weight,
    cross_value_weight,
    cross_out_weight,
    image_weight,
    ffn_in_weight,
    ffn_out_weight,
    text_embed_weight,
    image_embed_weight,
    *norm_shards,
):
    dims = split_dims(lax.axis_size("dp"))
    mp = lax.axis_index("mp")
    pairs, patch_count, depth = patches.shape
    length, model_width = text.shape[1:]
    half = query_weight.shape[1]
    rows = query_weight.shape[0]
    hidden_blocks = ffn_in_weight.shape[1] // half
    embed_half = text_embed_weight.shape[1] // 2

    def own_half(x, size, dim):
        return lax.dynamic_slice_in_dim(x, mp * size, size, dim)

    def padded(x, to):
        x = jnp.pad(x, ((0, 0), (0, to - x.shape[1]), (0, 0)))
        return x.reshape(-1, x.shape[-1])

    small = jnp.concatenate(
        [own_half(text_embed_weight, embed_half, 1), own_half(image_embed_weight, embed_half, 1)]
        + [jnp.pad(jnp.stack(norm_shards, 1), ((0, 0), (0, half - 2 * embed_half - len(norm_shards))))],
        1,
    )
    ffn_out_t = ffn_out_weight.T
    shards = {
        IMAGE: own_half(image_weight, half, 1),
        QUERY: query_weight,
        KEY: key_weight,
        VALUE: value_weight,
        ATTN_OUT: attn_out_weight.T,
        SMALL: small,
        CROSS_KEY: cross_key_weight,
        CROSS_VALUE: cross_value_weight,
        CROSS_QUERY: cross_query_weight,
        CROSS_OUT: cross_out_weight.T,
    }
    for k in range(hidden_blocks):
        shards[FFN + k] = ffn_in_weight[:, k * half : (k + 1) * half]
        shards[FFN + hidden_blocks + k] = ffn_out_t[:, k * half : (k + 1) * half]
    order = range(FFN + 2 * hidden_blocks)
    sizes = types.SimpleNamespace(
        pairs=pairs,
        length=length,
        patch_count=patch_count,
        half=half,
        hidden_blocks=hidden_blocks,
        embed_half=embed_half,
        ring_total=len(order) - 1,
    )
    count, text_rows, patch_rows = len(order), pairs * TEXT_PAD, pairs * PATCH_PAD
    couples = model_width // 128
    anywhere, vmem = pl.BlockSpec(memory_space=pl.ANY), pl.BlockSpec(memory_space=pltpu.VMEM)

    inputs = dict(
        text_in=(padded(own_half(text, pairs, 0), TEXT_PAD), anywhere),
        cot_in=(padded(own_half(cotangent, pairs, 0), TEXT_PAD), anywhere),
        patches_in=(padded(patches, PATCH_PAD), anywhere),
        counts=(region_counts.reshape(-1, 1), vmem),
        starts=(phrase_starts, vmem),
        lengths=(phrase_lengths, vmem),
        picks=(box_patches, vmem),
    )
    outputs = dict(
        joined_out=(jax.ShapeDtypeStruct((2, pairs, length, model_width), BF16), anywhere),
        text_out_ref=(jax.ShapeDtypeStruct((2, pairs, length, model_width), F32), anywhere),
        patch_grad=(jax.ShapeDtypeStruct((pairs, patch_count, depth), F32), anywhere),
    )
    result_shapes = []
    for name in order:
        shape = shards[name].shape
        result_shapes.append(jax.ShapeDtypeStruct(((2,) if name in (IMAGE, SMALL) else ()) + shape, F32))
    units = max(arrive_units(dims, o) for o in KINDS)
    dma, regular = pltpu.SemaphoreType.DMA, pltpu.SemaphoreType.REGULAR
    scratch = dict(
        t=pltpu.VMEM((42, text_rows, half), BF16),
        u=pltpu.VMEM((8, patch_rows, half), BF16),
        patches=pltpu.VMEM((patch_rows, depth), BF16),
        p1=pltpu.VMEM((pairs, couples * TEXT_PAD, 2 * TEXT_PAD), BF16),
        p2=pltpu.VMEM((pairs, couples * TEXT_PAD, 2 * PATCH_PAD), BF16),
        z=pltpu.VMEM((text_rows, model_width), F32),
        hid=pltpu.VMEM((text_rows, model_width), F32),
        inv=pltpu.VMEM((2, text_rows, 1), F32),
        norms=pltpu.VMEM((8, model_width), F32),
        norm_grad=pltpu.VMEM((8, model_width), F32),
        pool=pltpu.VMEM((2, 16, model_width), F32),
        raw=pltpu.VMEM((2, 16, 2 * embed_half), F32),
        own_emb=pltpu.VMEM((16, 4 * embed_half), BF16),
        emb=pltpu.VMEM((2,) + dims + (16, 4 * embed_half), BF16),
        extra=pltpu.VMEM((2, 16, model_width), F32),
        chosen=pltpu.VMEM((pairs, 8, PATCH_PAD), F32),
        span=pltpu.VMEM((pairs, TEXT_PAD, 8), F32),
        regions=pltpu.VMEM((pairs, 8, model_width), F32),
        joined=pltpu.VMEM((pairs, length, model_width), BF16),
        text_stage=pltpu.VMEM((2, length, model_width), F32),
        patch_stage=pltpu.VMEM((2, patch_count, depth), F32),
        peer_in=pltpu.VMEM((RING,) + dims + (rows, half), BF16),
        arrive=pltpu.VMEM((RING, units, rows, half), BF16),
        load_sem=dma((5,)),
        own_sem=dma((count,)),
        g_send=dma((count + 1, send_slots(dims))),
        g_recv=dma((count + 1, gather_slots(dims))),
        gp_send=dma((count + 1,)),
        gp_recv=dma((count + 1,)),
        s_send=dma((RING + 1, send_slots(dims))),
        s_recv=dma((RING + 1, send_slots(dims))),
        sp_send=dma((RING + 1,)),
        sp_recv=dma((RING + 1,)),
        h_send=dma((2,)),
        h_recv=dma((2,)),
        out_own=dma,
        out_send=dma,
        out_recv=dma,
        text_own=dma((pairs,)),
        text_send=dma((pairs,)),
        text_recv=dma((pairs,)),
        patch_sem=dma((2,)),
        credits=regular((RING + 1, 7)),
    )
    weights = [pltpu.VMEM((2,) + dims + shards[name].shape, BF16) for name in order]

    def kernel(*refs):
        refs = list(refs)

        def some(names):
            part = dict(zip(names, refs))
            del refs[: len(part)]
            return part

        table = some(inputs)
        table.update(shards=some(order))
        table.update(some(outputs))
        table.update(results=some(order))
        table.update(some(scratch))
        table.update(w=some(order))
        fused_kernel(dims, sizes, table)

    results = pl.pallas_call(
        kernel,
        out_shape=[s for s, _ in outputs.values()] + result_shapes,
        in_specs=[spec for _, spec in inputs.values()] + [anywhere] * count,
        out_specs=[spec for _, spec in outputs.values()] + [vmem] * count,
        scratch_shapes=list(scratch.values()) + weights,
        compiler_params=pltpu.CompilerParams(
            collective_id=2, has_side_effects=True, vmem_limit_bytes=64 * 2**20
        ),
        name="layer",
    )(*[x for x, _ in inputs.values()], *[shards[n] for n in order])
    joined, text_grad = (r.reshape(2 * pairs, length, model_width) for r in results[:2])
    own = dict(zip(order, results[3:]))

    def columns(x, start, width):
        return jnp.concatenate([x[0, :, start : start + width], x[1, :, start : start + width]], 1)

    norm_own = lax.dynamic_index_in_dim(own[SMALL], mp, 0, keepdims=False)[:, 2 * embed_half :]
    return (
        joined,
        text_grad,
        results[2],
        own[QUERY],
        own[KEY],
        own[VALUE],
        own[ATTN_OUT].T,
        own[CROSS_QUERY],
        own[CROSS_KEY],
        own[CROSS_VALUE],
        own[CROSS_OUT].T,
        columns(own[IMAGE], 0, half),
        jnp.concatenate([own[FFN + k] for k in range(hidden_blocks)], 1),
        jnp.concatenate([own[FFN + hidden_blocks + k] for k in range(hidden_blocks)], 1).T,
        columns(own[SMALL], 0, embed_half),
        columns(own[SMALL], embed_half, embed_half),
        *(norm_own[:, k] for k in range(len(norm_shards))),
    )


def pad_rows(x, rows):
    return jnp.pad(x, ((0, rows - x.shape[0]), (0, 0)))


def body(
    text,
    patches,
    cotangent,
    region_counts,
    phrase_starts,
    phrase_lengths,
    box_patches,
    query_weight,
    key_weight,
    value_weight,
    attn_out_weight,
    cross_query_weight,
    cross_key_weight,
    cross_value_weight,
    cross_out_weight,
    image_weight,
    ffn_in_weight,
    ffn_out_weight,
    text_embed_weight,
    image_embed_weight,
    *norm_shards,
):
    dp = lax.axis_size("dp")
    dims = split_dims(dp)
    mp = lax.axis_index("mp")
    half_pairs, patch_count, _ = patches.shape
    length, model_width = text.shape[1:]
    half = query_weight.shape[1]
    rows = query_weight.shape[0]
    hidden_blocks = ffn_in_weight.shape[1] // half
    embed_half = text_embed_weight.shape[1] // 2
    image_rows_own = image_weight.shape[0]

    if rows % 16 == 0 and dims[0] % 2 == 0 and half % 128 == 0 and half == model_width // 2 and half_pairs % 2 == 0:
        return fused_body(
            text, patches, cotangent, region_counts, phrase_starts, phrase_lengths, box_patches,
            query_weight, key_weight, value_weight, attn_out_weight, cross_query_weight, cross_key_weight,
            cross_value_weight, cross_out_weight, image_weight, ffn_in_weight, ffn_out_weight,
            text_embed_weight, image_embed_weight, *norm_shards,
        )

    def own_half(x, size, dim):
        return lax.dynamic_slice_in_dim(x, mp * size, size, dim)

    text, cotangent = own_half(text, half_pairs, 0), own_half(cotangent, half_pairs, 0)
    region_counts, phrase_starts = own_half(region_counts, half_pairs, 0), own_half(phrase_starts, half_pairs, 0)
    phrase_lengths, box_patches = own_half(phrase_lengths, half_pairs, 0), own_half(box_patches, half_pairs, 0)

    padded = -(-rows // 16) * 16
    small = jnp.concatenate(
        [own_half(text_embed_weight, embed_half, 1), own_half(image_embed_weight, embed_half, 1)]
        + [jnp.pad(jnp.stack(norm_shards, 1), ((0, 0), (0, half - 2 * embed_half - len(norm_shards))))],
        1,
    )
    ffn_out_t = ffn_out_weight.T
    shards = [
        own_half(image_weight, half, 1),
        query_weight,
        key_weight,
        value_weight,
        attn_out_weight.T,
        small,
        cross_key_weight,
        cross_value_weight,
        cross_query_weight,
        cross_out_weight.T,
        *(ffn_in_weight[:, k * half : (k + 1) * half] for k in range(hidden_blocks)),
        *(ffn_out_t[:, k * half : (k + 1) * half] for k in range(hidden_blocks)),
    ]
    real = [s.shape[0] for s in shards]
    shards = [pad_rows(s, -(-s.shape[0] // 16) * 16) for s in shards]
    gathered = gather(shards, dims)

    def merge(g, n):
        g = g.reshape(2, dp, *g.shape[-2:])[:, :, :n]
        return g.reshape(2, dp * n, g.shape[-1])

    gathered = [merge(g, n) for g, n in zip(gathered, real)]

    def columns(g):
        return jnp.concatenate([g[0], g[1]], 1)

    def blocks(gs):
        return jnp.concatenate([g[0] for g in gs] + [g[1] for g in gs], 1)

    image_w, query_w, key_w, value_w, attn_out_t = (columns(g) for g in gathered[:5])
    embeds = gathered[5]
    text_embed32 = columns(embeds[:, :, :embed_half]).astype(F32)
    image_embed32 = columns(embeds[:, :, embed_half : 2 * embed_half]).astype(F32)
    norms = embeds[0, :, 2 * embed_half : 2 * embed_half + len(norm_shards)].astype(F32).T
    gain_one, bias_one, gain_two, bias_two, gain_three, bias_three = (norms[k] for k in range(6))
    cross_key_w, cross_value_w, cross_query_w, cross_out_t = (columns(g) for g in gathered[6:10])
    ffn_in_w = blocks(gathered[10 : 10 + hidden_blocks])
    ffn_out_tw = blocks(gathered[10 + hidden_blocks :])

    text_rows = text.reshape(half_pairs * length, model_width)
    patch_rows = patches.reshape(half_pairs * patch_count, -1)
    image_rows = matmul(patch_rows, image_w).astype(BF16)
    image32 = image_rows.astype(F32).reshape(half_pairs, patch_count, model_width)
    queries = split_heads(matmul(text_rows, query_w).astype(BF16), half_pairs)
    key_heads = split_heads(matmul(text_rows, key_w).astype(BF16), half_pairs)
    value_heads = split_heads(matmul(text_rows, value_w).astype(BF16), half_pairs)
    self_mixed, self_total = attend(queries, key_heads, value_heads)
    first = text_rows.astype(F32) + contract_cols(self_mixed, attn_out_t)
    hidden_one, normed_one, inv_one = layer_norm(first, gain_one, bias_one)
    low_one = hidden_one.astype(BF16)
    cross_queries = split_heads(matmul(low_one, cross_query_w).astype(BF16), half_pairs)
    cross_keys = split_heads(matmul(image_rows, cross_key_w).astype(BF16), half_pairs)
    cross_values = split_heads(matmul(image_rows, cross_value_w).astype(BF16), half_pairs)
    cross_mixed, cross_total = attend(cross_queries, cross_keys, cross_values)
    second = hidden_one + contract_cols(cross_mixed, cross_out_t)
    hidden_two, normed_two, inv_two = layer_norm(second, gain_two, bias_two)
    low_two = hidden_two.astype(BF16)
    inner = matmul(low_two, ffn_in_w)
    active = jax.nn.gelu(inner, approximate=False).astype(BF16)
    third = hidden_two + contract_cols(active, ffn_out_tw)
    output, normed_three, inv_three = layer_norm(third, gain_three, bias_three)
    output3 = output.reshape(half_pairs, length, model_width)
    joined = output3.astype(BF16)

    text_pool = jnp.mean(text.astype(F32), 1)
    image_pool = jnp.mean(image32, 1)
    grad_text_embed, grad_image_embed, text_extra, image_pool_grad = contrast(
        text_pool, image_pool, text_embed32, image_embed32
    )
    text_extra = (text_extra / length)[:, None, :]
    image_pool_grad = image_pool_grad / patch_count
    positions = jnp.arange(length, dtype=jnp.int32)
    slots = jnp.arange(phrase_starts.shape[1], dtype=jnp.int32)
    valid = (slots[None, :] < region_counts[:, None]).astype(F32)
    ends = phrase_starts + phrase_lengths
    inside = ((positions >= phrase_starts[..., None]) & (positions < ends[..., None])).astype(F32) * valid[..., None]
    span_weight = inside / phrase_lengths[..., None].astype(F32)
    chosen = (
        jnp.sum((box_patches[..., None] == jnp.arange(patch_count, dtype=jnp.int32)).astype(F32), axis=2)
        / box_patches.shape[2]
    )
    phrase = jnp.einsum("pbt,ptd->pbd", span_weight, output3, precision=HIGHEST)
    region = jnp.einsum("pbn,pnd->pbd", chosen, image32, precision=HIGHEST)
    mismatch = (phrase - region) * valid[..., None]
    box_text = jnp.einsum("pbt,pbd->ptd", span_weight, mismatch, precision=HIGHEST)
    box_image = -jnp.einsum("pbn,pbd->pnd", chosen, mismatch, precision=HIGHEST)
    image_extra = (box_image + image_pool_grad[:, None, :]).reshape(-1, model_width)

    upstream = cotangent.astype(F32).reshape(-1, model_width) + box_text.reshape(-1, model_width)
    grad_third, gain_three_grad, bias_three_grad = norm_back(upstream, normed_three, inv_three, gain_three)
    low_third = grad_third.astype(BF16)
    grad_ffn_out_t = contract_rows(low_third, active)
    dactive = matmul(low_third, ffn_out_tw)
    gelu_pull = jax.vjp(lambda values: jax.nn.gelu(values, approximate=False), inner)[1]
    dinner = gelu_pull(dactive)[0].astype(BF16)
    grad_ffn_in = contract_rows(low_two, dinner)
    grad_second = grad_third + contract_cols(dinner, ffn_in_w)
    grad_second, gain_two_grad, bias_two_grad = norm_back(grad_second, normed_two, inv_two, gain_two)
    low_second = grad_second.astype(BF16)
    grad_cross_out_t = contract_rows(low_second, cross_mixed)
    dcross = split_heads(matmul(low_second, cross_out_t).astype(BF16), half_pairs)
    dqueries, dkeys, dvalues = attend_back(cross_queries, cross_keys, cross_values, cross_total, dcross)
    grad_cross_query = contract_rows(low_one, dqueries)
    grad_first = grad_second + contract_cols(dqueries, cross_query_w)
    grad_cross_key = contract_rows(image_rows, dkeys)
    grad_cross_value = contract_rows(image_rows, dvalues)
    dimage = contract_cols(dkeys, cross_key_w) + contract_cols(dvalues, cross_value_w) + image_extra
    low_image = dimage.astype(BF16)
    grad_image = contract_rows(patch_rows, low_image)
    patch_grad = contract_cols(low_image, image_w).reshape(patches.shape)
    grad_first, gain_one_grad, bias_one_grad = norm_back(grad_first, normed_one, inv_one, gain_one)
    low_first = grad_first.astype(BF16)
    grad_attn_out_t = contract_rows(low_first, self_mixed)
    dself = split_heads(matmul(low_first, attn_out_t).astype(BF16), half_pairs)
    dqueries, dkeys, dvalues = attend_back(queries, key_heads, value_heads, self_total, dself)
    grad_query = contract_rows(text_rows, dqueries)
    grad_key = contract_rows(text_rows, dkeys)
    grad_value = contract_rows(text_rows, dvalues)
    dtext = contract_cols(dqueries, query_w) + contract_cols(dkeys, key_w) + contract_cols(dvalues, value_w)
    text_grad = (grad_first + dtext).reshape(half_pairs, length, model_width) + text_extra

    def halves(g):
        g = g.astype(BF16)
        return jnp.stack([g[:, :half], g[:, half:]], 0)

    def hidden_halves(g):
        g = g.astype(BF16)
        return [
            jnp.stack([g[:, k * half : (k + 1) * half], g[:, (hidden_blocks + k) * half : (hidden_blocks + k + 1) * half]])
            for k in range(hidden_blocks)
        ]

    norm_grads = jnp.stack(
        [gain_one_grad, bias_one_grad, gain_two_grad, bias_two_grad, gain_three_grad, bias_three_grad], 1
    ).astype(BF16)
    norm_grads = jnp.pad(norm_grads, ((0, 0), (0, half - 2 * embed_half - len(norm_shards))))
    text_half, image_half = grad_text_embed.astype(BF16), grad_image_embed.astype(BF16)
    small_grads = jnp.stack(
        [
            jnp.concatenate(
                [text_half[:, k * embed_half : (k + 1) * embed_half], image_half[:, k * embed_half : (k + 1) * embed_half], norm_grads], 1
            )
            for k in range(2)
        ]
    )
    grads = [
        *hidden_halves(grad_ffn_out_t),
        *hidden_halves(grad_ffn_in),
        halves(grad_cross_out_t),
        halves(grad_cross_query),
        halves(grad_cross_key),
        halves(grad_cross_value),
        halves(grad_image),
        halves(grad_attn_out_t),
        halves(grad_query),
        halves(grad_key),
        halves(grad_value),
        small_grads,
    ]
    shared = (2 * hidden_blocks + 4, len(grads) - 1)

    def cut(g):
        n = g.shape[1] // dp
        g = g.reshape(2, dp, n, g.shape[-1])
        g = jnp.pad(g, ((0, 0), (0, 0), (0, -(-n // 16) * 16 - n), (0, 0)))
        return g.reshape(2, *dims, *g.shape[-2:])

    results = scatter([cut(g) for g in grads], shared, (joined, text_grad), dims)
    joined_all, text_grad_all = (r.reshape(2 * half_pairs, length, model_width) for r in results[len(grads) :])
    sums = [r[..., :n, :] for r, n in zip(results, [g.shape[1] // dp for g in grads])]
    ffn_out_own = jnp.concatenate(sums[:hidden_blocks], 1).T
    ffn_in_own = jnp.concatenate(sums[hidden_blocks : 2 * hidden_blocks], 1)
    cross_out_own, cross_query_own, cross_key_own, cross_value_own, image_own, attn_out_own, query_own, key_own, value_own, small_own = sums[2 * hidden_blocks :]
    own_norm = lax.dynamic_index_in_dim(small_own, mp, 0, keepdims=False)[:, 2 * embed_half :]
    return (
        joined_all,
        text_grad_all,
        patch_grad,
        query_own,
        key_own,
        value_own,
        attn_out_own.T,
        cross_query_own,
        cross_key_own,
        cross_value_own,
        cross_out_own.T,
        jnp.concatenate([image_own[0], image_own[1]], 1),
        ffn_in_own,
        ffn_out_own,
        jnp.concatenate([small_own[0, :, :embed_half], small_own[1, :, :embed_half]], 1),
        jnp.concatenate([small_own[0, :, embed_half : 2 * embed_half], small_own[1, :, embed_half : 2 * embed_half]], 1),
        own_norm[:, 0],
        own_norm[:, 1],
        own_norm[:, 2],
        own_norm[:, 3],
        own_norm[:, 4],
        own_norm[:, 5],
    )


def solution(mesh):
    pairs, weight, turned, single = P("dp", None, None), P("dp", "mp"), P("mp", "dp"), P("dp", None)
    weights = (weight, weight, weight, turned, weight, weight, weight, turned, single, weight, turned, single, single)
    norms = (P("dp"),) * 6
    halves = P(("dp", "mp"), None, None)
    in_specs = (pairs, halves, pairs, P("dp"), single, single, pairs) + weights + norms
    out_specs = (pairs, pairs, halves) + weights + norms
    return jax.shard_map(body, mesh=mesh, in_specs=in_specs, out_specs=out_specs, check_vma=False)
```

```python
import functools
import math
import types

import jax
import jax.numpy as jnp
from jax import lax
from jax.experimental import pallas as pl
from jax.experimental.pallas import tpu as pltpu
from jax.sharding import PartitionSpec as P

HEAD_DIM = 64
EPS = 1e-06
TEMP_INVERSE = 20.0
GRAD_SCALE = 10.0
HIGHEST = lax.Precision.HIGHEST
MESH = pl.DeviceIdType.MESH
BF16 = jnp.bfloat16
F32 = jnp.float32


def split_dims(count):
    side = math.isqrt(count // 4) if count % 4 == 0 else 0
    if side and 4 * side * side == count:
        return (4, side, side)
    return (count, 1, 1)


class Place:
    def __init__(self, dims):
        self.dims = dims
        dp = lax.axis_index("dp")
        self.mp = lax.axis_index("mp")
        self.pos = (dp // (dims[1] * dims[2]), (dp // dims[2]) % dims[1], dp % dims[2])

    def at(self, axis, coord):
        spot = list(self.pos)
        spot[axis] = coord
        return ((spot[0] * self.dims[1] + spot[1]) * self.dims[2] + spot[2], self.mp)

    def peer(self):
        return (lax.axis_index("dp"), 1 - self.mp)


def block_of(place, order, stage, coord):
    index = [None] * 3
    for rank, axis in enumerate(order):
        index[axis] = slice(None) if rank < stage else (coord if rank == stage else place.pos[axis])
    return tuple(index)


def remote(src, dst, send_sem, recv_sem, device):
    return pltpu.make_async_remote_copy(
        src_ref=src,
        dst_ref=dst,
        send_sem=send_sem,
        recv_sem=recv_sem,
        device_id=device,
        device_id_type=MESH,
    )


def greet_lines(place):
    sem = pltpu.get_barrier_semaphore()

    def greet(device):
        pl.semaphore_signal(sem, inc=1, device_id=device, device_id_type=MESH)

    greet(place.peer())
    count = 1
    for axis in range(3):
        for away in range(1, place.dims[axis]):
            greet(place.at(axis, lax.rem(place.pos[axis] + away, place.dims[axis])))
            count += 1
    pl.semaphore_wait(sem, count)


def line_slots(length):
    return (2 if length > 2 else 1) * (length - 1)


def line_slot(dims, axis, way, step):
    length = dims[axis]
    return sum(line_slots(d) for d in dims[:axis]) + (way * (length - 1) if length > 2 else 0) + step - 1


def send_slots(dims):
    return sum(line_slots(d) for d in dims)


def gather_slots(dims):
    return sum(d - 1 for d in dims)


def gather_steps(place, order, buf, send_sem, recv_sem):
    sent = []
    for stage, axis in enumerate(order):
        length, pos = place.dims[axis], place.pos[axis]
        if length == 1:
            continue
        base = sum(d - 1 for d in place.dims[:axis])

        def copy(way, step, coord, to, stage=stage, axis=axis, pos=pos, base=base):
            ref = buf.at[block_of(place, order, stage, coord)]
            arrival = recv_sem.at[base + coord - (coord > to).astype(jnp.int32)]
            return remote(ref, ref, send_sem.at[line_slot(place.dims, axis, way, step)], arrival, place.at(axis, to))

        for step in range(1, length + 1):
            for way in (0, 1):
                coord = pos - (step - 1) if way == 0 else pos + (step - 1)
                to = pos + 1 if way == 0 else pos - 1
                here = (coord >= 0) if way == 0 else (coord < length)
                if step > 1:
                    pl.when(here)(lambda: copy(way, step - 1, coord, pos).wait_recv())
                if step < length:
                    more = jnp.logical_and(here, (to < length) if way == 0 else (to >= 0))
                    pl.when(more)(lambda: copy(way, step, coord, to).start())
                    sent.append((more, functools.partial(copy, way, step, coord, to)))
            if step < length:
                yield
    return sent


def scatter_steps(place, order, acc, arrive, send_sem, recv_sem, result):
    sent = []
    last = [axis for axis in order if place.dims[axis] > 1][0]
    at = 0
    for stage in reversed(range(3)):
        axis = order[stage]
        length, pos = place.dims[axis], place.pos[axis]
        if length == 1:
            continue
        units = math.prod(place.dims[a] for a in order[:stage])
        shape = tuple(place.dims[a] for a in sorted(order[:stage]))

        def copy(way, step, coord, stage=stage, axis=axis, pos=pos, at=at, units=units, length=length, shape=shape):
            src = acc.at[block_of(place, order, stage, coord)]
            slot = at + ((way * (length - 1) if length > 2 else 0) + step - 1) * units
            dst = arrive.at[pl.ds(slot, units)].reshape(*shape, *arrive.shape[1:])
            sem = line_slot(place.dims, axis, way, step)
            device = place.at(axis, pos + 1 if way == 0 else pos - 1)
            return remote(src, dst, send_sem.at[sem], recv_sem.at[sem], device), dst

        for step in range(length - 1, 0, -1):
            for way in (0, 1):
                coord = pos + step if way == 0 else pos - step
                has = (coord < length) if way == 0 else (coord >= 0)
                pl.when(has)(lambda: copy(way, step, coord)[0].start())
                sent.append((has, functools.partial(lambda move, *a: move(*a)[0], copy, way, step, coord)))
            yield
            for way in (0, 1):
                coord = pos - 1 + step if way == 0 else pos + 1 - step
                if way == 0:
                    comes = jnp.logical_and(pos > 0, coord < length)
                else:
                    comes = jnp.logical_and(pos < length - 1, coord >= 0)

                def take():
                    move, ref = copy(way, step, coord)
                    move.wait_recv()
                    index = block_of(place, order, stage, coord)
                    if axis == last and step == 1:
                        total = acc[index].astype(F32) + ref[...].astype(F32)
                        result[...] = total
                        acc[index] = total.astype(BF16)
                    else:
                        acc[index] = acc[index] + ref[...]

                pl.when(comes)(take)
        at += line_slots(length) * units
    return sent


def arrive_units(dims, order):
    units = 0
    for stage in range(3):
        if dims[order[stage]] > 1:
            length = dims[order[stage]]
            units += (2 if length > 2 else 1) * (length - 1) * math.prod(dims[a] for a in order[:stage])
    return units


def in_turn(plan):
    events = sorted((time, which, step) for which, (times, _) in enumerate(plan) for step, time in enumerate(times))
    results = [None] * len(plan)
    for _, which, _ in events:
        if results[which] is None:
            try:
                next(plan[which][1])
            except StopIteration as stop:
                results[which] = stop.value
    assert all(r is not None for r in results)
    return results


def wait_sent(sent):
    for cond, make in sent:
        if cond is None:
            make().wait_send()
        else:
            pl.when(cond)(lambda: make().wait_send())


ORDERS = ((2, 0, 1), (1, 0, 2), (0, 2, 1), (2, 0, 1), (1, 0, 2), (0, 1, 2))


def step_times(dims, order, start, back=False):
    times = [0.0]
    units = 1
    for axis in order:
        for _ in range(dims[axis] - 1):
            times.append(times[-1] + 1.6 * units + 3.0)
        units *= dims[axis]
    times.append(times[-1] + 4.0)
    if back:
        times = [times[-1] - t for t in reversed(times)]
    return [start + t for t in times] + [start + times[-1] + 4.0, start + times[-1] + 8.0]


def gather_kernel(dims, count, *refs):
    ins, outs = refs[:count], refs[count : 2 * count]
    send_sem, recv_sem, own_sem, peer_send, peer_recv = refs[2 * count :]
    place = Place(dims)
    own = [
        pltpu.make_async_copy(ins[c], outs[c].at[(place.mp,) + place.pos], own_sem.at[c]) for c in range(count)
    ]
    for copy in own:
        copy.start()
    greet_lines(place)

    def chunk(c, order):
        own[c].wait()
        mine, other = outs[c].at[place.mp], outs[c].at[1 - place.mp]
        sent = yield from gather_steps(place, order, mine, send_sem.at[c], recv_sem.at[c])

        def copy(ref):
            return remote(ref, ref, peer_send.at[c], peer_recv.at[c], place.peer())

        copy(mine).start()
        yield
        copy(other).wait_recv()
        return sent + [(None, lambda: copy(mine))]

    plan = []
    for c in range(count):
        order = ORDERS[c % len(ORDERS)]
        plan.append((step_times(dims, order, 3.9 * c), chunk(c, order)))
    for sent in in_turn(plan):
        wait_sent(sent)


def gather(shards, dims):
    count = len(shards)
    return pl.pallas_call(
        functools.partial(gather_kernel, dims, count),
        out_shape=[jax.ShapeDtypeStruct((2,) + dims + s.shape, BF16) for s in shards],
        in_specs=[pl.BlockSpec(memory_space=pl.ANY)] * count,
        out_specs=[pl.BlockSpec(memory_space=pl.ANY)] * count,
        scratch_shapes=[
            pltpu.SemaphoreType.DMA((count, send_slots(dims))),
            pltpu.SemaphoreType.DMA((count, gather_slots(dims))),
        ]
        + [pltpu.SemaphoreType.DMA((count,))] * 3,
        compiler_params=pltpu.CompilerParams(collective_id=0, has_side_effects=True),
        name="gather_weights",
    )(*shards)


def scatter_kernel(dims, count, shared, extra, *refs):
    ins, pieces = refs[:count], refs[count : count + extra]
    refs = refs[count + extra :]
    outs, wholes = refs[:count], refs[count : count + extra]
    refs = refs[count + extra :]
    acc, peer_in, arrive = refs[:count], refs[count : 2 * count], refs[2 * count : 3 * count]
    send_sem, recv_sem, own_sem, peer_send, peer_recv, end_send, end_recv, ex_own, ex_send, ex_recv = refs[3 * count :]
    place = Place(dims)
    own = [pltpu.make_async_copy(ins[c].at[place.mp], acc[c], own_sem.at[c]) for c in range(count)]
    for copy in own:
        copy.start()
    keep = [pltpu.make_async_copy(pieces[e], wholes[e].at[place.mp], ex_own.at[e]) for e in range(extra)]
    for copy in keep:
        copy.start()
    greet_lines(place)
    give = [
        remote(pieces[e], wholes[e].at[place.mp], ex_send.at[e], ex_recv.at[e], place.peer()) for e in range(extra)
    ]

    def chunk(c, order):
        def copy():
            return remote(ins[c].at[1 - place.mp], peer_in[c], peer_send.at[c], peer_recv.at[c], place.peer())

        copy().start()
        yield
        own[c].wait()
        copy().wait_recv()
        acc[c][...] = acc[c][...] + peer_in[c][...]
        result = outs[c].at[place.mp] if c in shared else outs[c]
        sent = yield from scatter_steps(
            place, order, acc[c], arrive[c], send_sem.at[c], recv_sem.at[c], result
        )
        sent.append((None, copy))
        if c in shared:

            def hand(half):
                ref = outs[c].at[half]
                return remote(ref, ref, end_send.at[c], end_recv.at[c], place.peer())

            hand(place.mp).start()
            yield
            hand(1 - place.mp).wait_recv()
            sent.append((None, lambda: hand(place.mp)))
        return sent

    plan = []
    for c in range(count):
        order = ORDERS[c % len(ORDERS)]
        plan.append((step_times(dims, order, 3.9 * c, True), chunk(c, order)))
    for copy in give:
        copy.start()
    for sent in in_turn(plan):
        wait_sent(sent)
    for copy in keep:
        copy.wait()
    for copy in give:
        copy.wait()


def scatter(grads, shared, pieces, dims):
    count, extra = len(grads), len(pieces)
    shapes = [
        jax.ShapeDtypeStruct(((2,) if c in shared else ()) + g.shape[-2:], F32) for c, g in enumerate(grads)
    ]
    wholes = [jax.ShapeDtypeStruct((2,) + p.shape, p.dtype) for p in pieces]
    return pl.pallas_call(
        functools.partial(scatter_kernel, dims, count, shared, extra),
        out_shape=shapes + wholes,
        in_specs=[pl.BlockSpec(memory_space=pl.ANY)] * (count + extra),
        out_specs=[pl.BlockSpec(memory_space=pltpu.VMEM)] * count + [pl.BlockSpec(memory_space=pl.ANY)] * extra,
        scratch_shapes=[pltpu.VMEM(g.shape[1:], BF16) for g in grads] * 2
        + [
            pltpu.VMEM((arrive_units(dims, ORDERS[c % len(ORDERS)]),) + g.shape[-2:], BF16)
            for c, g in enumerate(grads)
        ]
        + [pltpu.SemaphoreType.DMA((count, send_slots(dims)))] * 2
        + [pltpu.SemaphoreType.DMA((count,))] * 5
        + [pltpu.SemaphoreType.DMA((extra,))] * 3,
        compiler_params=pltpu.CompilerParams(
            collective_id=1, has_side_effects=True, vmem_limit_bytes=60 * 2**20
        ),
        name="scatter_gradients",
    )(*grads, *pieces)


def matmul(left, right):
    return jnp.dot(left, right, preferred_element_type=F32)


def contract_rows(left, right):
    return lax.dot_general(left, right, (((0,), (0,)), ((), ())), preferred_element_type=F32)


def contract_cols(left, right):
    return lax.dot_general(left, right, (((1,), (1,)), ((), ())), preferred_element_type=F32)


def layer_norm(inputs, gain, shift):
    centred = inputs - jnp.mean(inputs, -1, keepdims=True)
    inv_std = lax.rsqrt(jnp.mean(centred * centred, -1, keepdims=True) + EPS)
    normed = centred * inv_std
    return (normed * gain + shift, normed, inv_std)


def norm_back(upstream, normed, inv_std, gain):
    scaled = upstream * gain
    inner_mean = jnp.mean(scaled * normed, -1, keepdims=True)
    result = inv_std * (scaled - jnp.mean(scaled, -1, keepdims=True) - normed * inner_mean)
    return (result, jnp.sum(upstream * normed, 0), jnp.sum(upstream, 0))


def split_heads(flat, pair_count):
    return flat.reshape(pair_count, -1, flat.shape[-1] // HEAD_DIM, HEAD_DIM)


def attend(queries, key_heads, value_heads):
    factor = 1.0 / math.sqrt(HEAD_DIM)
    scores = jnp.einsum("pqhd,pkhd->phqk", queries, key_heads, preferred_element_type=F32) * factor
    row_max = jnp.max(scores, -1, keepdims=True)
    expd = jnp.exp(scores - row_max)
    row_sum = jnp.sum(expd, -1, keepdims=True)
    probs = (expd / row_sum).astype(BF16)
    mixed = jnp.einsum("phqk,pkhd->pqhd", probs, value_heads, preferred_element_type=F32)
    flat_rows = queries.shape[0] * queries.shape[1]
    return (mixed.astype(BF16).reshape(flat_rows, -1), row_max + jnp.log(row_sum))


def attend_back(queries, key_heads, value_heads, log_total, upstream):
    factor = 1.0 / math.sqrt(HEAD_DIM)
    scores = jnp.einsum("pqhd,pkhd->phqk", queries, key_heads, preferred_element_type=F32) * factor
    probs = jnp.exp(scores - log_total)
    dprobs = jnp.einsum("pqhd,pkhd->phqk", upstream, value_heads, preferred_element_type=F32)
    dscores = (probs * (dprobs - jnp.sum(dprobs * probs, -1, keepdims=True))).astype(BF16)
    dqueries = jnp.einsum("phqk,pkhd->pqhd", dscores, key_heads, preferred_element_type=F32) * factor
    dkeys = jnp.einsum("phqk,pqhd->pkhd", dscores, queries, preferred_element_type=F32) * factor
    dvalues = jnp.einsum("phqk,pqhd->pkhd", probs.astype(BF16), upstream, preferred_element_type=F32)
    return tuple(t.astype(BF16).reshape(-1, t.shape[2] * t.shape[3]) for t in (dqueries, dkeys, dvalues))


def unit_back(raw, inv_norm, upstream):
    cubed = inv_norm * inv_norm * inv_norm
    return inv_norm * upstream - raw * cubed * jnp.sum(raw * upstream, -1, keepdims=True)


def contrast(text_pool, image_pool, text_embed32, image_embed32):
    text_raw = jnp.dot(text_pool, text_embed32, precision=HIGHEST)
    text_inv = lax.rsqrt(jnp.sum(text_raw * text_raw, -1, keepdims=True) + EPS)
    image_raw = jnp.dot(image_pool, image_embed32, precision=HIGHEST)
    image_inv = lax.rsqrt(jnp.sum(image_raw * image_raw, -1, keepdims=True) + EPS)
    both = jnp.concatenate([(text_raw * text_inv).astype(BF16), (image_raw * image_inv).astype(BF16)], 1)
    width = text_raw.shape[1]
    everyone = lax.all_gather(both, ("dp", "mp"), axis=0, tiled=True)
    text_all, image_all = everyone[:, :width], everyone[:, width:]
    logits = contract_cols(text_all, image_all) * TEMP_INVERSE
    weights = jnp.exp(logits - jax.nn.logsumexp(logits, axis=1, keepdims=True)) + jnp.exp(
        logits - jax.nn.logsumexp(logits, axis=0, keepdims=True)
    )
    weights = weights - 2.0 * jnp.eye(logits.shape[0], dtype=F32)
    count = text_pool.shape[0]
    start = (lax.axis_index("dp") * 2 + lax.axis_index("mp")) * count
    rows = lax.dynamic_slice_in_dim(weights, start, count, 0)
    columns = lax.dynamic_slice_in_dim(weights, start, count, 1)
    dtext = GRAD_SCALE * jnp.dot(rows, image_all.astype(F32), precision=HIGHEST)
    dimage = GRAD_SCALE * jnp.dot(columns.T, text_all.astype(F32), precision=HIGHEST)
    dtext_raw = unit_back(text_raw, text_inv, dtext)
    dimage_raw = unit_back(image_raw, image_inv, dimage)
    return (
        jnp.dot(text_pool.T, dtext_raw, precision=HIGHEST),
        jnp.dot(image_pool.T, dimage_raw, precision=HIGHEST),
        jnp.dot(dtext_raw, text_embed32.T, precision=HIGHEST),
        jnp.dot(dimage_raw, image_embed32.T, precision=HIGHEST),
    )


FACTOR = 1.0 / math.sqrt(HEAD_DIM)
LOWEST = -1e30
TEXT_PAD = 64
PATCH_PAD = 160
PEER_RING = 3
ARRIVE_RING = 11


def nn(a, b):
    return lax.dot_general(a, b, (((1,), (0,)), ((), ())), preferred_element_type=F32)


def nt(a, b):
    return lax.dot_general(a, b, (((1,), (1,)), ((), ())), preferred_element_type=F32)


def tn(a, b):
    return lax.dot_general(a, b, (((0,), (0,)), ((), ())), preferred_element_type=F32)


def exact(a, b, dims):
    return lax.dot_general(a, b, (dims, ((), ())), precision=HIGHEST, preferred_element_type=F32)


def terms(x):
    high = x.astype(BF16)
    return high, (x - high.astype(F32)).astype(BF16)


def near(a, b, dims):
    def dot(x, y):
        return lax.dot_general(x, y, (dims, ((), ())), preferred_element_type=F32)

    (a_high, a_low), (b_high, b_low) = terms(a), terms(b)
    return dot(a_high, b_high) + (dot(a_high, b_low) + dot(a_low, b_high))


class Blocks:
    def __init__(self):
        self.free, self.top = [], 0

    def take(self, count):
        spare = sorted(self.free)
        for at in spare:
            if all(at + k in spare for k in range(count)):
                for k in range(count):
                    self.free.remove(at + k)
                return at
        at, self.top = self.top, self.top + count
        return at

    def give(self, at, count):
        self.free += range(at, at + count)


def lane_masks(width, split):
    lane = lax.broadcasted_iota(jnp.int32, (1, width), 1)
    left = (lane < split).astype(F32)
    return left, 1.0 - left


def head_pair(x):
    left, right = lane_masks(128, 64)
    return jnp.concatenate([x * left.astype(BF16), x * right.astype(BF16)], 0)


def one_head_each(x):
    half = x.shape[0] // 2
    left = lax.broadcasted_iota(jnp.int32, (half, 128), 1) < 64
    return jnp.where(left, x[:half], x[half:])


def softmax_pair(scores, keys, real):
    lane = lax.broadcasted_iota(jnp.int32, scores.shape, 1)
    left = lane < keys
    within = jnp.where(left, lane, lane - keys)
    scores = jnp.where(within < real, scores * FACTOR, LOWEST)
    top0 = jnp.max(jnp.where(left, scores, LOWEST), 1, keepdims=True)
    top1 = jnp.max(jnp.where(left, LOWEST, scores), 1, keepdims=True)
    expd = jnp.exp(scores - jnp.where(left, top0, top1))
    sum0 = jnp.sum(jnp.where(left, expd, 0.0), 1, keepdims=True)
    sum1 = jnp.sum(jnp.where(left, 0.0, expd), 1, keepdims=True)
    return (expd * jnp.where(left, 1.0 / sum0, 1.0 / sum1)).astype(BF16)


def softmax_pair_back(probs, dprobs, keys):
    left = lax.broadcasted_iota(jnp.int32, dprobs.shape, 1) < keys
    probs = probs.astype(F32)
    both = probs * dprobs
    sum0 = jnp.sum(jnp.where(left, both, 0.0), 1, keepdims=True)
    sum1 = jnp.sum(jnp.where(left, 0.0, both), 1, keepdims=True)
    return (both - probs * jnp.where(left, sum0, sum1)).astype(BF16)


def norm_rows(x):
    centred = x - jnp.mean(x, -1, keepdims=True)
    inv_std = lax.rsqrt(jnp.mean(centred * centred, -1, keepdims=True) + EPS)
    return centred * inv_std, inv_std


class Layer:
    def __init__(self, dims, sizes, refs):
        self.dims, self.sizes = dims, sizes
        self.__dict__.update(refs)
        self.place = Place(dims)
        self.blocks, self.wide = Blocks(), Blocks()
        self.rows = sizes.pairs * TEXT_PAD
        self.patch_rows = sizes.pairs * PATCH_PAD
        self.half = sizes.half
        self.da = None


    def weight(self, slot, h):
        w = self.w[slot][h]
        return w.reshape(-1, w.shape[-1])

    def put_grad(self, slot, h, f, value):
        cut = self.dims[0] // 2
        shape = self.w[slot].shape[2:]
        self.w[slot][h, f * cut : (f + 1) * cut] = value.astype(BF16).reshape(cut, *shape)

    def project(self, at, slot, h):
        w = self.weight(slot, h)
        return nn(self.t[at], w[: self.half]) + nn(self.t[at + 1], w[self.half :])

    def two(self, fn):
        for h in range(2):
            fn(h)

    def text_loop(self, fn):
        def step(p, carry):
            fn(p, pl.ds(pl.multiple_of(p * TEXT_PAD, TEXT_PAD), TEXT_PAD))
            return carry

        lax.fori_loop(0, self.sizes.pairs, step, 0)

    def read_rows(self, at, rows):
        return jnp.concatenate([self.t[at, rows, :], self.t[at + 1, rows, :]], 1)

    def write_rows(self, at, rows, value):
        self.t[at, rows, :] = value[:, : self.half].astype(BF16)
        self.t[at + 1, rows, :] = value[:, self.half :].astype(BF16)


    def own_pairs(self, ref, sem):
        return pltpu.make_async_copy(
            ref.at[pl.ds(self.place.mp * self.sizes.pairs, self.sizes.pairs)], self.joined, sem
        )

    def load(self):
        self.x, self.cot = self.blocks.take(2), self.blocks.take(2)
        pltpu.make_async_copy(self.patches_in, self.patches, self.load_sem.at[0]).start()
        self.own_pairs(self.text_in, self.load_sem.at[1]).start()

    def unpack(self, at):
        gap = jnp.zeros((TEXT_PAD - self.sizes.length, 2 * self.half), F32)
        for p in range(self.sizes.pairs):
            value = jnp.concatenate([self.joined[p].astype(F32), gap], 0)
            self.write_rows(at, pl.ds(p * TEXT_PAD, TEXT_PAD), value)

    def take_text(self):
        self.own_pairs(self.text_in, self.load_sem.at[1]).wait()
        self.unpack(self.x)
        self.own_pairs(self.cot_in, self.load_sem.at[2]).start()

    def take_patches(self):
        pltpu.make_async_copy(self.patches_in, self.patches, self.load_sem.at[0]).wait()

    def take_cotangent(self):
        self.own_pairs(self.cot_in, self.load_sem.at[2]).wait()
        self.unpack(self.cot)

    def own_copies(self, c, name):
        dst = self.w[name].at[(self.place.mp,) + self.place.pos]
        blocks, width = self.sizes.hidden_blocks, self.sizes.embed_half

        def copy(src, dst, sem):
            return pltpu.make_async_copy(src, dst, self.own_sem.at[sem])

        if name == IMAGE:
            return [copy(self.shards[name].at[:, pl.ds(self.place.mp * self.half, self.half)], dst, c)]
        if name == SMALL:
            cols = pl.ds(self.place.mp * width, width)
            refs = self.text_embed, self.image_embed
            spare = FFN + 2 * blocks
            return [
                copy(ref.at[:, cols], dst.at[:, pl.ds(k * width, width)], c if k == 0 else spare)
                for k, ref in enumerate(refs)
            ]
        if name >= FFN:
            ref = self.ffn_in_all if name < FFN + blocks else self.ffn_out_all
            return [copy(ref.at[:, pl.ds((name - FFN) % blocks * self.half, self.half)], dst, c)]
        return [copy(self.shards[name], dst, c)]

    def place_norms(self):
        rows = self.norm_rows_in[...]
        width = 2 * self.sizes.embed_half
        lane = lax.broadcasted_iota(jnp.int32, (rows.shape[0], self.half - width), 1)
        unit = (lane == lax.broadcasted_iota(jnp.int32, lane.shape, 0)).astype(F32).astype(BF16)
        ref = self.w[SMALL].at[(self.place.mp,) + self.place.pos]
        ref[:, width:] = tn(rows, unit).astype(BF16)

    def image_features(self):
        self.im = self.wide.take(2)
        block = self.patch_rows // 3

        def step(i, carry):
            rows = pl.ds(pl.multiple_of(i * block, block), block)
            left = self.patches[rows, :]
            for h in range(2):
                self.u[self.im + h, rows, :] = nn(left, self.weight(IMAGE, h)).astype(BF16)
            return carry

        lax.fori_loop(0, 3, step, 0)

    def self_projections(self):
        self.q = self.blocks.take(6)
        for k, slot in enumerate((QUERY, KEY, VALUE)):
            self.two(lambda h: self.t.__setitem__(self.q + 2 * k + h, self.project(self.x, slot, h).astype(BF16)))

    def couples(self):
        return [(h, slice(128 * j, 128 * j + 128)) for h in range(2) for j in range(self.half // 128)]

    def put_couples(self, ref, at, rows, values):
        each = len(values) // 2
        for h in range(2):
            ref[at + h, rows, :] = jnp.concatenate(values[h * each : (h + 1) * each], 1)

    def attention(self, p, rows, queries, keys, values, saved, key_pad, real, out):
        scores = jnp.concatenate([nt(q, head_pair(k)) for q, k in zip(queries, keys)], 0)
        probs = softmax_pair(scores, key_pad, real)
        saved[p] = probs
        mixed = [
            nn(probs[TEXT_PAD * i : TEXT_PAD * (i + 1)], head_pair(v)).astype(BF16) for i, v in enumerate(values)
        ]
        self.put_couples(self.t, out, rows, mixed)

    def attention_back(self, p, queries, keys, values, upstream, saved, key_pad):
        probs = saved[p]
        dprobs = jnp.concatenate([nt(d, head_pair(v)) for d, v in zip(upstream, values)], 0)
        dscores = softmax_pair_back(probs, dprobs, key_pad)
        part = [slice(TEXT_PAD * i, TEXT_PAD * (i + 1)) for i in range(len(queries))]
        dqueries = [(nn(dscores[r], head_pair(k)) * FACTOR).astype(BF16) for r, k in zip(part, keys)]
        dkeys = [(one_head_each(tn(dscores[r], q)) * FACTOR).astype(BF16) for r, q in zip(part, queries)]
        dvalues = [one_head_each(tn(probs[r], d)).astype(BF16) for r, d in zip(part, upstream)]
        return dqueries, dkeys, dvalues

    def self_attention(self):
        self.a1 = self.blocks.take(2)

        def pair(p, rows):
            q, k, v = ([self.t[self.q + 2 * m + h, rows, lanes] for h, lanes in self.couples()] for m in range(3))
            self.attention(p, rows, q, k, v, self.p1, TEXT_PAD, self.sizes.length, self.a1)

        self.text_loop(pair)

    def norm_params(self):
        cols = self.weight(SMALL, 0)[:, 2 * self.sizes.embed_half :].astype(F32)
        self.norms[...] = jnp.transpose(cols)[: self.norms.shape[0]]

    def after_branch(self, at, slot, k):
        self.z[...] = nt(self.t[at], self.weight(slot, 0)) + nt(self.t[at + 1], self.weight(slot, 1))
        normed_at, low_at = self.blocks.take(2), self.blocks.take(2)

        def rows_step(p, rows):
            residual = self.read_rows(self.x, rows).astype(F32) if k == 0 else self.hid[rows, :]
            normed, inv_std = norm_rows(residual + self.z[rows, :])
            hidden = normed * self.norms[2 * k : 2 * k + 1, :] + self.norms[2 * k + 1 : 2 * k + 2, :]
            self.hid[rows, :] = hidden
            self.inv[k, rows, :] = inv_std
            self.write_rows(normed_at, rows, normed)
            self.write_rows(low_at, rows, hidden)

        self.text_loop(rows_step)
        return normed_at, low_at

    def turned(self, at):
        out = self.blocks.take(2)
        for h in range(2):
            self.t[out + h] = jnp.transpose(self.t[at + h])
        return out

    def after_self(self):
        self.n1, low = self.after_branch(self.a1, ATTN_OUT, 0)
        self.low1, self.low1_t = low, self.turned(low)

    def cross_keys(self, slot):
        at = self.wide.take(2)
        block = self.patch_rows // 3

        def step(i, carry):
            rows = pl.ds(pl.multiple_of(i * block, block), block)
            for h in range(2):
                w = self.weight(slot, h)
                self.u[at + h, rows, :] = (
                    nn(self.u[self.im, rows, :], w[: self.half]) + nn(self.u[self.im + 1, rows, :], w[self.half :])
                ).astype(BF16)
            return carry

        lax.fori_loop(0, 3, step, 0)
        return at

    def make_keys(self):
        self.k2 = self.cross_keys(CROSS_KEY)

    def make_values(self):
        self.v2 = self.cross_keys(CROSS_VALUE)

    def cross_query(self):
        self.q2 = self.blocks.take(2)
        self.two(lambda h: self.t.__setitem__(self.q2 + h, self.project(self.low1, CROSS_QUERY, h).astype(BF16)))
        self.blocks.give(self.low1, 2)

    def patch_rows_of(self, p):
        return pl.ds(pl.multiple_of(p * PATCH_PAD, PATCH_PAD), PATCH_PAD)

    def cross_attention(self):
        self.a2 = self.blocks.take(2)

        def pair(p, rows):
            keys = self.patch_rows_of(p)
            q = [self.t[self.q2 + h, rows, lanes] for h, lanes in self.couples()]
            k, v = ([self.u[at + h, keys, lanes] for h, lanes in self.couples()] for at in (self.k2, self.v2))
            self.attention(p, rows, q, k, v, self.p2, PATCH_PAD, self.sizes.patch_count, self.a2)

        self.text_loop(pair)

    def after_cross(self):
        self.n2, low = self.after_branch(self.a2, CROSS_OUT, 1)
        self.low2, self.low2_t = low, self.turned(low)
        self.g, self.dg = self.blocks.take(2 * self.sizes.hidden_blocks), self.blocks.take(2 * self.sizes.hidden_blocks)

    def ffn_in(self, k):
        def half(h, carry):
            inner = self.project(self.low2, FFN + k, h)
            cdf = 0.5 * (1.0 + lax.erf(inner * math.sqrt(0.5)))
            pdf = jnp.exp(-0.5 * inner * inner) * (1.0 / math.sqrt(2.0 * math.pi))
            self.t[self.g + 2 * k + h] = (inner * cdf).astype(BF16)
            self.t[self.dg + 2 * k + h] = (cdf + inner * pdf).astype(BF16)
            return carry

        lax.fori_loop(0, 2, half, 0)
        if k == self.sizes.hidden_blocks - 1:
            self.blocks.give(self.low2, 2)

    def ffn_out(self, k):
        def half(h, carry):
            self.hid[...] += nt(self.t[self.g + 2 * k + h], self.weight(FFN + self.sizes.hidden_blocks + k, h))
            return carry

        lax.fori_loop(0, 2, half, 0)


    def pools(self):
        pairs, length, patch_count = self.sizes.pairs, self.sizes.length, self.sizes.patch_count
        self.pool[...] = jnp.zeros_like(self.pool)
        for p in range(pairs):
            rows = pl.ds(p * TEXT_PAD, TEXT_PAD)
            self.pool[0, p : p + 1, :] = jnp.sum(self.read_rows(self.x, rows).astype(F32), 0, keepdims=True) * (1.0 / length)
            keys = pl.ds(p * PATCH_PAD, PATCH_PAD)
            for h in range(2):
                self.pool[1, p : p + 1, h * self.half : (h + 1) * self.half] = jnp.sum(
                    self.u[self.im + h, keys, :].astype(F32), 0, keepdims=True
                ) * (1.0 / patch_count)

    def embed_weight(self, which, h):
        width = self.sizes.embed_half
        return self.weight(SMALL, h)[:, which * width : (which + 1) * width].astype(F32)

    def embed(self):
        width = self.sizes.embed_half
        for which in range(2):
            for h in range(2):
                self.raw[which, :, h * width : (h + 1) * width] = exact(
                    self.pool[which], self.embed_weight(which, h), ((1,), (0,))
                )
            raw = self.raw[which]
            inv = lax.rsqrt(jnp.sum(raw * raw, -1, keepdims=True) + EPS)
            self.own_emb[:, which * 2 * width : (which + 1) * 2 * width] = (raw * inv).astype(BF16)

    def contrast(self):
        width, pairs = self.sizes.embed_half, self.sizes.pairs
        everyone = self.emb[...].reshape(-1, 4 * width)
        count = everyone.shape[0]
        both = everyone[:, : 2 * width], everyone[:, 2 * width :]
        own = self.own_emb[...][:, : 2 * width], self.own_emb[...][:, 2 * width :]
        spot = self.place.pos
        me = self.place.mp * (count // 2) + ((spot[0] * self.dims[1] + spot[1]) * self.dims[2] + spot[2]) * 16
        real_row = (lax.broadcasted_iota(jnp.int32, (1, count), 1) % 16 < pairs).astype(F32)
        real_col = (lax.broadcasted_iota(jnp.int32, (count, 1), 0) % 16 < pairs).astype(F32)
        own_row = (lax.broadcasted_iota(jnp.int32, (16, 1), 0) < pairs).astype(F32)
        match = (
            lax.broadcasted_iota(jnp.int32, (16, count), 1) == lax.broadcasted_iota(jnp.int32, (16, count), 0) + me
        ).astype(F32)
        for which in range(2):
            mine, others = own[which], both[1 - which]
            column_sum = jnp.zeros((1, count), F32)
            for at in range(0, count, 128):
                cross = nt(both[which][at : at + 128], others) * TEMP_INVERSE - TEMP_INVERSE
                column_sum = column_sum + jnp.sum(jnp.exp(cross) * real_col[at : at + 128], 0, keepdims=True)
            logits = nt(mine, others) * TEMP_INVERSE - TEMP_INVERSE
            expd = jnp.exp(logits) * (real_row * own_row)
            row_sum = jnp.sum(expd, 1, keepdims=True) + (1.0 - own_row)
            pull = expd * (1.0 / row_sum) + expd * (1.0 / column_sum) - 2.0 * match * own_row
            upstream = GRAD_SCALE * exact(pull, others.astype(F32), ((1,), (0,)))
            raw = self.raw[which]
            inv = lax.rsqrt(jnp.sum(raw * raw, -1, keepdims=True) + EPS)
            draw = unit_back(raw, inv, upstream)
            scale = 1.0 / (self.sizes.length if which == 0 else self.sizes.patch_count)
            extra = exact(draw[:, :width], self.embed_weight(which, 0), ((1,), (1,))) + exact(
                draw[:, width:], self.embed_weight(which, 1), ((1,), (1,))
            )
            self.extra[which] = extra * scale
            for h in range(2):
                value = exact(self.pool[which], draw[:, h * width : (h + 1) * width], ((0,), (0,)))
                self.put_small(h, which * width, value)


    def region(self):
        pairs, length, patch_count = self.sizes.pairs, self.sizes.length, self.sizes.patch_count
        boxes, listed = self.picks.shape[1:]
        self.chosen[...] = jnp.zeros_like(self.chosen)
        self.span[...] = jnp.zeros_like(self.span)
        for p in range(pairs):
            me = self.place.mp * pairs + p

            def column(ref):
                lane = lax.broadcasted_iota(jnp.int32, ref.shape, 1)
                return jnp.sum(jnp.where(lane == me, ref[...].astype(F32), 0.0), 1, keepdims=True)

            counts, starts, lengths = column(self.counts), column(self.starts), column(self.lengths)
            picks = self.picks[me]
            spot = lax.broadcasted_iota(jnp.int32, (boxes, PATCH_PAD), 1)
            listing = jnp.zeros((boxes, PATCH_PAD), F32)
            for k in range(listed):
                listing = listing + (picks[:, k : k + 1] == spot).astype(F32)
            valid = lax.broadcasted_iota(jnp.int32, (boxes, 1), 0).astype(F32) < counts
            self.chosen[p, :boxes, :] = jnp.where(valid, listing * (1.0 / listed), 0.0)
            token = lax.broadcasted_iota(jnp.int32, (boxes, TEXT_PAD), 1).astype(F32)
            inside = (token >= starts) & (token < starts + lengths) & valid
            self.span[p, :boxes, :] = jnp.where(inside, 1.0 / lengths, 0.0)
            keys = pl.ds(p * PATCH_PAD, PATCH_PAD)
            for h in range(2):
                self.regions[p, :, h * self.half : (h + 1) * self.half] = nn(
                    self.chosen[p].astype(BF16), self.u[self.im + h, keys, :]
                )


    def norm_back(self, k, upstream, normed, inv_std, rows):
        scaled = upstream * self.norms[2 * k : 2 * k + 1, :]
        inner = jnp.mean(scaled * normed, -1, keepdims=True)
        self.norm_grad[2 * k : 2 * k + 1, :] += jnp.sum(upstream * normed, 0, keepdims=True)
        self.norm_grad[2 * k + 1 : 2 * k + 2, :] += jnp.sum(upstream, 0, keepdims=True)
        result = inv_std * (scaled - jnp.mean(scaled, -1, keepdims=True) - normed * inner)
        self.z[rows, :] = result
        self.write_rows(self.db, rows, result)

    def output_and_back(self):
        self.db = self.blocks.take(2)
        self.norm_grad[...] = jnp.zeros_like(self.norm_grad)

        def pair(p, rows):
            normed, inv_std = norm_rows(self.hid[rows, :])
            output = normed * self.norms[4:5, :] + self.norms[5:6, :]
            self.joined[p] = output[: self.sizes.length].astype(BF16)
            mismatch = near(self.span[p], output, ((1,), (0,))) - self.regions[p]
            self.regions[p] = mismatch
            upstream = self.read_rows(self.cot, rows).astype(F32) + near(self.span[p], mismatch, ((0,), (0,)))
            self.norm_back(2, upstream, normed, inv_std, rows)

        self.text_loop(pair)
        self.blocks.give(self.cot, 2)
        self.db_t = self.turned(self.db)

    def grads(self, slot, h, left_t, right):
        for f in range(2):
            self.put_grad(slot, h, f, nn(self.t[left_t + f], right))

    def ffn_out_back(self, k):
        slot = FFN + self.sizes.hidden_blocks + k

        def half(h, carry):
            at = 2 * k + h
            dactive = self.project(self.db, slot, h)
            self.t[self.dg + at] = (dactive * self.t[self.dg + at].astype(F32)).astype(BF16)
            self.grads(slot, h, self.db_t, self.t[self.g + at])
            return carry

        lax.fori_loop(0, 2, half, 0)
        self.blocks.give(self.g + 2 * k, 2)

    def ffn_in_back(self, k):
        slot = FFN + k

        def half(h, carry):
            dinner = self.t[self.dg + 2 * k + h]
            self.z[...] += nt(dinner, self.weight(slot, h))
            self.grads(slot, h, self.low2_t, dinner)
            return carry

        lax.fori_loop(0, 2, half, 0)

    def back_through_norm(self, k):
        normed_at = (self.n1, self.n2)[k]

        def step(p, rows):
            self.norm_back(k, self.z[rows, :], self.read_rows(normed_at, rows).astype(F32), self.inv[k, rows, :], rows)

        self.text_loop(step)
        for h in range(2):
            self.t[self.db_t + h] = jnp.transpose(self.t[self.db + h])

    def branch_back(self, slot, at):
        if self.da is None:
            self.da = self.blocks.take(2)

        def half(h, carry):
            self.t[self.da + h] = self.project(self.db, slot, h).astype(BF16)
            self.grads(slot, h, self.db_t, self.t[at + h])
            return carry

        lax.fori_loop(0, 2, half, 0)

    def cross_attention_back(self):
        def pair(p, rows):
            keys = self.patch_rows_of(p)
            q, d = ([self.t[at + h, rows, lanes] for h, lanes in self.couples()] for at in (self.q2, self.da))
            k, v = ([self.u[at + h, keys, lanes] for h, lanes in self.couples()] for at in (self.k2, self.v2))
            dq, dk, dv = self.attention_back(p, q, k, v, d, self.p2, PATCH_PAD)
            self.put_couples(self.t, self.q2, rows, dq)
            self.put_couples(self.u, self.k2, keys, dk)
            self.put_couples(self.u, self.v2, keys, dv)

        self.text_loop(pair)

    def cross_query_back(self):
        def half(h, carry):
            dq = self.t[self.q2 + h]
            self.z[...] += nt(dq, self.weight(CROSS_QUERY, h))
            self.grads(CROSS_QUERY, h, self.low1_t, dq)
            return carry

        lax.fori_loop(0, 2, half, 0)

    def image_back(self):
        self.dim = self.wide.take(2)
        block = 2 * PATCH_PAD

        def step(i, carry):
            rows = pl.ds(pl.multiple_of(i * block, block), block)
            parts = [self.u[at + h, rows, :] for at in (self.k2, self.v2) for h in range(2)]
            for half in range(2):
                cols = slice(half * self.half, (half + 1) * self.half)
                weights = [self.weight(slot, h)[cols] for slot in (CROSS_KEY, CROSS_VALUE) for h in range(2)]
                total = sum(nt(part, weight) for part, weight in zip(parts, weights))
                for k in range(2):
                    p = 2 * i + k
                    value = total[k * PATCH_PAD : (k + 1) * PATCH_PAD]
                    value = value - sum(tn(self.chosen[p].astype(BF16), m) for m in terms(self.regions[p, :, cols]))
                    value = value + self.extra[1, pl.ds(p, 1), cols]
                    self.u[self.dim + half, self.patch_rows_of(p), :] = value.astype(BF16)
            return carry

        lax.fori_loop(0, self.sizes.pairs // 2, step, 0)

    def cross_key_back(self, slot, at):
        for f in range(2):

            def half(h, carry):
                self.put_grad(slot, h, f, tn(self.u[self.im + f], self.u[at + h]))
                return carry

            lax.fori_loop(0, 2, half, 0)

    def patch_back(self):
        pairs, patch_count = self.sizes.pairs, self.sizes.patch_count

        def out(p):
            return pltpu.make_async_copy(self.patch_stage.at[p % 2], self.patch_grad.at[p], self.patch_sem.at[p % 2])

        for p in range(pairs):
            if p >= 2:
                out(p - 2).wait()
            keys = pl.ds(p * PATCH_PAD, PATCH_PAD)
            value = nt(self.u[self.dim, keys, :], self.weight(IMAGE, 0)) + nt(
                self.u[self.dim + 1, keys, :], self.weight(IMAGE, 1)
            )
            self.patch_stage[p % 2] = value[:patch_count]
            out(p).start()
        for p in range(max(pairs - 2, 0), pairs):
            out(p).wait()

    def image_weight_back(self):
        cut = self.dims[0] // 2
        shape = self.w[IMAGE].shape[2:]
        half_depth = self.patches.shape[1] // 2
        for f in range(2):

            def half(h, carry):
                value = tn(self.patches[:, f * half_depth : (f + 1) * half_depth], self.u[self.dim + h])
                self.w[IMAGE][h, f * cut : (f + 1) * cut] = value.astype(BF16).reshape(cut, *shape)
                return carry

            lax.fori_loop(0, 2, half, 0)

    def put_small(self, h, start, value):
        ref = self.w[SMALL]
        ref[h, :, :, :, :, start : start + value.shape[1]] = value.astype(BF16).reshape(
            *ref.shape[1:-1], value.shape[1]
        )

    def small_grads(self):
        rows = jnp.concatenate([self.norm_grad[...], jnp.zeros((128 - self.norm_grad.shape[0], 2 * self.half), F32)], 0)
        columns = jnp.transpose(rows)
        for h in range(2):
            self.put_small(h, 2 * self.sizes.embed_half, columns)

    def self_attention_back(self):
        def pair(p, rows):
            q, k, v = ([self.t[self.q + 2 * m + h, rows, lanes] for h, lanes in self.couples()] for m in range(3))
            d = [self.t[self.da + h, rows, lanes] for h, lanes in self.couples()]
            for m, values in enumerate(self.attention_back(p, q, k, v, d, self.p1, TEXT_PAD)):
                self.put_couples(self.t, self.q + 2 * m, rows, values)

        self.text_loop(pair)
        for h in range(2):
            self.t[self.db_t + h] = jnp.transpose(self.t[self.x + h])

    def self_projection_back(self, k):
        slot = (QUERY, KEY, VALUE)[k]

        def half(h, carry):
            d = self.t[self.q + 2 * k + h]
            self.z[...] += nt(d, self.weight(slot, h))
            self.grads(slot, h, self.db_t, d)
            return carry

        lax.fori_loop(0, 2, half, 0)

    def text_out(self):
        def moves(p):
            src, dst = self.text_stage.at[p % 2], self.text_out_ref.at[self.place.mp, p]
            own = pltpu.make_async_copy(src, dst, self.text_own.at[p])
            return own, remote(src, dst, self.text_send.at[p], self.text_recv.at[p], self.place.peer())

        def done(p):
            own, give = moves(p)
            own.wait()
            give.wait_send()

        pairs = self.sizes.pairs
        for p in range(pairs):
            if p >= 2:
                done(p - 2)
            rows = pl.ds(p * TEXT_PAD, TEXT_PAD)
            value = self.z[rows, :] + self.extra[0, p : p + 1, :]
            self.text_stage[p % 2] = value[: self.sizes.length]
            for move in moves(p):
                move.start()

        def end():
            for p in range(max(pairs - 2, 0), pairs):
                done(p)
            for p in range(pairs):
                moves(p)[1].wait_recv()

        self.ends.append(end)


    def gather_to_peer(self, c, name, order, buf):
        mine, other = buf.at[self.place.mp], buf.at[1 - self.place.mp]
        sent = yield from gather_steps(self.place, order, mine, self.g_send.at[c], self.g_recv.at[c])

        def copy(ref):
            return remote(ref, ref, self.gp_send.at[c], self.gp_recv.at[c], self.place.peer())

        copy(mine).start()
        yield
        copy(other).wait_recv()
        self.sending[name] = sent + [(None, lambda: copy(mine))]

    def gather(self, c, name, order):
        buf = self.w[name]
        for copy in self.own_copies(c, name):
            copy.start()
        if name == SMALL:
            self.place_norms()
        yield
        for copy in self.own_copies(c, name):
            copy.wait()
        yield from self.gather_to_peer(c, name, order, buf)

    def gather_embeddings(self, c, order):
        self.emb[(self.place.mp,) + self.place.pos] = self.own_emb[...]
        yield from self.gather_to_peer(c, EMBEDDINGS, order, self.emb)

    def settle(self, names):
        for name in names:
            wait_sent(self.sending.pop(name))

    def credit(self, slot, give):
        place = self.place

        def act(index, device):
            sem = self.credits.at[slot, index]
            if give:
                pl.semaphore_signal(sem, inc=1, device_id=device, device_id_type=MESH)
            else:
                pl.semaphore_wait(sem, 1)

        for axis in range(3):
            length, pos = place.dims[axis], place.pos[axis]
            if length > 1:
                pl.when(pos > 0)(lambda: act(2 * axis + (1 if give else 0), place.at(axis, pos - 1)))
                pl.when(pos < length - 1)(lambda: act(2 * axis + (0 if give else 1), place.at(axis, pos + 1)))

    def peer_credit(self, slot, give):
        sem = self.peer_credits.at[slot]
        if give:
            pl.semaphore_signal(sem, inc=1, device_id=self.place.peer(), device_id_type=MESH)
        else:
            pl.semaphore_wait(sem, 1)

    def image_credit(self):
        self.credit(ARRIVE_RING, True)
        self.peer_credit(PEER_RING, True)

    def spare(self, at, units, rows):
        blocks = self.u.at[pl.ds(at, 2)].reshape(-1, rows, self.half)
        return blocks.at[pl.ds(0, units)]

    def scatter(self, c, turn, name, order, total):
        buf, ringed = self.w[name], name != IMAGE
        mine, other = buf.at[self.place.mp], buf.at[1 - self.place.mp]
        if ringed:
            peer_slot, slot = turn % PEER_RING, turn % ARRIVE_RING
            peer_in, arrive = self.peer_in.at[peer_slot], self.arrive.at[slot]
        else:
            peer_slot, slot = PEER_RING, ARRIVE_RING
            peer_in = self.spare(0, math.prod(self.dims), buf.shape[-2]).reshape(*buf.shape[1:])
            arrive = self.spare(2, arrive_units(self.dims, order), buf.shape[-2])

        def copy():
            return remote(other, peer_in, self.sp_send.at[peer_slot], self.sp_recv.at[peer_slot], self.place.peer())

        if not ringed or turn >= PEER_RING:
            self.peer_credit(peer_slot, False)
        wait_sent(self.peer_sent.pop(peer_slot, ()))
        copy().start()
        self.peer_sent[peer_slot] = [(None, copy)]
        yield
        copy().wait_recv()
        mine[...] = mine[...] + peer_in[...]
        if ringed and turn + PEER_RING < total:
            self.peer_credit(peer_slot, True)
        if not ringed or turn >= ARRIVE_RING:
            self.credit(slot, False)
        wait_sent(self.ring_sent.pop(slot, ()))
        result = self.results[name]
        target = result.at[self.place.mp] if len(result.shape) == 3 else result
        sent = yield from scatter_steps(
            self.place, order, mine, arrive, self.s_send.at[slot], self.s_recv.at[slot], target
        )
        if ringed and turn + ARRIVE_RING < total:
            self.credit(slot, True)
        self.ring_sent[slot] = sent
        if len(result.shape) == 3:

            def hand(half):
                ref = result.at[half]
                return remote(ref, ref, self.h_send.at[int(name == IMAGE)], self.h_recv.at[int(name == IMAGE)], self.place.peer())

            hand(self.place.mp).start()
            yield
            hand(1 - self.place.mp).wait_recv()
            self.sent.append((None, lambda: hand(self.place.mp)))

    def joined_over(self):
        stage, whole = self.joined, self.joined_out
        own = pltpu.make_async_copy(stage, whole.at[self.place.mp], self.out_own)
        give = remote(stage, whole.at[self.place.mp], self.out_send, self.out_recv, self.place.peer())
        own.start()
        give.start()
        self.ends += [own.wait, give.wait]


IMAGE, QUERY, KEY, VALUE, SMALL, ATTN_OUT, CROSS_KEY, CROSS_VALUE, CROSS_QUERY, CROSS_OUT, FFN = range(11)
EMBEDDINGS = -1


def grad_order(hidden_blocks):
    ffn = (*range(FFN + hidden_blocks, FFN + 2 * hidden_blocks), *range(FFN, FFN + hidden_blocks))
    return ffn + (CROSS_OUT, CROSS_QUERY, CROSS_KEY, CROSS_VALUE, IMAGE, ATTN_OUT, SMALL, QUERY, KEY, VALUE)


class Timeline:
    def __init__(self):
        self.events = []

    def add(self, time, fn):
        self.events.append((time, len(self.events), fn))

    def add_steps(self, times, steps):
        last = [False]

        def advance():
            if not last[0]:
                try:
                    next(steps)
                except StopIteration:
                    last[0] = True

        for time in times:
            self.add(time, advance)

    def run(self):
        for _, _, fn in sorted(self.events, key=lambda e: e[:2]):
            fn()


CHUNK = 3.9
KINDS = ((2, 0, 1), (1, 0, 2), (0, 2, 1), (0, 1, 2))

GATHER_KINDS = (2, 1, 2, 1, 3, 2, 1, 0, 0, 3, 2, 1, 0, 1, 2, 3, 0, 1)
GATHER_START = (0.0, 35.78, 9.14, 7.29, 8.49, 34.08, 32.19, 18.67, 13.4, 23.56, 64.34, 62.53, 73.03, 62.92, 87.05, 47.64, 73.57, 73.11)
GATHER_STEPS = (
    (0.0, 9.86, 19.46, 20.54, 44.84, 69.22, 77.55),
    (0.0, 9.5, 18.16, 25.51, 36.27, 56.29, 63.23),
    (0.0, 4.91, 13.38, 28.77, 37.2, 65.33, 87.19),
    (0.0, 20.6, 34.85, 38.31, 50.92, 77.49, 86.82),
    (0.0, 2.0, 14.0, 20.51, 31.8, 45.01, 50.55),
    (0.0, 10.96, 15.65, 18.67, 37.8, 45.42, 88.59),
    (0.0, 36.34, 39.98, 42.92, 45.73, 67.89, 69.96),
    (0.0, 12.35, 52.03, 62.19, 68.96, 91.36, 91.73),
    (0.0, 48.13, 60.52, 77.82, 83.43, 113.81, 119.75),
    (0.0, 26.68, 32.47, 48.62, 62.07, 91.48, 127.96),
    (0.0, 12.23, 15.22, 26.74, 57.19, 75.56, 109.53),
    (0.0, 20.34, 32.76, 43.48, 47.67, 108.99, 138.63),
    (0.0, 20.85, 35.36, 60.72, 72.87, 115.45, 141.33),
    (0.0, 26.1, 44.43, 60.04, 73.87, 147.49, 156.02),
    (0.0, 9.02, 14.88, 21.06, 39.31, 105.07, 131.21),
    (0.0, 6.63, 26.12, 35.19, 66.26, 164.18, 194.81),
    (0.0, 37.17, 73.98, 78.09, 99.34, 152.56, 170.68),
    (0.0, 30.29, 50.44, 98.38, 99.94, 169.35, 241.95),
)
EMBED_STEPS = (0.0, 8.91, 16.59, 27.36, 29.51, 45.31, 65.65)
SCATTER_KINDS = (0, 1, 0, 1, 3, 2, 3, 2, 1, 3, 0, 0, 1, 2, 1, 2, 2, 3)
SCATTER_GAPS = (191.0, 0.0, 5.73, 2.04, 0.46, 0.0, 7.0, 4.69, 0.0, 4.57, 0.08, 3.68, 7.84, 0.0, 3.15, 0.0, 21.45, 10.42)
SCATTER_STEPS = (
    (0.0, 4.04, 12.95, 23.87, 32.6, 36.14, 42.79),
    (0.0, 3.0, 16.04, 20.81, 25.89, 31.51, 36.95),
    (0.0, 1.97, 9.58, 17.57, 26.02, 34.36, 45.87),
    (0.0, 1.34, 11.81, 18.03, 25.35, 32.29, 46.72),
    (0.0, 5.46, 23.87, 29.46, 35.73, 45.62, 73.83),
    (0.0, 4.56, 17.74, 24.03, 29.36, 35.29, 63.7),
    (0.0, 5.03, 14.62, 19.72, 24.8, 28.81, 109.64),
    (0.0, 2.85, 10.48, 21.98, 25.03, 54.32, 92.15),
    (0.0, 6.97, 13.67, 20.43, 25.72, 77.02, 206.52),
    (0.0, 12.41, 21.43, 58.18, 71.76, 81.1, 168.25),
    (0.0, 3.91, 15.0, 16.25, 21.35, 24.72, 121.97),
    (0.0, 8.0, 14.81, 21.25, 76.96, 144.83, 236.56),
    (0.0, 2.83, 11.79, 24.73, 61.73, 150.58, 197.54),
    (0.0, 2.49, 11.12, 55.01, 102.76, 109.24, 203.32),
    (0.0, 3.22, 41.46, 48.01, 73.25, 126.87, 208.6),
    (0.0, 3.06, 48.3, 102.56, 113.82, 171.84, 210.86),
    (0.0, 19.43, 79.99, 83.8, 142.14, 167.44, 256.6),
    (0.0, 1.16, 68.62, 72.95, 111.24, 153.3, 212.93),
)
PACE = 1.058


class Plan:
    def __init__(self, dims, count):
        self.dims = dims
        self.tabled = dims == (4, 2, 2) and count == len(GATHER_START)
        self.gather_kinds = GATHER_KINDS if self.tabled else [k % 2 for k in range(count)]
        self.scatter_kinds = SCATTER_KINDS if self.tabled else [k % 2 for k in range(count)]
        self.gaps = SCATTER_GAPS if self.tabled else [CHUNK] * count
        self.pace = PACE if self.tabled else 1.0

    def steps(self, order, back):
        units = [math.prod(self.dims[a] for a in order[:k]) for k in range(3) for _ in range(self.dims[order[k]] - 1)]
        times = [0.0, 3.0] if back else [0.0]
        for unit in reversed(units) if back else units:
            times.append(times[-1] + 1.6 * unit + 3.0)
        return times if back else times + [times[-1] + 4.0]

    def gather(self, c):
        kind = self.gather_kinds[c]
        if self.tabled:
            return KINDS[kind], [GATHER_START[c] + t for t in GATHER_STEPS[c]]
        return KINDS[kind], [CHUNK * c + t for t in self.steps(KINDS[kind], False)]

    def scatter(self, c):
        kind = self.scatter_kinds[c]
        return KINDS[kind], SCATTER_STEPS[c] if self.tabled else self.steps(KINDS[kind], True)

    def embeddings(self, start):
        order = (2, 1, 0)
        return order, [start + t for t in (EMBED_STEPS if self.tabled else self.steps(order, False))]


def fused_kernel(dims, sizes, refs):
    layer = Layer(dims, sizes, refs)
    blocks = sizes.hidden_blocks
    layer.sent, layer.ends, layer.sending, layer.ring_sent, layer.peer_sent = [], [], {}, {}, {}
    timeline = Timeline()

    layer.load()
    layer.own_emb[...] = jnp.zeros_like(layer.own_emb)
    ready = {}
    plan = Plan(dims, FFN + 2 * blocks)
    for c, name in enumerate(range(FFN + 2 * blocks)):
        order, times = plan.gather(c)
        timeline.add_steps([-1.0] + times, layer.gather(c, name, order))
        ready[name] = times[-1]
    timeline.add(-0.5, lambda: greet_lines(layer.place))

    clock = [0.0]

    def compute(fn, cost, *needs):
        clock[0] = max([clock[0] + 0.001] + [ready[n] + 0.01 for n in needs])
        timeline.add(clock[0], fn)
        clock[0] += cost * plan.pace
        return clock[0]

    compute(layer.take_patches, 0.1)
    compute(layer.take_text, 0.5)
    compute(layer.image_features, 1.6, IMAGE)
    compute(layer.region, 0.8)
    compute(layer.take_cotangent, 0.5)
    compute(layer.self_projections, 2.0, QUERY, KEY, VALUE)
    compute(layer.self_attention, 4.0)
    compute(layer.norm_params, 0.2, SMALL)
    compute(layer.pools, 0.3)
    start = compute(layer.embed, 0.3)
    order, times = plan.embeddings(start)
    timeline.add_steps(times, layer.gather_embeddings(len(ready), order))
    ready[EMBEDDINGS] = times[-1]
    compute(layer.after_self, 2.7, ATTN_OUT)
    compute(layer.make_keys, 2.3, CROSS_KEY)
    compute(layer.make_values, 2.3, CROSS_VALUE)
    compute(layer.cross_query, 0.6, CROSS_QUERY)
    compute(layer.cross_attention, 4.5)
    compute(layer.after_cross, 2.0, CROSS_OUT)
    compute(lambda: layer.settle([SMALL]), 0.0, EMBEDDINGS)
    compute(layer.contrast, 4.0)
    for k in range(blocks):
        compute(functools.partial(layer.ffn_in, k), 1.6, FFN + k)
    for k in range(blocks):
        compute(functools.partial(layer.ffn_out, k), 1.0, FFN + blocks + k)

    done = {}
    compute(layer.output_and_back, 4.0)
    compute(lambda: layer.settle(list(layer.sending)), 0.0)
    compute(layer.joined_over, 0.1)
    for k in range(blocks):
        done[FFN + blocks + k] = compute(functools.partial(layer.ffn_out_back, k), 2.2)
    for k in range(blocks):
        done[FFN + k] = compute(functools.partial(layer.ffn_in_back, k), 1.9)
    compute(functools.partial(layer.back_through_norm, 1), 1.8)
    done[CROSS_OUT] = compute(lambda: layer.branch_back(CROSS_OUT, layer.a2), 1.8)
    compute(layer.cross_attention_back, 5.0)
    done[CROSS_QUERY] = compute(layer.cross_query_back, 1.5)
    compute(layer.image_back, 5.0)
    done[CROSS_KEY] = compute(lambda: layer.cross_key_back(CROSS_KEY, layer.k2), 2.4)
    done[CROSS_VALUE] = compute(lambda: layer.cross_key_back(CROSS_VALUE, layer.v2), 2.4)
    compute(layer.patch_back, 5.5)
    done[IMAGE] = compute(layer.image_weight_back, 2.3)
    compute(layer.image_credit, 0.1)
    compute(functools.partial(layer.back_through_norm, 0), 1.8)
    done[ATTN_OUT] = compute(lambda: layer.branch_back(ATTN_OUT, layer.a1), 1.8)
    done[SMALL] = compute(layer.small_grads, 0.5)
    compute(layer.self_attention_back, 5.0)
    for k, name in enumerate((QUERY, KEY, VALUE)):
        done[name] = compute(functools.partial(layer.self_projection_back, k), 1.5)
    compute(layer.text_out, 2.0)

    start, ends, peer_ends = 0.0, [], []
    for c, name in enumerate(grad_order(blocks)):
        order, steps = plan.scatter(c)
        start = max(start + plan.gaps[c], done[name])
        if name != IMAGE and len(ends) >= PEER_RING:
            start = max(start, peer_ends[len(ends) - PEER_RING] + 0.1)
        if name != IMAGE and len(ends) >= ARRIVE_RING:
            start = max(start, ends[len(ends) - ARRIVE_RING] + 0.1 - steps[1])
        times = [start + 0.02 + t for t in steps]
        if name in (IMAGE, SMALL):
            times.append(times[-1] + 3.0)
        timeline.add_steps(times, layer.scatter(c, len(ends), name, order, sizes.ring_total))
        if name != IMAGE:
            peer_ends.append(times[1])
            ends.append(times[len(steps) - 1])
    timeline.run()
    assert not layer.sending
    for end in layer.ends:
        end()
    for sent in (layer.sent, *layer.ring_sent.values(), *layer.peer_sent.values()):
        wait_sent(sent)
    assert layer.blocks.top <= layer.t.shape[0], layer.blocks.top
    assert layer.wide.top <= layer.u.shape[0], layer.wide.top


def fused_body(
    text,
    patches,
    cotangent,
    region_counts,
    phrase_starts,
    phrase_lengths,
    box_patches,
    query_weight,
    key_weight,
    value_weight,
    attn_out_weight,
    cross_query_weight,
    cross_key_weight,
    cross_value_weight,
    cross_out_weight,
    image_weight,
    ffn_in_weight,
    ffn_out_weight,
    text_embed_weight,
    image_embed_weight,
    *norm_shards,
):
    dims = split_dims(lax.axis_size("dp"))
    mp = lax.axis_index("mp")
    pairs, patch_count, depth = patches.shape
    length, model_width = text.shape[1:]
    half = query_weight.shape[1]
    rows = query_weight.shape[0]
    hidden_blocks = ffn_in_weight.shape[1] // half
    embed_half = text_embed_weight.shape[1] // 2

    slot = jax.ShapeDtypeStruct((rows, half), BF16)
    shards = {name: slot for name in range(FFN + 2 * hidden_blocks)}
    shards[IMAGE] = jax.ShapeDtypeStruct((image_weight.shape[0], half), BF16)
    whole = {
        IMAGE: image_weight,
        QUERY: query_weight,
        KEY: key_weight,
        VALUE: value_weight,
        ATTN_OUT: attn_out_weight.T,
        CROSS_KEY: cross_key_weight,
        CROSS_VALUE: cross_value_weight,
        CROSS_QUERY: cross_query_weight,
        CROSS_OUT: cross_out_weight.T,
    }
    order = range(FFN + 2 * hidden_blocks)
    sizes = types.SimpleNamespace(
        pairs=pairs,
        length=length,
        patch_count=patch_count,
        half=half,
        hidden_blocks=hidden_blocks,
        embed_half=embed_half,
        ring_total=len(order) - 1,
    )
    count, text_rows, patch_rows = len(order), pairs * TEXT_PAD, pairs * PATCH_PAD
    couples = model_width // 128
    anywhere, vmem = pl.BlockSpec(memory_space=pl.ANY), pl.BlockSpec(memory_space=pltpu.VMEM)

    inputs = dict(
        text_in=(text, anywhere),
        cot_in=(cotangent, anywhere),
        patches_in=(
            jnp.pad(patches, ((0, 0), (0, PATCH_PAD - patch_count), (0, 0))).reshape(-1, depth),
            anywhere,
        ),
        ffn_in_all=(ffn_in_weight, anywhere),
        ffn_out_all=(ffn_out_weight.T, anywhere),
        text_embed=(text_embed_weight, anywhere),
        image_embed=(image_embed_weight, anywhere),
        norm_rows_in=(jnp.stack(norm_shards), vmem),
        counts=(region_counts.reshape(1, -1), vmem),
        starts=(phrase_starts.T, vmem),
        lengths=(phrase_lengths.T, vmem),
        picks=(box_patches, vmem),
    )
    outputs = dict(
        joined_out=(jax.ShapeDtypeStruct((2, pairs, length, model_width), BF16), anywhere),
        text_out_ref=(jax.ShapeDtypeStruct((2, pairs, length, model_width), F32), anywhere),
        patch_grad=(jax.ShapeDtypeStruct((pairs, patch_count, depth), F32), anywhere),
    )
    result_shapes = []
    for name in order:
        shape = shards[name].shape
        result_shapes.append(jax.ShapeDtypeStruct(((2,) if name in (IMAGE, SMALL) else ()) + shape, F32))
    units = max(arrive_units(dims, o) for o in KINDS)
    dma, regular = pltpu.SemaphoreType.DMA, pltpu.SemaphoreType.REGULAR
    scratch = dict(
        t=pltpu.VMEM((42, text_rows, half), BF16),
        u=pltpu.VMEM((8, patch_rows, half), BF16),
        patches=pltpu.VMEM((patch_rows, depth), BF16),
        p1=pltpu.VMEM((pairs, couples * TEXT_PAD, 2 * TEXT_PAD), BF16),
        p2=pltpu.VMEM((pairs, couples * TEXT_PAD, 2 * PATCH_PAD), BF16),
        z=pltpu.VMEM((text_rows, model_width), F32),
        hid=pltpu.VMEM((text_rows, model_width), F32),
        inv=pltpu.VMEM((2, text_rows, 1), F32),
        norms=pltpu.VMEM((8, model_width), F32),
        norm_grad=pltpu.VMEM((8, model_width), F32),
        pool=pltpu.VMEM((2, 16, model_width), F32),
        raw=pltpu.VMEM((2, 16, 2 * embed_half), F32),
        own_emb=pltpu.VMEM((16, 4 * embed_half), BF16),
        emb=pltpu.VMEM((2,) + dims + (16, 4 * embed_half), BF16),
        extra=pltpu.VMEM((2, 16, model_width), F32),
        chosen=pltpu.VMEM((pairs, 8, PATCH_PAD), F32),
        span=pltpu.VMEM((pairs, 8, TEXT_PAD), F32),
        regions=pltpu.VMEM((pairs, 8, model_width), F32),
        joined=pltpu.VMEM((pairs, length, model_width), BF16),
        text_stage=pltpu.VMEM((2, length, model_width), F32),
        patch_stage=pltpu.VMEM((2, patch_count, depth), F32),
        peer_in=pltpu.VMEM((PEER_RING,) + dims + (rows, half), BF16),
        arrive=pltpu.VMEM((ARRIVE_RING, units, rows, half), BF16),
        load_sem=dma((3,)),
        own_sem=dma((count + 1,)),
        g_send=dma((count + 1, send_slots(dims))),
        g_recv=dma((count + 1, gather_slots(dims))),
        gp_send=dma((count + 1,)),
        gp_recv=dma((count + 1,)),
        s_send=dma((ARRIVE_RING + 1, send_slots(dims))),
        s_recv=dma((ARRIVE_RING + 1, send_slots(dims))),
        sp_send=dma((PEER_RING + 1,)),
        sp_recv=dma((PEER_RING + 1,)),
        h_send=dma((2,)),
        h_recv=dma((2,)),
        out_own=dma,
        out_send=dma,
        out_recv=dma,
        text_own=dma((pairs,)),
        text_send=dma((pairs,)),
        text_recv=dma((pairs,)),
        patch_sem=dma((2,)),
        credits=regular((ARRIVE_RING + 1, 6)),
        peer_credits=regular((PEER_RING + 1,)),
    )
    weights = [pltpu.VMEM((2,) + dims + shards[name].shape, BF16) for name in order]

    def kernel(*refs):
        refs = list(refs)

        def some(names):
            part = dict(zip(names, refs))
            del refs[: len(part)]
            return part

        table = some(inputs)
        table.update(shards=some(whole))
        table.update(some(outputs))
        table.update(results=some(order))
        table.update(some(scratch))
        table.update(w=some(order))
        fused_kernel(dims, sizes, table)

    results = pl.pallas_call(
        kernel,
        out_shape=[s for s, _ in outputs.values()] + result_shapes,
        in_specs=[spec for _, spec in inputs.values()] + [anywhere] * len(whole),
        out_specs=[spec for _, spec in outputs.values()] + [vmem] * count,
        scratch_shapes=list(scratch.values()) + weights,
        compiler_params=pltpu.CompilerParams(
            collective_id=2, has_side_effects=True, vmem_limit_bytes=64 * 2**20
        ),
        name="layer",
    )(*[x for x, _ in inputs.values()], *whole.values())
    return finish(results, sizes, dims, model_width)


def finish_kernel(sizes, count, joined, text_grad, patch_grad, *refs):
    blocks, half, width = sizes.hidden_blocks, sizes.half, sizes.embed_half
    own, small = refs[:count], refs[SMALL]
    outs, (stage_joined, stage_text, stage_patch, in_sem, out_sem) = refs[count:-5], refs[-5:]
    pieces = []
    for src, stage, dst in ((joined, stage_joined, outs[0]), (text_grad, stage_text, outs[1])):
        pieces += [(src.at[k], stage.at[k], dst.at[k]) for k in range(2)]
    pieces += [(patch_grad.at[p], stage_patch.at[p], outs[2].at[p]) for p in range(sizes.pairs)]
    into = [pltpu.make_async_copy(src, stage, in_sem.at[k]) for k, (src, stage, _) in enumerate(pieces)]
    back = [pltpu.make_async_copy(stage, dst, out_sem.at[k]) for k, (_, stage, dst) in enumerate(pieces)]
    for copy in into:
        copy.start()
    for first, second in zip(into, back):
        first.wait()
        second.start()
    for k in range(2):
        outs[11][:, k * half : (k + 1) * half] = own[IMAGE][k]
        for j in range(2):
            outs[14 + j][:, k * width : (k + 1) * width] = small[k, :, j * width : (j + 1) * width]
    singles = (QUERY, KEY, VALUE, ATTN_OUT, CROSS_QUERY, CROSS_KEY, CROSS_VALUE, CROSS_OUT)
    for k, name in enumerate(singles):
        outs[3 + k][...] = own[name][...]
    for k in range(blocks):
        cols = slice(k * half, (k + 1) * half)
        outs[12][:, cols] = own[FFN + k][...]
        outs[13][:, cols] = own[FFN + blocks + k][...]
    rows = jnp.transpose(small[lax.axis_index("mp")][:, 2 * width :])
    for k in range(6):
        outs[16 + k][...] = rows[k : k + 1]
    for copy in back:
        copy.wait()


def finish(results, sizes, dims, model_width):
    anywhere, vmem = pl.BlockSpec(memory_space=pl.ANY), pl.BlockSpec(memory_space=pltpu.VMEM)
    own = results[3:]
    rows, half, width, blocks = own[QUERY].shape[0], sizes.half, sizes.embed_half, sizes.hidden_blocks
    shapes = [r.shape for r in results[:3]] + [(rows, half)] * 8
    shapes += [(own[IMAGE].shape[1], 2 * half)] + [(rows, blocks * half)] * 2 + [(rows, 2 * width)] * 2 + [(1, rows)] * 6
    types = [BF16] + [F32] * (len(shapes) - 1)
    outs = pl.pallas_call(
        functools.partial(finish_kernel, sizes, len(own)),
        out_shape=[jax.ShapeDtypeStruct(s, t) for s, t in zip(shapes, types)],
        in_specs=[anywhere] * 3 + [vmem] * len(own),
        out_specs=[anywhere] * 3 + [vmem] * 19,
        scratch_shapes=[pltpu.VMEM(r.shape, r.dtype) for r in results[:3]]
        + [pltpu.SemaphoreType.DMA((4 + sizes.pairs,))] * 2,
        compiler_params=pltpu.CompilerParams(vmem_limit_bytes=60 * 2**20),
        name="results",
    )(*results)
    whole = (2 * sizes.pairs, sizes.length, model_width)
    turned = (6, 10, 13)
    done = [outs[0].reshape(whole), outs[1].reshape(whole), *outs[2:16]]
    done = [x.T if k in turned else x for k, x in enumerate(done)]
    return (*done, *(x.reshape(-1) for x in outs[16:]))


def pad_rows(x, rows):
    return jnp.pad(x, ((0, rows - x.shape[0]), (0, 0)))


def body(
    text,
    patches,
    cotangent,
    region_counts,
    phrase_starts,
    phrase_lengths,
    box_patches,
    query_weight,
    key_weight,
    value_weight,
    attn_out_weight,
    cross_query_weight,
    cross_key_weight,
    cross_value_weight,
    cross_out_weight,
    image_weight,
    ffn_in_weight,
    ffn_out_weight,
    text_embed_weight,
    image_embed_weight,
    *norm_shards,
):
    dp = lax.axis_size("dp")
    dims = split_dims(dp)
    mp = lax.axis_index("mp")
    half_pairs, patch_count, _ = patches.shape
    length, model_width = text.shape[1:]
    half = query_weight.shape[1]
    rows = query_weight.shape[0]
    hidden_blocks = ffn_in_weight.shape[1] // half
    embed_half = text_embed_weight.shape[1] // 2
    image_rows_own = image_weight.shape[0]

    if rows % 16 == 0 and dims[0] % 2 == 0 and half % 128 == 0 and half == model_width // 2 and half_pairs % 2 == 0:
        return fused_body(
            text, patches, cotangent, region_counts, phrase_starts, phrase_lengths, box_patches,
            query_weight, key_weight, value_weight, attn_out_weight, cross_query_weight, cross_key_weight,
            cross_value_weight, cross_out_weight, image_weight, ffn_in_weight, ffn_out_weight,
            text_embed_weight, image_embed_weight, *norm_shards,
        )

    def own_half(x, size, dim):
        return lax.dynamic_slice_in_dim(x, mp * size, size, dim)

    text, cotangent = own_half(text, half_pairs, 0), own_half(cotangent, half_pairs, 0)
    region_counts, phrase_starts = own_half(region_counts, half_pairs, 0), own_half(phrase_starts, half_pairs, 0)
    phrase_lengths, box_patches = own_half(phrase_lengths, half_pairs, 0), own_half(box_patches, half_pairs, 0)

    padded = -(-rows // 16) * 16
    small = jnp.concatenate(
        [own_half(text_embed_weight, embed_half, 1), own_half(image_embed_weight, embed_half, 1)]
        + [jnp.pad(jnp.stack(norm_shards, 1), ((0, 0), (0, half - 2 * embed_half - len(norm_shards))))],
        1,
    )
    ffn_out_t = ffn_out_weight.T
    shards = [
        own_half(image_weight, half, 1),
        query_weight,
        key_weight,
        value_weight,
        attn_out_weight.T,
        small,
        cross_key_weight,
        cross_value_weight,
        cross_query_weight,
        cross_out_weight.T,
        *(ffn_in_weight[:, k * half : (k + 1) * half] for k in range(hidden_blocks)),
        *(ffn_out_t[:, k * half : (k + 1) * half] for k in range(hidden_blocks)),
    ]
    real = [s.shape[0] for s in shards]
    shards = [pad_rows(s, -(-s.shape[0] // 16) * 16) for s in shards]
    gathered = gather(shards, dims)

    def merge(g, n):
        g = g.reshape(2, dp, *g.shape[-2:])[:, :, :n]
        return g.reshape(2, dp * n, g.shape[-1])

    gathered = [merge(g, n) for g, n in zip(gathered, real)]

    def columns(g):
        return jnp.concatenate([g[0], g[1]], 1)

    def blocks(gs):
        return jnp.concatenate([g[0] for g in gs] + [g[1] for g in gs], 1)

    image_w, query_w, key_w, value_w, attn_out_t = (columns(g) for g in gathered[:5])
    embeds = gathered[5]
    text_embed32 = columns(embeds[:, :, :embed_half]).astype(F32)
    image_embed32 = columns(embeds[:, :, embed_half : 2 * embed_half]).astype(F32)
    norms = embeds[0, :, 2 * embed_half : 2 * embed_half + len(norm_shards)].astype(F32).T
    gain_one, bias_one, gain_two, bias_two, gain_three, bias_three = (norms[k] for k in range(6))
    cross_key_w, cross_value_w, cross_query_w, cross_out_t = (columns(g) for g in gathered[6:10])
    ffn_in_w = blocks(gathered[10 : 10 + hidden_blocks])
    ffn_out_tw = blocks(gathered[10 + hidden_blocks :])

    text_rows = text.reshape(half_pairs * length, model_width)
    patch_rows = patches.reshape(half_pairs * patch_count, -1)
    image_rows = matmul(patch_rows, image_w).astype(BF16)
    image32 = image_rows.astype(F32).reshape(half_pairs, patch_count, model_width)
    queries = split_heads(matmul(text_rows, query_w).astype(BF16), half_pairs)
    key_heads = split_heads(matmul(text_rows, key_w).astype(BF16), half_pairs)
    value_heads = split_heads(matmul(text_rows, value_w).astype(BF16), half_pairs)
    self_mixed, self_total = attend(queries, key_heads, value_heads)
    first = text_rows.astype(F32) + contract_cols(self_mixed, attn_out_t)
    hidden_one, normed_one, inv_one = layer_norm(first, gain_one, bias_one)
    low_one = hidden_one.astype(BF16)
    cross_queries = split_heads(matmul(low_one, cross_query_w).astype(BF16), half_pairs)
    cross_keys = split_heads(matmul(image_rows, cross_key_w).astype(BF16), half_pairs)
    cross_values = split_heads(matmul(image_rows, cross_value_w).astype(BF16), half_pairs)
    cross_mixed, cross_total = attend(cross_queries, cross_keys, cross_values)
    second = hidden_one + contract_cols(cross_mixed, cross_out_t)
    hidden_two, normed_two, inv_two = layer_norm(second, gain_two, bias_two)
    low_two = hidden_two.astype(BF16)
    inner = matmul(low_two, ffn_in_w)
    active = jax.nn.gelu(inner, approximate=False).astype(BF16)
    third = hidden_two + contract_cols(active, ffn_out_tw)
    output, normed_three, inv_three = layer_norm(third, gain_three, bias_three)
    output3 = output.reshape(half_pairs, length, model_width)
    joined = output3.astype(BF16)

    text_pool = jnp.mean(text.astype(F32), 1)
    image_pool = jnp.mean(image32, 1)
    grad_text_embed, grad_image_embed, text_extra, image_pool_grad = contrast(
        text_pool, image_pool, text_embed32, image_embed32
    )
    text_extra = (text_extra / length)[:, None, :]
    image_pool_grad = image_pool_grad / patch_count
    positions = jnp.arange(length, dtype=jnp.int32)
    slots = jnp.arange(phrase_starts.shape[1], dtype=jnp.int32)
    valid = (slots[None, :] < region_counts[:, None]).astype(F32)
    ends = phrase_starts + phrase_lengths
    inside = ((positions >= phrase_starts[..., None]) & (positions < ends[..., None])).astype(F32) * valid[..., None]
    span_weight = inside / phrase_lengths[..., None].astype(F32)
    chosen = (
        jnp.sum((box_patches[..., None] == jnp.arange(patch_count, dtype=jnp.int32)).astype(F32), axis=2)
        / box_patches.shape[2]
    )
    phrase = jnp.einsum("pbt,ptd->pbd", span_weight, output3, precision=HIGHEST)
    region = jnp.einsum("pbn,pnd->pbd", chosen, image32, precision=HIGHEST)
    mismatch = (phrase - region) * valid[..., None]
    box_text = jnp.einsum("pbt,pbd->ptd", span_weight, mismatch, precision=HIGHEST)
    box_image = -jnp.einsum("pbn,pbd->pnd", chosen, mismatch, precision=HIGHEST)
    image_extra = (box_image + image_pool_grad[:, None, :]).reshape(-1, model_width)

    upstream = cotangent.astype(F32).reshape(-1, model_width) + box_text.reshape(-1, model_width)
    grad_third, gain_three_grad, bias_three_grad = norm_back(upstream, normed_three, inv_three, gain_three)
    low_third = grad_third.astype(BF16)
    grad_ffn_out_t = contract_rows(low_third, active)
    dactive = matmul(low_third, ffn_out_tw)
    gelu_pull = jax.vjp(lambda values: jax.nn.gelu(values, approximate=False), inner)[1]
    dinner = gelu_pull(dactive)[0].astype(BF16)
    grad_ffn_in = contract_rows(low_two, dinner)
    grad_second = grad_third + contract_cols(dinner, ffn_in_w)
    grad_second, gain_two_grad, bias_two_grad = norm_back(grad_second, normed_two, inv_two, gain_two)
    low_second = grad_second.astype(BF16)
    grad_cross_out_t = contract_rows(low_second, cross_mixed)
    dcross = split_heads(matmul(low_second, cross_out_t).astype(BF16), half_pairs)
    dqueries, dkeys, dvalues = attend_back(cross_queries, cross_keys, cross_values, cross_total, dcross)
    grad_cross_query = contract_rows(low_one, dqueries)
    grad_first = grad_second + contract_cols(dqueries, cross_query_w)
    grad_cross_key = contract_rows(image_rows, dkeys)
    grad_cross_value = contract_rows(image_rows, dvalues)
    dimage = contract_cols(dkeys, cross_key_w) + contract_cols(dvalues, cross_value_w) + image_extra
    low_image = dimage.astype(BF16)
    grad_image = contract_rows(patch_rows, low_image)
    patch_grad = contract_cols(low_image, image_w).reshape(patches.shape)
    grad_first, gain_one_grad, bias_one_grad = norm_back(grad_first, normed_one, inv_one, gain_one)
    low_first = grad_first.astype(BF16)
    grad_attn_out_t = contract_rows(low_first, self_mixed)
    dself = split_heads(matmul(low_first, attn_out_t).astype(BF16), half_pairs)
    dqueries, dkeys, dvalues = attend_back(queries, key_heads, value_heads, self_total, dself)
    grad_query = contract_rows(text_rows, dqueries)
    grad_key = contract_rows(text_rows, dkeys)
    grad_value = contract_rows(text_rows, dvalues)
    dtext = contract_cols(dqueries, query_w) + contract_cols(dkeys, key_w) + contract_cols(dvalues, value_w)
    text_grad = (grad_first + dtext).reshape(half_pairs, length, model_width) + text_extra

    def halves(g):
        g = g.astype(BF16)
        return jnp.stack([g[:, :half], g[:, half:]], 0)

    def hidden_halves(g):
        g = g.astype(BF16)
        return [
            jnp.stack([g[:, k * half : (k + 1) * half], g[:, (hidden_blocks + k) * half : (hidden_blocks + k + 1) * half]])
            for k in range(hidden_blocks)
        ]

    norm_grads = jnp.stack(
        [gain_one_grad, bias_one_grad, gain_two_grad, bias_two_grad, gain_three_grad, bias_three_grad], 1
    ).astype(BF16)
    norm_grads = jnp.pad(norm_grads, ((0, 0), (0, half - 2 * embed_half - len(norm_shards))))
    text_half, image_half = grad_text_embed.astype(BF16), grad_image_embed.astype(BF16)
    small_grads = jnp.stack(
        [
            jnp.concatenate(
                [text_half[:, k * embed_half : (k + 1) * embed_half], image_half[:, k * embed_half : (k + 1) * embed_half], norm_grads], 1
            )
            for k in range(2)
        ]
    )
    grads = [
        *hidden_halves(grad_ffn_out_t),
        *hidden_halves(grad_ffn_in),
        halves(grad_cross_out_t),
        halves(grad_cross_query),
        halves(grad_cross_key),
        halves(grad_cross_value),
        halves(grad_image),
        halves(grad_attn_out_t),
        halves(grad_query),
        halves(grad_key),
        halves(grad_value),
        small_grads,
    ]
    shared = (2 * hidden_blocks + 4, len(grads) - 1)

    def cut(g):
        n = g.shape[1] // dp
        g = g.reshape(2, dp, n, g.shape[-1])
        g = jnp.pad(g, ((0, 0), (0, 0), (0, -(-n // 16) * 16 - n), (0, 0)))
        return g.reshape(2, *dims, *g.shape[-2:])

    results = scatter([cut(g) for g in grads], shared, (joined, text_grad), dims)
    joined_all, text_grad_all = (r.reshape(2 * half_pairs, length, model_width) for r in results[len(grads) :])
    sums = [r[..., :n, :] for r, n in zip(results, [g.shape[1] // dp for g in grads])]
    ffn_out_own = jnp.concatenate(sums[:hidden_blocks], 1).T
    ffn_in_own = jnp.concatenate(sums[hidden_blocks : 2 * hidden_blocks], 1)
    cross_out_own, cross_query_own, cross_key_own, cross_value_own, image_own, attn_out_own, query_own, key_own, value_own, small_own = sums[2 * hidden_blocks :]
    own_norm = lax.dynamic_index_in_dim(small_own, mp, 0, keepdims=False)[:, 2 * embed_half :]
    return (
        joined_all,
        text_grad_all,
        patch_grad,
        query_own,
        key_own,
        value_own,
        attn_out_own.T,
        cross_query_own,
        cross_key_own,
        cross_value_own,
        cross_out_own.T,
        jnp.concatenate([image_own[0], image_own[1]], 1),
        ffn_in_own,
        ffn_out_own,
        jnp.concatenate([small_own[0, :, :embed_half], small_own[1, :, :embed_half]], 1),
        jnp.concatenate([small_own[0, :, embed_half : 2 * embed_half], small_own[1, :, embed_half : 2 * embed_half]], 1),
        own_norm[:, 0],
        own_norm[:, 1],
        own_norm[:, 2],
        own_norm[:, 3],
        own_norm[:, 4],
        own_norm[:, 5],
    )


def solution(mesh):
    pairs, weight, turned, single = P("dp", None, None), P("dp", "mp"), P("mp", "dp"), P("dp", None)
    weights = (weight, weight, weight, turned, weight, weight, weight, turned, single, weight, turned, single, single)
    norms = (P("dp"),) * 6
    halves = P(("dp", "mp"), None, None)
    in_specs = (pairs, halves, pairs, P("dp"), single, single, pairs) + weights + norms
    out_specs = (pairs, pairs, halves) + weights + norms
    return jax.shard_map(body, mesh=mesh, in_specs=in_specs, out_specs=out_specs, check_vma=False)
```

```python
import functools
import math
import types

import jax
import jax.numpy as jnp
from jax import lax
from jax.experimental import pallas as pl
from jax.experimental.pallas import tpu as pltpu
from jax.sharding import PartitionSpec as P

HEAD_DIM = 64
EPS = 1e-06
TEMP_INVERSE = 20.0
GRAD_SCALE = 10.0
HIGHEST = lax.Precision.HIGHEST
MESH = pl.DeviceIdType.MESH
BF16 = jnp.bfloat16
F32 = jnp.float32


def split_dims(count):
    side = math.isqrt(count // 4) if count % 4 == 0 else 0
    if side and 4 * side * side == count:
        return (4, side, side)
    return (count, 1, 1)


class Place:
    def __init__(self, dims):
        self.dims = dims
        dp = lax.axis_index("dp")
        self.mp = lax.axis_index("mp")
        self.pos = (dp // (dims[1] * dims[2]), (dp // dims[2]) % dims[1], dp % dims[2])

    def at(self, axis, coord):
        spot = list(self.pos)
        spot[axis] = coord
        return ((spot[0] * self.dims[1] + spot[1]) * self.dims[2] + spot[2], self.mp)

    def peer(self):
        return (lax.axis_index("dp"), 1 - self.mp)


def block_of(place, order, stage, coord):
    index = [None] * 3
    for rank, axis in enumerate(order):
        index[axis] = slice(None) if rank < stage else (coord if rank == stage else place.pos[axis])
    return tuple(index)


def remote(src, dst, send_sem, recv_sem, device):
    return pltpu.make_async_remote_copy(
        src_ref=src,
        dst_ref=dst,
        send_sem=send_sem,
        recv_sem=recv_sem,
        device_id=device,
        device_id_type=MESH,
    )


def greet_lines(place):
    sem = pltpu.get_barrier_semaphore()

    def greet(device):
        pl.semaphore_signal(sem, inc=1, device_id=device, device_id_type=MESH)

    greet(place.peer())
    count = 1
    for axis in range(3):
        for away in range(1, place.dims[axis]):
            greet(place.at(axis, lax.rem(place.pos[axis] + away, place.dims[axis])))
            count += 1
    pl.semaphore_wait(sem, count)


def line_ways(length):
    return 2 if length > 2 else min(length - 1, 1)


def line_slots(length):
    return line_ways(length) * (length - 1)


def send_slot(dims, axis, way):
    return sum(line_ways(d) for d in dims[:axis]) + (way if dims[axis] > 2 else 0)


def send_slots(dims):
    return sum(line_ways(d) for d in dims)


def sum_slot(dims, axis, way, step):
    length = dims[axis]
    return sum(line_slots(d) for d in dims[:axis]) + (way * (length - 1) if length > 2 else 0) + step - 1


def sum_slots(dims):
    return sum(line_slots(d) for d in dims)


def gather_slots(dims):
    return sum(d - 1 for d in dims)


def gather_steps(place, order, buf, send_sem, recv_sem):
    sent = []
    for stage, axis in enumerate(order):
        length, pos = place.dims[axis], place.pos[axis]
        if length == 1:
            continue
        base = sum(d - 1 for d in place.dims[:axis])

        def copy(way, step, coord, to, stage=stage, axis=axis, pos=pos, base=base):
            ref = buf.at[block_of(place, order, stage, coord)]
            arrival = recv_sem.at[base + coord - (coord > to).astype(jnp.int32)]
            return remote(ref, ref, send_sem.at[send_slot(place.dims, axis, way)], arrival, place.at(axis, to))

        for step in range(1, length + 1):
            for way in (0, 1):
                coord = pos - (step - 1) if way == 0 else pos + (step - 1)
                to = pos + 1 if way == 0 else pos - 1
                here = (coord >= 0) if way == 0 else (coord < length)
                if step > 1:
                    pl.when(here)(lambda: copy(way, step - 1, coord, pos).wait_recv())
                if step < length:
                    more = jnp.logical_and(here, (to < length) if way == 0 else (to >= 0))

                    def send():
                        if step > 1:
                            copy(way, step, coord, to).wait_send()
                        copy(way, step, coord, to).start()

                    pl.when(more)(send)
                    if step == 1:
                        sent.append((more, functools.partial(copy, way, step, coord, to)))
            if step < length:
                yield
    return sent


def scatter_steps(place, order, acc, arrive, send_sem, recv_sem, result):
    sent = []
    last = [axis for axis in order if place.dims[axis] > 1][0]
    at = 0
    for stage in reversed(range(3)):
        axis = order[stage]
        length, pos = place.dims[axis], place.pos[axis]
        if length == 1:
            continue
        units = math.prod(place.dims[a] for a in order[:stage])
        shape = tuple(place.dims[a] for a in sorted(order[:stage]))

        def copy(way, step, coord, stage=stage, axis=axis, pos=pos, at=at, units=units, length=length, shape=shape):
            src = acc.at[block_of(place, order, stage, coord)]
            slot = at + ((way * (length - 1) if length > 2 else 0) + step - 1) * units
            dst = arrive.at[pl.ds(slot, units)].reshape(*shape, *arrive.shape[1:])
            leaves = send_sem.at[send_slot(place.dims, axis, way)]
            arrives = recv_sem.at[sum_slot(place.dims, axis, way, step)]
            device = place.at(axis, pos + 1 if way == 0 else pos - 1)
            return remote(src, dst, leaves, arrives, device), dst

        for step in range(length - 1, 0, -1):
            for way in (0, 1):
                coord = pos + step if way == 0 else pos - step
                has = (coord < length) if way == 0 else (coord >= 0)
                if step < length - 1:
                    farther = coord + 1 if way == 0 else coord - 1
                    before = (farther < length) if way == 0 else (farther >= 0)
                    pl.when(before)(lambda: copy(way, step, coord)[0].wait_send())
                pl.when(has)(lambda: copy(way, step, coord)[0].start())
                if step == 1:
                    sent.append((has, functools.partial(lambda move, *a: move(*a)[0], copy, way, step, coord)))
            yield
            for way in (0, 1):
                coord = pos - 1 + step if way == 0 else pos + 1 - step
                if way == 0:
                    comes = jnp.logical_and(pos > 0, coord < length)
                else:
                    comes = jnp.logical_and(pos < length - 1, coord >= 0)

                def take():
                    move, ref = copy(way, step, coord)
                    move.wait_recv()
                    index = block_of(place, order, stage, coord)
                    if axis == last and step == 1:
                        total = acc[index].astype(F32) + ref[...].astype(F32)
                        result[...] = total
                        acc[index] = total.astype(BF16)
                    else:
                        acc[index] = acc[index] + ref[...]

                pl.when(comes)(take)
        at += line_slots(length) * units
    return sent


def arrive_units(dims, order):
    units = 0
    for stage in range(3):
        if dims[order[stage]] > 1:
            length = dims[order[stage]]
            units += (2 if length > 2 else 1) * (length - 1) * math.prod(dims[a] for a in order[:stage])
    return units


def in_turn(plan):
    events = sorted((time, which, step) for which, (times, _) in enumerate(plan) for step, time in enumerate(times))
    results = [None] * len(plan)
    for _, which, _ in events:
        if results[which] is None:
            try:
                next(plan[which][1])
            except StopIteration as stop:
                results[which] = stop.value
    assert all(r is not None for r in results)
    return results


def wait_sent(sent):
    for cond, make in sent:
        if cond is None:
            make().wait_send()
        else:
            pl.when(cond)(lambda: make().wait_send())


ORDERS = ((2, 0, 1), (1, 0, 2), (0, 2, 1), (2, 0, 1), (1, 0, 2), (0, 1, 2))


def step_times(dims, order, start, back=False):
    times = [0.0]
    units = 1
    for axis in order:
        for _ in range(dims[axis] - 1):
            times.append(times[-1] + 1.6 * units + 3.0)
        units *= dims[axis]
    times.append(times[-1] + 4.0)
    if back:
        times = [times[-1] - t for t in reversed(times)]
    return [start + t for t in times] + [start + times[-1] + 4.0, start + times[-1] + 8.0]


def gather_kernel(dims, count, *refs):
    ins, outs = refs[:count], refs[count : 2 * count]
    send_sem, recv_sem, own_sem, peer_send, peer_recv = refs[2 * count :]
    place = Place(dims)
    own = [
        pltpu.make_async_copy(ins[c], outs[c].at[(place.mp,) + place.pos], own_sem.at[c]) for c in range(count)
    ]
    for copy in own:
        copy.start()
    greet_lines(place)

    def chunk(c, order):
        own[c].wait()
        mine, other = outs[c].at[place.mp], outs[c].at[1 - place.mp]
        sent = yield from gather_steps(place, order, mine, send_sem.at[c], recv_sem.at[c])

        def copy(ref):
            return remote(ref, ref, peer_send.at[c], peer_recv.at[c], place.peer())

        copy(mine).start()
        yield
        copy(other).wait_recv()
        return sent + [(None, lambda: copy(mine))]

    plan = []
    for c in range(count):
        order = ORDERS[c % len(ORDERS)]
        plan.append((step_times(dims, order, 3.9 * c), chunk(c, order)))
    for sent in in_turn(plan):
        wait_sent(sent)


def gather(shards, dims):
    count = len(shards)
    return pl.pallas_call(
        functools.partial(gather_kernel, dims, count),
        out_shape=[jax.ShapeDtypeStruct((2,) + dims + s.shape, BF16) for s in shards],
        in_specs=[pl.BlockSpec(memory_space=pl.ANY)] * count,
        out_specs=[pl.BlockSpec(memory_space=pl.ANY)] * count,
        scratch_shapes=[
            pltpu.SemaphoreType.DMA((count, send_slots(dims))),
            pltpu.SemaphoreType.DMA((count, gather_slots(dims))),
        ]
        + [pltpu.SemaphoreType.DMA((count,))] * 3,
        compiler_params=pltpu.CompilerParams(collective_id=0, has_side_effects=True),
        name="gather_weights",
    )(*shards)


def scatter_kernel(dims, count, shared, extra, *refs):
    ins, pieces = refs[:count], refs[count : count + extra]
    refs = refs[count + extra :]
    outs, wholes = refs[:count], refs[count : count + extra]
    refs = refs[count + extra :]
    acc, peer_in, arrive = refs[:count], refs[count : 2 * count], refs[2 * count : 3 * count]
    send_sem, recv_sem, own_sem, peer_send, peer_recv, end_send, end_recv, ex_own, ex_send, ex_recv = refs[3 * count :]
    place = Place(dims)
    own = [pltpu.make_async_copy(ins[c].at[place.mp], acc[c], own_sem.at[c]) for c in range(count)]
    for copy in own:
        copy.start()
    keep = [pltpu.make_async_copy(pieces[e], wholes[e].at[place.mp], ex_own.at[e]) for e in range(extra)]
    for copy in keep:
        copy.start()
    greet_lines(place)
    give = [
        remote(pieces[e], wholes[e].at[place.mp], ex_send.at[e], ex_recv.at[e], place.peer()) for e in range(extra)
    ]

    def chunk(c, order):
        def copy():
            return remote(ins[c].at[1 - place.mp], peer_in[c], peer_send.at[c], peer_recv.at[c], place.peer())

        copy().start()
        yield
        own[c].wait()
        copy().wait_recv()
        acc[c][...] = acc[c][...] + peer_in[c][...]
        result = outs[c].at[place.mp] if c in shared else outs[c]
        sent = yield from scatter_steps(
            place, order, acc[c], arrive[c], send_sem.at[c], recv_sem.at[c], result
        )
        sent.append((None, copy))
        if c in shared:

            def hand(half):
                ref = outs[c].at[half]
                return remote(ref, ref, end_send.at[c], end_recv.at[c], place.peer())

            hand(place.mp).start()
            yield
            hand(1 - place.mp).wait_recv()
            sent.append((None, lambda: hand(place.mp)))
        return sent

    plan = []
    for c in range(count):
        order = ORDERS[c % len(ORDERS)]
        plan.append((step_times(dims, order, 3.9 * c, True), chunk(c, order)))
    for copy in give:
        copy.start()
    for sent in in_turn(plan):
        wait_sent(sent)
    for copy in keep:
        copy.wait()
    for copy in give:
        copy.wait()


def scatter(grads, shared, pieces, dims):
    count, extra = len(grads), len(pieces)
    shapes = [
        jax.ShapeDtypeStruct(((2,) if c in shared else ()) + g.shape[-2:], F32) for c, g in enumerate(grads)
    ]
    wholes = [jax.ShapeDtypeStruct((2,) + p.shape, p.dtype) for p in pieces]
    return pl.pallas_call(
        functools.partial(scatter_kernel, dims, count, shared, extra),
        out_shape=shapes + wholes,
        in_specs=[pl.BlockSpec(memory_space=pl.ANY)] * (count + extra),
        out_specs=[pl.BlockSpec(memory_space=pltpu.VMEM)] * count + [pl.BlockSpec(memory_space=pl.ANY)] * extra,
        scratch_shapes=[pltpu.VMEM(g.shape[1:], BF16) for g in grads] * 2
        + [
            pltpu.VMEM((arrive_units(dims, ORDERS[c % len(ORDERS)]),) + g.shape[-2:], BF16)
            for c, g in enumerate(grads)
        ]
        + [pltpu.SemaphoreType.DMA((count, send_slots(dims))), pltpu.SemaphoreType.DMA((count, sum_slots(dims)))]
        + [pltpu.SemaphoreType.DMA((count,))] * 5
        + [pltpu.SemaphoreType.DMA((extra,))] * 3,
        compiler_params=pltpu.CompilerParams(
            collective_id=1, has_side_effects=True, vmem_limit_bytes=60 * 2**20
        ),
        name="scatter_gradients",
    )(*grads, *pieces)


def matmul(left, right):
    return jnp.dot(left, right, preferred_element_type=F32)


def contract_rows(left, right):
    return lax.dot_general(left, right, (((0,), (0,)), ((), ())), preferred_element_type=F32)


def contract_cols(left, right):
    return lax.dot_general(left, right, (((1,), (1,)), ((), ())), preferred_element_type=F32)


def layer_norm(inputs, gain, shift):
    centred = inputs - jnp.mean(inputs, -1, keepdims=True)
    inv_std = lax.rsqrt(jnp.mean(centred * centred, -1, keepdims=True) + EPS)
    normed = centred * inv_std
    return (normed * gain + shift, normed, inv_std)


def norm_back(upstream, normed, inv_std, gain):
    scaled = upstream * gain
    inner_mean = jnp.mean(scaled * normed, -1, keepdims=True)
    result = inv_std * (scaled - jnp.mean(scaled, -1, keepdims=True) - normed * inner_mean)
    return (result, jnp.sum(upstream * normed, 0), jnp.sum(upstream, 0))


def split_heads(flat, pair_count):
    return flat.reshape(pair_count, -1, flat.shape[-1] // HEAD_DIM, HEAD_DIM)


def attend(queries, key_heads, value_heads):
    factor = 1.0 / math.sqrt(HEAD_DIM)
    scores = jnp.einsum("pqhd,pkhd->phqk", queries, key_heads, preferred_element_type=F32) * factor
    row_max = jnp.max(scores, -1, keepdims=True)
    expd = jnp.exp(scores - row_max)
    row_sum = jnp.sum(expd, -1, keepdims=True)
    probs = (expd / row_sum).astype(BF16)
    mixed = jnp.einsum("phqk,pkhd->pqhd", probs, value_heads, preferred_element_type=F32)
    flat_rows = queries.shape[0] * queries.shape[1]
    return (mixed.astype(BF16).reshape(flat_rows, -1), row_max + jnp.log(row_sum))


def attend_back(queries, key_heads, value_heads, log_total, upstream):
    factor = 1.0 / math.sqrt(HEAD_DIM)
    scores = jnp.einsum("pqhd,pkhd->phqk", queries, key_heads, preferred_element_type=F32) * factor
    probs = jnp.exp(scores - log_total)
    dprobs = jnp.einsum("pqhd,pkhd->phqk", upstream, value_heads, preferred_element_type=F32)
    dscores = (probs * (dprobs - jnp.sum(dprobs * probs, -1, keepdims=True))).astype(BF16)
    dqueries = jnp.einsum("phqk,pkhd->pqhd", dscores, key_heads, preferred_element_type=F32) * factor
    dkeys = jnp.einsum("phqk,pqhd->pkhd", dscores, queries, preferred_element_type=F32) * factor
    dvalues = jnp.einsum("phqk,pqhd->pkhd", probs.astype(BF16), upstream, preferred_element_type=F32)
    return tuple(t.astype(BF16).reshape(-1, t.shape[2] * t.shape[3]) for t in (dqueries, dkeys, dvalues))


def unit_back(raw, inv_norm, upstream):
    cubed = inv_norm * inv_norm * inv_norm
    return inv_norm * upstream - raw * cubed * jnp.sum(raw * upstream, -1, keepdims=True)


def contrast(text_pool, image_pool, text_embed32, image_embed32):
    text_raw = jnp.dot(text_pool, text_embed32, precision=HIGHEST)
    text_inv = lax.rsqrt(jnp.sum(text_raw * text_raw, -1, keepdims=True) + EPS)
    image_raw = jnp.dot(image_pool, image_embed32, precision=HIGHEST)
    image_inv = lax.rsqrt(jnp.sum(image_raw * image_raw, -1, keepdims=True) + EPS)
    both = jnp.concatenate([(text_raw * text_inv).astype(BF16), (image_raw * image_inv).astype(BF16)], 1)
    width = text_raw.shape[1]
    everyone = lax.all_gather(both, ("dp", "mp"), axis=0, tiled=True)
    text_all, image_all = everyone[:, :width], everyone[:, width:]
    logits = contract_cols(text_all, image_all) * TEMP_INVERSE
    weights = jnp.exp(logits - jax.nn.logsumexp(logits, axis=1, keepdims=True)) + jnp.exp(
        logits - jax.nn.logsumexp(logits, axis=0, keepdims=True)
    )
    weights = weights - 2.0 * jnp.eye(logits.shape[0], dtype=F32)
    count = text_pool.shape[0]
    start = (lax.axis_index("dp") * 2 + lax.axis_index("mp")) * count
    rows = lax.dynamic_slice_in_dim(weights, start, count, 0)
    columns = lax.dynamic_slice_in_dim(weights, start, count, 1)
    dtext = GRAD_SCALE * jnp.dot(rows, image_all.astype(F32), precision=HIGHEST)
    dimage = GRAD_SCALE * jnp.dot(columns.T, text_all.astype(F32), precision=HIGHEST)
    dtext_raw = unit_back(text_raw, text_inv, dtext)
    dimage_raw = unit_back(image_raw, image_inv, dimage)
    return (
        jnp.dot(text_pool.T, dtext_raw, precision=HIGHEST),
        jnp.dot(image_pool.T, dimage_raw, precision=HIGHEST),
        jnp.dot(dtext_raw, text_embed32.T, precision=HIGHEST),
        jnp.dot(dimage_raw, image_embed32.T, precision=HIGHEST),
    )


FACTOR = 1.0 / math.sqrt(HEAD_DIM)
LOWEST = -1e30
TEXT_PAD = 64
PATCH_PAD = 160
PEER_RING = 3
ARRIVE_RING = 11


def nn(a, b):
    return lax.dot_general(a, b, (((1,), (0,)), ((), ())), preferred_element_type=F32)


def nt(a, b):
    return lax.dot_general(a, b, (((1,), (1,)), ((), ())), preferred_element_type=F32)


def tn(a, b):
    return lax.dot_general(a, b, (((0,), (0,)), ((), ())), preferred_element_type=F32)


def exact(a, b, dims):
    return lax.dot_general(a, b, (dims, ((), ())), precision=HIGHEST, preferred_element_type=F32)


def terms(x):
    high = x.astype(BF16)
    return high, (x - high.astype(F32)).astype(BF16)


def near(a, b, dims):
    def dot(x, y):
        return lax.dot_general(x, y, (dims, ((), ())), preferred_element_type=F32)

    (a_high, a_low), (b_high, b_low) = terms(a), terms(b)
    return dot(a_high, b_high) + (dot(a_high, b_low) + dot(a_low, b_high))


class Blocks:
    def __init__(self):
        self.free, self.top = [], 0

    def take(self, count):
        spare = sorted(self.free)
        for at in spare:
            if all(at + k in spare for k in range(count)):
                for k in range(count):
                    self.free.remove(at + k)
                return at
        at, self.top = self.top, self.top + count
        return at

    def give(self, at, count):
        self.free += range(at, at + count)


def lane_masks(width, split):
    lane = lax.broadcasted_iota(jnp.int32, (1, width), 1)
    left = (lane < split).astype(F32)
    return left, 1.0 - left


def head_pair(x):
    left, right = lane_masks(128, 64)
    return jnp.concatenate([x * left.astype(BF16), x * right.astype(BF16)], 0)


def one_head_each(x):
    half = x.shape[0] // 2
    left = lax.broadcasted_iota(jnp.int32, (half, 128), 1) < 64
    return jnp.where(left, x[:half], x[half:])


def softmax_pair(scores, keys, real):
    lane = lax.broadcasted_iota(jnp.int32, scores.shape, 1)
    left = lane < keys
    within = jnp.where(left, lane, lane - keys)
    scores = jnp.where(within < real, scores * FACTOR, LOWEST)
    top0 = jnp.max(jnp.where(left, scores, LOWEST), 1, keepdims=True)
    top1 = jnp.max(jnp.where(left, LOWEST, scores), 1, keepdims=True)
    expd = jnp.exp(scores - jnp.where(left, top0, top1))
    sum0 = jnp.sum(jnp.where(left, expd, 0.0), 1, keepdims=True)
    sum1 = jnp.sum(jnp.where(left, 0.0, expd), 1, keepdims=True)
    return (expd * jnp.where(left, 1.0 / sum0, 1.0 / sum1)).astype(BF16)


def softmax_pair_back(probs, dprobs, keys):
    left = lax.broadcasted_iota(jnp.int32, dprobs.shape, 1) < keys
    probs = probs.astype(F32)
    both = probs * dprobs
    sum0 = jnp.sum(jnp.where(left, both, 0.0), 1, keepdims=True)
    sum1 = jnp.sum(jnp.where(left, 0.0, both), 1, keepdims=True)
    return (both - probs * jnp.where(left, sum0, sum1)).astype(BF16)


def norm_rows(x):
    centred = x - jnp.mean(x, -1, keepdims=True)
    inv_std = lax.rsqrt(jnp.mean(centred * centred, -1, keepdims=True) + EPS)
    return centred * inv_std, inv_std


class Layer:
    def __init__(self, dims, sizes, refs):
        self.dims, self.sizes = dims, sizes
        self.__dict__.update(refs)
        self.place = Place(dims)
        self.blocks, self.wide = Blocks(), Blocks()
        self.rows = sizes.pairs * TEXT_PAD
        self.patch_rows = sizes.pairs * PATCH_PAD
        self.half = sizes.half
        self.da = None


    def weight(self, slot, h):
        w = self.w[slot][h]
        return w.reshape(-1, w.shape[-1])

    def put_grad(self, slot, h, f, value):
        cut = self.dims[0] // 2
        shape = self.w[slot].shape[2:]
        self.w[slot][h, f * cut : (f + 1) * cut] = value.astype(BF16).reshape(cut, *shape)

    def project(self, at, slot, h):
        w = self.weight(slot, h)
        return nn(self.t[at], w[: self.half]) + nn(self.t[at + 1], w[self.half :])

    def two(self, fn):
        for h in range(2):
            fn(h)

    def text_loop(self, fn):
        def step(p, carry):
            fn(p, pl.ds(pl.multiple_of(p * TEXT_PAD, TEXT_PAD), TEXT_PAD))
            return carry

        lax.fori_loop(0, self.sizes.pairs, step, 0)

    def read_rows(self, at, rows):
        return jnp.concatenate([self.t[at, rows, :], self.t[at + 1, rows, :]], 1)

    def write_rows(self, at, rows, value):
        self.t[at, rows, :] = value[:, : self.half].astype(BF16)
        self.t[at + 1, rows, :] = value[:, self.half :].astype(BF16)


    def own_pairs(self, ref, sem):
        return pltpu.make_async_copy(
            ref.at[pl.ds(self.place.mp * self.sizes.pairs, self.sizes.pairs)], self.joined, sem
        )

    def load(self):
        self.x, self.cot = self.blocks.take(2), self.blocks.take(2)
        for p in range(2):
            self.patch_load(p).start()
        self.own_pairs(self.text_in, self.load_sem.at[0]).start()

    def unpack(self, at):
        gap = jnp.zeros((TEXT_PAD - self.sizes.length, 2 * self.half), F32)
        for p in range(self.sizes.pairs):
            value = jnp.concatenate([self.joined[p].astype(F32), gap], 0)
            self.write_rows(at, pl.ds(p * TEXT_PAD, TEXT_PAD), value)

    def take_text(self):
        self.own_pairs(self.text_in, self.load_sem.at[0]).wait()
        self.unpack(self.x)
        self.own_pairs(self.cot_in, self.load_sem.at[1]).start()

    def patch_load(self, p):
        return pltpu.make_async_copy(self.patches_in.at[p], self.patch_in.at[p % 2], self.patch_sem.at[p % 2])

    def take_patches(self):
        gap = jnp.zeros((PATCH_PAD - self.sizes.patch_count, self.patches.shape[1]), F32)
        for p in range(self.sizes.pairs):
            self.patch_load(p).wait()
            value = jnp.concatenate([self.patch_in[p % 2].astype(F32), gap], 0)
            self.patches[p * PATCH_PAD : (p + 1) * PATCH_PAD, :] = value.astype(BF16)
            if p + 2 < self.sizes.pairs:
                self.patch_load(p + 2).start()

    def take_cotangent(self):
        self.own_pairs(self.cot_in, self.load_sem.at[1]).wait()
        self.unpack(self.cot)

    def own_copies(self, c, name):
        dst = self.w[name].at[(self.place.mp,) + self.place.pos]
        blocks, width = self.sizes.hidden_blocks, self.sizes.embed_half

        def copy(src, dst, sem):
            return pltpu.make_async_copy(src, dst, self.own_sem.at[sem])

        if name == IMAGE:
            return [copy(self.shards[name].at[:, pl.ds(self.place.mp * self.half, self.half)], dst, c)]
        if name == SMALL:
            cols = pl.ds(self.place.mp * width, width)
            refs = self.text_embed, self.image_embed
            spare = FFN + 2 * blocks
            return [
                copy(ref.at[:, cols], dst.at[:, pl.ds(k * width, width)], c if k == 0 else spare)
                for k, ref in enumerate(refs)
            ]
        if name >= FFN:
            ref = self.ffn_in_all if name < FFN + blocks else self.ffn_out_all
            return [copy(ref.at[:, pl.ds((name - FFN) % blocks * self.half, self.half)], dst, c)]
        return [copy(self.shards[name], dst, c)]

    def place_norms(self):
        rows = [ref[...].astype(F32) for ref in self.norm_in.values()]
        rows = jnp.concatenate(rows + [jnp.zeros((8 - len(rows), rows[0].shape[1]), F32)], 0).astype(BF16)
        width = 2 * self.sizes.embed_half
        lane = lax.broadcasted_iota(jnp.int32, (rows.shape[0], self.half - width), 1)
        unit = (lane == lax.broadcasted_iota(jnp.int32, lane.shape, 0)).astype(F32).astype(BF16)
        ref = self.w[SMALL].at[(self.place.mp,) + self.place.pos]
        ref[:, width:] = tn(rows, unit).astype(BF16)

    def image_features(self):
        self.im = self.wide.take(2)
        block = self.patch_rows // 3

        def step(i, carry):
            rows = pl.ds(pl.multiple_of(i * block, block), block)
            left = self.patches[rows, :]
            for h in range(2):
                self.u[self.im + h, rows, :] = nn(left, self.weight(IMAGE, h)).astype(BF16)
            return carry

        lax.fori_loop(0, 3, step, 0)

    def self_projections(self):
        self.q = self.blocks.take(6)
        for k, slot in enumerate((QUERY, KEY, VALUE)):
            self.two(lambda h: self.t.__setitem__(self.q + 2 * k + h, self.project(self.x, slot, h).astype(BF16)))

    def couples(self):
        return [(h, slice(128 * j, 128 * j + 128)) for h in range(2) for j in range(self.half // 128)]

    def put_couples(self, ref, at, rows, values):
        each = len(values) // 2
        for h in range(2):
            ref[at + h, rows, :] = jnp.concatenate(values[h * each : (h + 1) * each], 1)

    def attention(self, p, rows, queries, keys, values, saved, key_pad, real, out):
        scores = jnp.concatenate([nt(q, head_pair(k)) for q, k in zip(queries, keys)], 0)
        probs = softmax_pair(scores, key_pad, real)
        saved[p] = probs
        mixed = [
            nn(probs[TEXT_PAD * i : TEXT_PAD * (i + 1)], head_pair(v)).astype(BF16) for i, v in enumerate(values)
        ]
        self.put_couples(self.t, out, rows, mixed)

    def attention_back(self, p, queries, keys, values, upstream, saved, key_pad):
        probs = saved[p]
        dprobs = jnp.concatenate([nt(d, head_pair(v)) for d, v in zip(upstream, values)], 0)
        dscores = softmax_pair_back(probs, dprobs, key_pad)
        part = [slice(TEXT_PAD * i, TEXT_PAD * (i + 1)) for i in range(len(queries))]
        dqueries = [(nn(dscores[r], head_pair(k)) * FACTOR).astype(BF16) for r, k in zip(part, keys)]
        dkeys = [(one_head_each(tn(dscores[r], q)) * FACTOR).astype(BF16) for r, q in zip(part, queries)]
        dvalues = [one_head_each(tn(probs[r], d)).astype(BF16) for r, d in zip(part, upstream)]
        return dqueries, dkeys, dvalues

    def self_attention(self):
        self.a1 = self.blocks.take(2)

        def pair(p, rows):
            q, k, v = ([self.t[self.q + 2 * m + h, rows, lanes] for h, lanes in self.couples()] for m in range(3))
            self.attention(p, rows, q, k, v, self.p1, TEXT_PAD, self.sizes.length, self.a1)

        self.text_loop(pair)

    def norm_params(self):
        cols = self.weight(SMALL, 0)[:, 2 * self.sizes.embed_half :].astype(F32)
        self.norms[...] = jnp.transpose(cols)[: self.norms.shape[0]]

    def after_branch(self, at, slot, k):
        self.z[...] = nt(self.t[at], self.weight(slot, 0)) + nt(self.t[at + 1], self.weight(slot, 1))
        normed_at, low_at = self.blocks.take(2), self.blocks.take(2)

        def rows_step(p, rows):
            residual = self.read_rows(self.x, rows).astype(F32) if k == 0 else self.hid[rows, :]
            normed, inv_std = norm_rows(residual + self.z[rows, :])
            hidden = normed * self.norms[2 * k : 2 * k + 1, :] + self.norms[2 * k + 1 : 2 * k + 2, :]
            self.hid[rows, :] = hidden
            self.inv[k, rows, :] = inv_std
            self.write_rows(normed_at, rows, normed)
            self.write_rows(low_at, rows, hidden)

        self.text_loop(rows_step)
        return normed_at, low_at

    def turned(self, at):
        out = self.blocks.take(2)
        for h in range(2):
            self.t[out + h] = jnp.transpose(self.t[at + h])
        return out

    def after_self(self):
        self.n1, low = self.after_branch(self.a1, ATTN_OUT, 0)
        self.low1, self.low1_t = low, self.turned(low)

    def cross_keys(self, slot):
        at = self.wide.take(2)
        block = self.patch_rows // 3

        def step(i, carry):
            rows = pl.ds(pl.multiple_of(i * block, block), block)
            for h in range(2):
                w = self.weight(slot, h)
                self.u[at + h, rows, :] = (
                    nn(self.u[self.im, rows, :], w[: self.half]) + nn(self.u[self.im + 1, rows, :], w[self.half :])
                ).astype(BF16)
            return carry

        lax.fori_loop(0, 3, step, 0)
        return at

    def make_keys(self):
        self.k2 = self.cross_keys(CROSS_KEY)

    def make_values(self):
        self.v2 = self.cross_keys(CROSS_VALUE)

    def cross_query(self):
        self.q2 = self.blocks.take(2)
        self.two(lambda h: self.t.__setitem__(self.q2 + h, self.project(self.low1, CROSS_QUERY, h).astype(BF16)))
        self.blocks.give(self.low1, 2)

    def patch_rows_of(self, p):
        return pl.ds(pl.multiple_of(p * PATCH_PAD, PATCH_PAD), PATCH_PAD)

    def cross_attention(self):
        self.a2 = self.blocks.take(2)

        def pair(p, rows):
            keys = self.patch_rows_of(p)
            q = [self.t[self.q2 + h, rows, lanes] for h, lanes in self.couples()]
            k, v = ([self.u[at + h, keys, lanes] for h, lanes in self.couples()] for at in (self.k2, self.v2))
            self.attention(p, rows, q, k, v, self.p2, PATCH_PAD, self.sizes.patch_count, self.a2)

        self.text_loop(pair)

    def after_cross(self):
        self.n2, low = self.after_branch(self.a2, CROSS_OUT, 1)
        self.low2, self.low2_t = low, self.turned(low)
        self.g, self.dg = self.blocks.take(2 * self.sizes.hidden_blocks), self.blocks.take(2 * self.sizes.hidden_blocks)

    def ffn_in(self, k):
        def half(h, carry):
            inner = self.project(self.low2, FFN + k, h)
            cdf = 0.5 * (1.0 + lax.erf(inner * math.sqrt(0.5)))
            pdf = jnp.exp(-0.5 * inner * inner) * (1.0 / math.sqrt(2.0 * math.pi))
            self.t[self.g + 2 * k + h] = (inner * cdf).astype(BF16)
            self.t[self.dg + 2 * k + h] = (cdf + inner * pdf).astype(BF16)
            return carry

        lax.fori_loop(0, 2, half, 0)
        if k == self.sizes.hidden_blocks - 1:
            self.blocks.give(self.low2, 2)

    def ffn_out(self, k):
        def half(h, carry):
            self.hid[...] += nt(self.t[self.g + 2 * k + h], self.weight(FFN + self.sizes.hidden_blocks + k, h))
            return carry

        lax.fori_loop(0, 2, half, 0)


    def pools(self):
        pairs, length, patch_count = self.sizes.pairs, self.sizes.length, self.sizes.patch_count
        self.pool[...] = jnp.zeros_like(self.pool)
        for p in range(pairs):
            rows = pl.ds(p * TEXT_PAD, TEXT_PAD)
            self.pool[0, p : p + 1, :] = jnp.sum(self.read_rows(self.x, rows).astype(F32), 0, keepdims=True) * (1.0 / length)
            keys = pl.ds(p * PATCH_PAD, PATCH_PAD)
            for h in range(2):
                self.pool[1, p : p + 1, h * self.half : (h + 1) * self.half] = jnp.sum(
                    self.u[self.im + h, keys, :].astype(F32), 0, keepdims=True
                ) * (1.0 / patch_count)

    def embed_weight(self, which, h):
        width = self.sizes.embed_half
        return self.weight(SMALL, h)[:, which * width : (which + 1) * width].astype(F32)

    def embed(self):
        width = self.sizes.embed_half
        for which in range(2):
            for h in range(2):
                self.raw[which, :, h * width : (h + 1) * width] = exact(
                    self.pool[which], self.embed_weight(which, h), ((1,), (0,))
                )
            raw = self.raw[which]
            inv = lax.rsqrt(jnp.sum(raw * raw, -1, keepdims=True) + EPS)
            self.own_emb[:, which * 2 * width : (which + 1) * 2 * width] = (raw * inv).astype(BF16)

    def contrast(self):
        width, pairs = self.sizes.embed_half, self.sizes.pairs
        everyone = self.emb[...].reshape(-1, 4 * width)
        count = everyone.shape[0]
        both = everyone[:, : 2 * width], everyone[:, 2 * width :]
        own = self.own_emb[...][:, : 2 * width], self.own_emb[...][:, 2 * width :]
        spot = self.place.pos
        me = self.place.mp * (count // 2) + ((spot[0] * self.dims[1] + spot[1]) * self.dims[2] + spot[2]) * 16
        real_row = (lax.broadcasted_iota(jnp.int32, (1, count), 1) % 16 < pairs).astype(F32)
        real_col = (lax.broadcasted_iota(jnp.int32, (count, 1), 0) % 16 < pairs).astype(F32)
        own_row = (lax.broadcasted_iota(jnp.int32, (16, 1), 0) < pairs).astype(F32)
        match = (
            lax.broadcasted_iota(jnp.int32, (16, count), 1) == lax.broadcasted_iota(jnp.int32, (16, count), 0) + me
        ).astype(F32)
        for which in range(2):
            mine, others = own[which], both[1 - which]
            column_sum = jnp.zeros((1, count), F32)
            for at in range(0, count, 128):
                cross = nt(both[which][at : at + 128], others) * TEMP_INVERSE - TEMP_INVERSE
                column_sum = column_sum + jnp.sum(jnp.exp(cross) * real_col[at : at + 128], 0, keepdims=True)
            logits = nt(mine, others) * TEMP_INVERSE - TEMP_INVERSE
            expd = jnp.exp(logits) * (real_row * own_row)
            row_sum = jnp.sum(expd, 1, keepdims=True) + (1.0 - own_row)
            pull = expd * (1.0 / row_sum) + expd * (1.0 / column_sum) - 2.0 * match * own_row
            upstream = GRAD_SCALE * exact(pull, others.astype(F32), ((1,), (0,)))
            raw = self.raw[which]
            inv = lax.rsqrt(jnp.sum(raw * raw, -1, keepdims=True) + EPS)
            draw = unit_back(raw, inv, upstream)
            scale = 1.0 / (self.sizes.length if which == 0 else self.sizes.patch_count)
            extra = exact(draw[:, :width], self.embed_weight(which, 0), ((1,), (1,))) + exact(
                draw[:, width:], self.embed_weight(which, 1), ((1,), (1,))
            )
            self.extra[which] = extra * scale
            for h in range(2):
                value = exact(self.pool[which], draw[:, h * width : (h + 1) * width], ((0,), (0,)))
                self.put_small(h, which * width, value)


    def region(self):
        pairs, length, patch_count = self.sizes.pairs, self.sizes.length, self.sizes.patch_count
        boxes, listed = self.picks.shape[1:]
        self.chosen[...] = jnp.zeros_like(self.chosen)
        self.span[...] = jnp.zeros_like(self.span)
        for p in range(pairs):
            me = self.place.mp * pairs + p

            def column(ref):
                lane = lax.broadcasted_iota(jnp.int32, ref.shape, 1)
                return jnp.sum(jnp.where(lane == me, ref[...].astype(F32), 0.0), 1, keepdims=True)

            counts, starts, lengths = column(self.counts), column(self.starts), column(self.lengths)
            picks = self.picks[me]
            spot = lax.broadcasted_iota(jnp.int32, (boxes, PATCH_PAD), 1)
            listing = jnp.zeros((boxes, PATCH_PAD), F32)
            for k in range(listed):
                listing = listing + (picks[:, k : k + 1] == spot).astype(F32)
            valid = lax.broadcasted_iota(jnp.int32, (boxes, 1), 0).astype(F32) < counts
            self.chosen[p, :boxes, :] = jnp.where(valid, listing * (1.0 / listed), 0.0)
            token = lax.broadcasted_iota(jnp.int32, (boxes, TEXT_PAD), 1).astype(F32)
            inside = (token >= starts) & (token < starts + lengths) & valid
            self.span[p, :boxes, :] = jnp.where(inside, 1.0 / lengths, 0.0)
            keys = pl.ds(p * PATCH_PAD, PATCH_PAD)
            for h in range(2):
                self.regions[p, :, h * self.half : (h + 1) * self.half] = nn(
                    self.chosen[p].astype(BF16), self.u[self.im + h, keys, :]
                )


    def norm_back(self, k, upstream, normed, inv_std, rows):
        scaled = upstream * self.norms[2 * k : 2 * k + 1, :]
        inner = jnp.mean(scaled * normed, -1, keepdims=True)
        self.norm_grad[2 * k : 2 * k + 1, :] += jnp.sum(upstream * normed, 0, keepdims=True)
        self.norm_grad[2 * k + 1 : 2 * k + 2, :] += jnp.sum(upstream, 0, keepdims=True)
        result = inv_std * (scaled - jnp.mean(scaled, -1, keepdims=True) - normed * inner)
        self.z[rows, :] = result
        self.write_rows(self.db, rows, result)

    def output_and_back(self):
        self.db = self.blocks.take(2)
        self.norm_grad[...] = jnp.zeros_like(self.norm_grad)

        def pair(p, rows):
            normed, inv_std = norm_rows(self.hid[rows, :])
            output = normed * self.norms[4:5, :] + self.norms[5:6, :]
            self.joined[p] = output[: self.sizes.length].astype(BF16)
            mismatch = near(self.span[p], output, ((1,), (0,))) - self.regions[p]
            self.regions[p] = mismatch
            upstream = self.read_rows(self.cot, rows).astype(F32) + near(self.span[p], mismatch, ((0,), (0,)))
            self.norm_back(2, upstream, normed, inv_std, rows)

        self.text_loop(pair)
        self.blocks.give(self.cot, 2)
        self.db_t = self.turned(self.db)

    def grads(self, slot, h, left_t, right):
        for f in range(2):
            self.put_grad(slot, h, f, nn(self.t[left_t + f], right))

    def ffn_out_back(self, k):
        slot = FFN + self.sizes.hidden_blocks + k

        def half(h, carry):
            at = 2 * k + h
            dactive = self.project(self.db, slot, h)
            self.t[self.dg + at] = (dactive * self.t[self.dg + at].astype(F32)).astype(BF16)
            self.grads(slot, h, self.db_t, self.t[self.g + at])
            return carry

        lax.fori_loop(0, 2, half, 0)
        self.blocks.give(self.g + 2 * k, 2)

    def ffn_in_back(self, k):
        slot = FFN + k

        def half(h, carry):
            dinner = self.t[self.dg + 2 * k + h]
            self.z[...] += nt(dinner, self.weight(slot, h))
            self.grads(slot, h, self.low2_t, dinner)
            return carry

        lax.fori_loop(0, 2, half, 0)

    def back_through_norm(self, k):
        normed_at = (self.n1, self.n2)[k]

        def step(p, rows):
            self.norm_back(k, self.z[rows, :], self.read_rows(normed_at, rows).astype(F32), self.inv[k, rows, :], rows)

        self.text_loop(step)
        for h in range(2):
            self.t[self.db_t + h] = jnp.transpose(self.t[self.db + h])

    def branch_back(self, slot, at):
        if self.da is None:
            self.da = self.blocks.take(2)

        def half(h, carry):
            self.t[self.da + h] = self.project(self.db, slot, h).astype(BF16)
            self.grads(slot, h, self.db_t, self.t[at + h])
            return carry

        lax.fori_loop(0, 2, half, 0)

    def cross_attention_back(self):
        def pair(p, rows):
            keys = self.patch_rows_of(p)
            q, d = ([self.t[at + h, rows, lanes] for h, lanes in self.couples()] for at in (self.q2, self.da))
            k, v = ([self.u[at + h, keys, lanes] for h, lanes in self.couples()] for at in (self.k2, self.v2))
            dq, dk, dv = self.attention_back(p, q, k, v, d, self.p2, PATCH_PAD)
            self.put_couples(self.t, self.q2, rows, dq)
            self.put_couples(self.u, self.k2, keys, dk)
            self.put_couples(self.u, self.v2, keys, dv)

        self.text_loop(pair)

    def cross_query_back(self):
        def half(h, carry):
            dq = self.t[self.q2 + h]
            self.z[...] += nt(dq, self.weight(CROSS_QUERY, h))
            self.grads(CROSS_QUERY, h, self.low1_t, dq)
            return carry

        lax.fori_loop(0, 2, half, 0)

    def image_back(self):
        self.dim = self.wide.take(2)
        group = self.sizes.pairs // 2
        block = group * PATCH_PAD

        def step(i, carry):
            rows = pl.ds(pl.multiple_of(i * block, block), block)
            parts = [self.u[at + h, rows, :] for at in (self.k2, self.v2) for h in range(2)]
            for half in range(2):
                cols = slice(half * self.half, (half + 1) * self.half)
                weights = [self.weight(slot, h)[cols] for slot in (CROSS_KEY, CROSS_VALUE) for h in range(2)]
                total = sum(nt(part, weight) for part, weight in zip(parts, weights))
                for k in range(group):
                    p = group * i + k
                    value = total[k * PATCH_PAD : (k + 1) * PATCH_PAD]
                    value = value - sum(tn(self.chosen[p].astype(BF16), m) for m in terms(self.regions[p, :, cols]))
                    value = value + self.extra[1, pl.ds(p, 1), cols]
                    self.u[self.dim + half, self.patch_rows_of(p), :] = value.astype(BF16)
            return carry

        lax.fori_loop(0, 2, step, 0)

    def cross_key_back(self, slot, at):
        for f in range(2):

            def half(h, carry):
                self.put_grad(slot, h, f, tn(self.u[self.im + f], self.u[at + h]))
                return carry

            lax.fori_loop(0, 2, half, 0)

    def patch_back(self):
        group, patch_count = self.sizes.pairs // 2, self.sizes.patch_count
        width = self.patch_stage.shape[-1]
        steps = [(n, g) for n in range(self.patches.shape[1] // width) for g in range(2)]

        def out(i):
            n, g = steps[i]
            dst = self.patch_grad.at[pl.ds(g * group, group), :, pl.ds(n * width, width)]
            return pltpu.make_async_copy(self.patch_stage.at[i % 2], dst, self.patch_sem.at[i % 2])

        for i, (n, g) in enumerate(steps):
            if i >= 2:
                out(i - 2).wait()
            rows, cols = pl.ds(g * group * PATCH_PAD, group * PATCH_PAD), slice(n * width, (n + 1) * width)
            value = nt(self.u[self.dim, rows, :], self.weight(IMAGE, 0)[cols])
            value = value + nt(self.u[self.dim + 1, rows, :], self.weight(IMAGE, 1)[cols])
            for k in range(group):
                self.patch_stage[i % 2, k] = value[k * PATCH_PAD : k * PATCH_PAD + patch_count]
            out(i).start()
        for i in range(len(steps) - 2, len(steps)):
            out(i).wait()

    def image_weight_back(self):
        cut = self.dims[0] // 2
        shape = self.w[IMAGE].shape[2:]
        half_depth = self.patches.shape[1] // 2
        for f in range(2):

            def half(h, carry):
                value = tn(self.patches[:, f * half_depth : (f + 1) * half_depth], self.u[self.dim + h])
                self.w[IMAGE][h, f * cut : (f + 1) * cut] = value.astype(BF16).reshape(cut, *shape)
                return carry

            lax.fori_loop(0, 2, half, 0)

    def put_small(self, h, start, value):
        ref = self.w[SMALL]
        ref[h, :, :, :, :, start : start + value.shape[1]] = value.astype(BF16).reshape(
            *ref.shape[1:-1], value.shape[1]
        )

    def small_grads(self):
        rows = jnp.concatenate([self.norm_grad[...], jnp.zeros((128 - self.norm_grad.shape[0], 2 * self.half), F32)], 0)
        columns = jnp.transpose(rows)
        for h in range(2):
            self.put_small(h, 2 * self.sizes.embed_half, columns)

    def self_attention_back(self):
        def pair(p, rows):
            q, k, v = ([self.t[self.q + 2 * m + h, rows, lanes] for h, lanes in self.couples()] for m in range(3))
            d = [self.t[self.da + h, rows, lanes] for h, lanes in self.couples()]
            for m, values in enumerate(self.attention_back(p, q, k, v, d, self.p1, TEXT_PAD)):
                self.put_couples(self.t, self.q + 2 * m, rows, values)

        self.text_loop(pair)
        for h in range(2):
            self.t[self.db_t + h] = jnp.transpose(self.t[self.x + h])

    def self_projection_back(self, k):
        slot = (QUERY, KEY, VALUE)[k]

        def half(h, carry):
            d = self.t[self.q + 2 * k + h]
            self.z[...] += nt(d, self.weight(slot, h))
            self.grads(slot, h, self.db_t, d)
            return carry

        lax.fori_loop(0, 2, half, 0)

    def text_out(self):
        def moves(p):
            src, dst = self.text_stage.at[p % 2], self.text_out_ref.at[self.place.mp, p]
            own = pltpu.make_async_copy(src, dst, self.text_own.at[p])
            return own, remote(src, dst, self.text_send.at[p], self.text_recv.at[p], self.place.peer())

        def done(p):
            own, give = moves(p)
            own.wait()
            give.wait_send()

        pairs = self.sizes.pairs
        for p in range(pairs):
            if p >= 2:
                done(p - 2)
            rows = pl.ds(p * TEXT_PAD, TEXT_PAD)
            value = self.z[rows, :] + self.extra[0, p : p + 1, :]
            self.text_stage[p % 2] = value[: self.sizes.length]
            for move in moves(p):
                move.start()

        def end():
            for p in range(max(pairs - 2, 0), pairs):
                done(p)
            for p in range(pairs):
                moves(p)[1].wait_recv()

        self.ends.append(end)


    def gather_to_peer(self, c, name, order, buf):
        mine, other = buf.at[self.place.mp], buf.at[1 - self.place.mp]
        sent = yield from gather_steps(self.place, order, mine, self.g_send.at[c], self.g_recv.at[c])

        def copy(ref):
            return remote(ref, ref, self.gp_send.at[c], self.gp_recv.at[c], self.place.peer())

        copy(mine).start()
        yield
        copy(other).wait_recv()
        self.sending[name] = sent + [(None, lambda: copy(mine))]

    def gather(self, c, name, order):
        buf = self.w[name]
        for copy in self.own_copies(c, name):
            copy.start()
        if name == SMALL:
            self.place_norms()
        yield
        for copy in self.own_copies(c, name):
            copy.wait()
        yield from self.gather_to_peer(c, name, order, buf)

    def gather_embeddings(self, c, order):
        self.emb[(self.place.mp,) + self.place.pos] = self.own_emb[...]
        yield from self.gather_to_peer(c, EMBEDDINGS, order, self.emb)

    def settle(self, names):
        for name in names:
            wait_sent(self.sending.pop(name))

    def credit(self, slot, give):
        place = self.place

        def act(index, device):
            sem = self.credits.at[slot, index]
            if give:
                pl.semaphore_signal(sem, inc=1, device_id=device, device_id_type=MESH)
            else:
                pl.semaphore_wait(sem, 1)

        for axis in range(3):
            length, pos = place.dims[axis], place.pos[axis]
            if length > 1:
                pl.when(pos > 0)(lambda: act(2 * axis + (1 if give else 0), place.at(axis, pos - 1)))
                pl.when(pos < length - 1)(lambda: act(2 * axis + (0 if give else 1), place.at(axis, pos + 1)))

    def peer_credit(self, slot, give):
        sem = self.peer_credits.at[slot]
        if give:
            pl.semaphore_signal(sem, inc=1, device_id=self.place.peer(), device_id_type=MESH)
        else:
            pl.semaphore_wait(sem, 1)

    def image_credit(self):
        self.credit(ARRIVE_RING, True)
        self.peer_credit(PEER_RING, True)

    def spare(self, at, units, rows):
        blocks = self.u.at[pl.ds(at, 2)].reshape(-1, rows, self.half)
        return blocks.at[pl.ds(0, units)]

    def scatter(self, c, turn, name, order, total):
        buf, ringed = self.w[name], name != IMAGE
        mine, other = buf.at[self.place.mp], buf.at[1 - self.place.mp]
        if ringed:
            peer_slot, slot = turn % PEER_RING, turn % ARRIVE_RING
            peer_in, arrive = self.peer_in.at[peer_slot], self.arrive.at[slot]
        else:
            peer_slot, slot = PEER_RING, ARRIVE_RING
            peer_in = self.spare(0, math.prod(self.dims), buf.shape[-2]).reshape(*buf.shape[1:])
            arrive = self.spare(2, arrive_units(self.dims, order), buf.shape[-2])

        def copy():
            return remote(other, peer_in, self.sp_send.at[peer_slot], self.sp_recv.at[peer_slot], self.place.peer())

        if not ringed or turn >= PEER_RING:
            self.peer_credit(peer_slot, False)
        wait_sent(self.peer_sent.pop(peer_slot, ()))
        copy().start()
        self.peer_sent[peer_slot] = [(None, copy)]
        yield
        copy().wait_recv()
        mine[...] = mine[...] + peer_in[...]
        if ringed and turn + PEER_RING < total:
            self.peer_credit(peer_slot, True)
        if not ringed or turn >= ARRIVE_RING:
            self.credit(slot, False)
        wait_sent(self.ring_sent.pop(slot, ()))
        result = self.results[name]
        target = result.at[self.place.mp] if len(result.shape) == 3 else result
        sent = yield from scatter_steps(
            self.place, order, mine, arrive, self.s_send.at[slot], self.s_recv.at[slot], target
        )
        if ringed and turn + ARRIVE_RING < total:
            self.credit(slot, True)
        self.ring_sent[slot] = sent
        if len(result.shape) == 3:

            def hand(half):
                ref = result.at[half]
                return remote(ref, ref, self.h_send.at[int(name == IMAGE)], self.h_recv.at[int(name == IMAGE)], self.place.peer())

            hand(self.place.mp).start()
            yield
            hand(1 - self.place.mp).wait_recv()
            self.sent.append((None, lambda: hand(self.place.mp)))

    def joined_over(self):
        stage, whole = self.joined, self.joined_out
        own = pltpu.make_async_copy(stage, whole.at[self.place.mp], self.out_own)
        give = remote(stage, whole.at[self.place.mp], self.out_send, self.out_recv, self.place.peer())
        own.start()
        give.start()
        self.ends += [own.wait, give.wait]


IMAGE, QUERY, KEY, VALUE, SMALL, ATTN_OUT, CROSS_KEY, CROSS_VALUE, CROSS_QUERY, CROSS_OUT, FFN = range(11)
EMBEDDINGS = -1


def grad_order(hidden_blocks):
    ffn = (*range(FFN + hidden_blocks, FFN + 2 * hidden_blocks), *range(FFN, FFN + hidden_blocks))
    return ffn + (CROSS_OUT, CROSS_QUERY, CROSS_KEY, CROSS_VALUE, IMAGE, ATTN_OUT, SMALL, QUERY, KEY, VALUE)


class Timeline:
    def __init__(self):
        self.events = []

    def add(self, time, fn):
        self.events.append((time, len(self.events), fn))

    def add_steps(self, times, steps):
        last = [False]

        def advance():
            if not last[0]:
                try:
                    next(steps)
                except StopIteration:
                    last[0] = True

        for time in times:
            self.add(time, advance)

    def run(self):
        for _, _, fn in sorted(self.events, key=lambda e: e[:2]):
            fn()


CHUNK = 3.9
KINDS = ((2, 0, 1), (1, 0, 2), (0, 2, 1), (0, 1, 2), (2, 1, 0), (1, 2, 0))

GATHER_KINDS = (2, 1, 2, 1, 3, 2, 1, 0, 0, 3, 2, 1, 0, 1, 2, 3, 0, 1)
GATHER_START = (0.0, 35.78, 9.14, 7.29, 8.49, 34.08, 32.19, 18.67, 13.4, 23.56, 64.34, 62.53, 73.03, 62.92, 87.05, 47.64, 73.57, 73.11)
GATHER_STEPS = (
    (0.0, 9.86, 19.46, 20.54, 44.84, 69.22, 77.55),
    (0.0, 9.5, 18.16, 25.51, 36.27, 56.29, 63.23),
    (0.0, 4.91, 13.38, 28.77, 37.2, 65.33, 87.19),
    (0.0, 20.6, 34.85, 38.31, 50.92, 77.49, 86.82),
    (0.0, 2.0, 14.0, 20.51, 31.8, 45.01, 50.55),
    (0.0, 10.96, 15.65, 18.67, 37.8, 45.42, 88.59),
    (0.0, 36.34, 39.98, 42.92, 45.73, 67.89, 69.96),
    (0.0, 12.35, 52.03, 62.19, 68.96, 91.36, 91.73),
    (0.0, 48.13, 60.52, 77.82, 83.43, 113.81, 119.75),
    (0.0, 26.68, 32.47, 48.62, 62.07, 91.48, 127.96),
    (0.0, 12.23, 15.22, 26.74, 57.19, 75.56, 109.53),
    (0.0, 20.34, 32.76, 43.48, 47.67, 108.99, 138.63),
    (0.0, 20.85, 35.36, 60.72, 72.87, 115.45, 141.33),
    (0.0, 26.1, 44.43, 60.04, 73.87, 147.49, 156.02),
    (0.0, 9.02, 14.88, 21.06, 39.31, 105.07, 131.21),
    (0.0, 6.63, 26.12, 35.19, 66.26, 164.18, 194.81),
    (0.0, 37.17, 73.98, 78.09, 99.34, 152.56, 170.68),
    (0.0, 30.29, 50.44, 98.38, 99.94, 169.35, 241.95),
)
EMBED_STEPS = (0.0, 8.91, 16.59, 27.36, 29.51, 45.31, 65.65)
SCATTER_KINDS = (0, 1, 0, 1, 3, 2, 3, 2, 1, 3, 0, 0, 1, 2, 1, 2, 2, 3)
SCATTER_GAPS = (191.0, 0.0, 5.73, 2.04, 0.46, 0.0, 7.0, 4.69, 0.0, 4.57, 0.08, 3.68, 7.84, 0.0, 3.15, 0.0, 21.45, 10.42)
SCATTER_STEPS = (
    (0.0, 4.04, 12.95, 23.87, 32.6, 36.14, 42.79),
    (0.0, 3.0, 16.04, 20.81, 25.89, 31.51, 36.95),
    (0.0, 1.97, 9.58, 17.57, 26.02, 34.36, 45.87),
    (0.0, 1.34, 11.81, 18.03, 25.35, 32.29, 46.72),
    (0.0, 5.46, 23.87, 29.46, 35.73, 45.62, 73.83),
    (0.0, 4.56, 17.74, 24.03, 29.36, 35.29, 63.7),
    (0.0, 5.03, 14.62, 19.72, 24.8, 28.81, 109.64),
    (0.0, 2.85, 10.48, 21.98, 25.03, 54.32, 92.15),
    (0.0, 6.97, 13.67, 20.43, 25.72, 77.02, 206.52),
    (0.0, 12.41, 21.43, 58.18, 71.76, 81.1, 168.25),
    (0.0, 3.91, 15.0, 16.25, 21.35, 24.72, 121.97),
    (0.0, 8.0, 14.81, 21.25, 76.96, 144.83, 236.56),
    (0.0, 2.83, 11.79, 24.73, 61.73, 150.58, 197.54),
    (0.0, 2.49, 11.12, 55.01, 102.76, 109.24, 203.32),
    (0.0, 3.22, 41.46, 48.01, 73.25, 126.87, 208.6),
    (0.0, 3.06, 48.3, 102.56, 113.82, 171.84, 210.86),
    (0.0, 19.43, 79.99, 83.8, 142.14, 167.44, 256.6),
    (0.0, 1.16, 68.62, 72.95, 111.24, 153.3, 212.93),
)
PACE = 1.058


class Plan:
    def __init__(self, dims, count):
        self.dims = dims
        self.tabled = dims == (4, 2, 2) and count == len(GATHER_START)
        self.gather_kinds = GATHER_KINDS if self.tabled else [k % 2 for k in range(count)]
        self.scatter_kinds = SCATTER_KINDS if self.tabled else [k % 2 for k in range(count)]
        self.gaps = SCATTER_GAPS if self.tabled else [CHUNK] * count
        self.pace = PACE if self.tabled else 1.0

    def steps(self, order, back):
        units = [math.prod(self.dims[a] for a in order[:k]) for k in range(3) for _ in range(self.dims[order[k]] - 1)]
        times = [0.0, 3.0] if back else [0.0]
        for unit in reversed(units) if back else units:
            times.append(times[-1] + 1.6 * unit + 3.0)
        return times if back else times + [times[-1] + 4.0]

    def gather(self, c):
        kind = self.gather_kinds[c]
        if self.tabled:
            return KINDS[kind], [GATHER_START[c] + t for t in GATHER_STEPS[c]]
        return KINDS[kind], [CHUNK * c + t for t in self.steps(KINDS[kind], False)]

    def scatter(self, c):
        kind = self.scatter_kinds[c]
        return KINDS[kind], SCATTER_STEPS[c] if self.tabled else self.steps(KINDS[kind], True)

    def embeddings(self, start):
        order = (2, 1, 0)
        return order, [start + t for t in (EMBED_STEPS if self.tabled else self.steps(order, False))]


def fused_kernel(dims, sizes, refs):
    layer = Layer(dims, sizes, refs)
    blocks = sizes.hidden_blocks
    layer.sent, layer.ends, layer.sending, layer.ring_sent, layer.peer_sent = [], [], {}, {}, {}
    timeline = Timeline()

    layer.load()
    layer.own_emb[...] = jnp.zeros_like(layer.own_emb)
    ready = {}
    plan = Plan(dims, FFN + 2 * blocks)
    for c, name in enumerate(range(FFN + 2 * blocks)):
        order, times = plan.gather(c)
        timeline.add_steps([-1.0] + times, layer.gather(c, name, order))
        ready[name] = times[-1]
    timeline.add(-0.5, lambda: greet_lines(layer.place))

    clock = [0.0]

    def compute(fn, cost, *needs):
        clock[0] = max([clock[0] + 0.001] + [ready[n] + 0.01 for n in needs])
        timeline.add(clock[0], fn)
        clock[0] += cost * plan.pace
        return clock[0]

    compute(layer.take_patches, 3.0)
    compute(layer.take_text, 0.5)
    compute(layer.image_features, 1.6, IMAGE)
    compute(layer.region, 0.8)
    compute(layer.take_cotangent, 0.5)
    compute(layer.self_projections, 2.0, QUERY, KEY, VALUE)
    compute(layer.self_attention, 4.0)
    compute(layer.norm_params, 0.2, SMALL)
    compute(layer.pools, 0.3)
    start = compute(layer.embed, 0.3)
    order, times = plan.embeddings(start)
    timeline.add_steps(times, layer.gather_embeddings(len(ready), order))
    ready[EMBEDDINGS] = times[-1]
    compute(layer.after_self, 2.7, ATTN_OUT)
    compute(layer.make_keys, 2.3, CROSS_KEY)
    compute(layer.make_values, 2.3, CROSS_VALUE)
    compute(layer.cross_query, 0.6, CROSS_QUERY)
    compute(layer.cross_attention, 4.5)
    compute(layer.after_cross, 2.0, CROSS_OUT)
    compute(lambda: layer.settle([SMALL]), 0.0, EMBEDDINGS)
    compute(layer.contrast, 4.0)
    for k in range(blocks):
        compute(functools.partial(layer.ffn_in, k), 1.6, FFN + k)
    for k in range(blocks):
        compute(functools.partial(layer.ffn_out, k), 1.0, FFN + blocks + k)

    done = {}
    compute(layer.output_and_back, 4.0)
    compute(lambda: layer.settle(list(layer.sending)), 0.0)
    compute(layer.joined_over, 0.1)
    for k in range(blocks):
        done[FFN + blocks + k] = compute(functools.partial(layer.ffn_out_back, k), 2.2)
    for k in range(blocks):
        done[FFN + k] = compute(functools.partial(layer.ffn_in_back, k), 1.9)
    compute(functools.partial(layer.back_through_norm, 1), 1.8)
    done[CROSS_OUT] = compute(lambda: layer.branch_back(CROSS_OUT, layer.a2), 1.8)
    compute(layer.cross_attention_back, 5.0)
    done[CROSS_QUERY] = compute(layer.cross_query_back, 1.5)
    compute(layer.image_back, 5.0)
    done[CROSS_KEY] = compute(lambda: layer.cross_key_back(CROSS_KEY, layer.k2), 2.4)
    done[CROSS_VALUE] = compute(lambda: layer.cross_key_back(CROSS_VALUE, layer.v2), 2.4)
    compute(layer.patch_back, 5.5)
    done[IMAGE] = compute(layer.image_weight_back, 2.3)
    compute(layer.image_credit, 0.1)
    compute(functools.partial(layer.back_through_norm, 0), 1.8)
    done[ATTN_OUT] = compute(lambda: layer.branch_back(ATTN_OUT, layer.a1), 1.8)
    done[SMALL] = compute(layer.small_grads, 0.5)
    compute(layer.self_attention_back, 5.0)
    for k, name in enumerate((QUERY, KEY, VALUE)):
        done[name] = compute(functools.partial(layer.self_projection_back, k), 1.5)
    compute(layer.text_out, 2.0)

    start, ends, peer_ends = 0.0, [], []
    for c, name in enumerate(grad_order(blocks)):
        order, steps = plan.scatter(c)
        start = max(start + plan.gaps[c], done[name])
        if name != IMAGE and len(ends) >= PEER_RING:
            start = max(start, peer_ends[len(ends) - PEER_RING] + 0.1)
        if name != IMAGE and len(ends) >= ARRIVE_RING:
            start = max(start, ends[len(ends) - ARRIVE_RING] + 0.1 - steps[1])
        times = [start + 0.02 + t for t in steps]
        if name in (IMAGE, SMALL):
            times.append(times[-1] + 3.0)
        timeline.add_steps(times, layer.scatter(c, len(ends), name, order, sizes.ring_total))
        if name != IMAGE:
            peer_ends.append(times[1])
            ends.append(times[len(steps) - 1])
    timeline.run()
    assert not layer.sending
    for end in layer.ends:
        end()
    for sent in (layer.sent, *layer.ring_sent.values(), *layer.peer_sent.values()):
        wait_sent(sent)
    assert layer.blocks.top <= layer.t.shape[0], layer.blocks.top
    assert layer.wide.top <= layer.u.shape[0], layer.wide.top


def fused_body(
    text,
    patches,
    cotangent,
    region_counts,
    phrase_starts,
    phrase_lengths,
    box_patches,
    query_weight,
    key_weight,
    value_weight,
    attn_out_weight,
    cross_query_weight,
    cross_key_weight,
    cross_value_weight,
    cross_out_weight,
    image_weight,
    ffn_in_weight,
    ffn_out_weight,
    text_embed_weight,
    image_embed_weight,
    *norm_shards,
):
    dims = split_dims(lax.axis_size("dp"))
    mp = lax.axis_index("mp")
    pairs, patch_count, depth = patches.shape
    length, model_width = text.shape[1:]
    half = query_weight.shape[1]
    rows = query_weight.shape[0]
    hidden_blocks = ffn_in_weight.shape[1] // half
    embed_half = text_embed_weight.shape[1] // 2

    slot = jax.ShapeDtypeStruct((rows, half), BF16)
    shards = {name: slot for name in range(FFN + 2 * hidden_blocks)}
    shards[IMAGE] = jax.ShapeDtypeStruct((image_weight.shape[0], half), BF16)
    whole = {
        IMAGE: image_weight,
        QUERY: query_weight,
        KEY: key_weight,
        VALUE: value_weight,
        ATTN_OUT: attn_out_weight.T,
        CROSS_KEY: cross_key_weight,
        CROSS_VALUE: cross_value_weight,
        CROSS_QUERY: cross_query_weight,
        CROSS_OUT: cross_out_weight.T,
    }
    order = range(FFN + 2 * hidden_blocks)
    sizes = types.SimpleNamespace(
        pairs=pairs,
        length=length,
        patch_count=patch_count,
        half=half,
        hidden_blocks=hidden_blocks,
        embed_half=embed_half,
        ring_total=len(order) - 1,
    )
    count, text_rows, patch_rows = len(order), pairs * TEXT_PAD, pairs * PATCH_PAD
    couples = model_width // 128
    anywhere, vmem = pl.BlockSpec(memory_space=pl.ANY), pl.BlockSpec(memory_space=pltpu.VMEM)

    inputs = dict(
        text_in=(text, anywhere),
        cot_in=(cotangent, anywhere),
        patches_in=(patches, anywhere),
        ffn_in_all=(ffn_in_weight, anywhere),
        ffn_out_all=(ffn_out_weight.T, anywhere),
        text_embed=(text_embed_weight, anywhere),
        image_embed=(image_embed_weight, anywhere),
        counts=(region_counts.reshape(1, -1), vmem),
        starts=(phrase_starts.T, vmem),
        lengths=(phrase_lengths.T, vmem),
        picks=(box_patches, vmem),
    )
    outputs = dict(
        joined_out=(jax.ShapeDtypeStruct((2, pairs, length, model_width), BF16), anywhere),
        text_out_ref=(jax.ShapeDtypeStruct((2, pairs, length, model_width), F32), anywhere),
        patch_grad=(jax.ShapeDtypeStruct((pairs, patch_count, depth), F32), anywhere),
    )
    result_shapes = []
    for name in order:
        shape = shards[name].shape
        result_shapes.append(jax.ShapeDtypeStruct(((2,) if name in (IMAGE, SMALL) else ()) + shape, F32))
    units = max(arrive_units(dims, o) for o in KINDS[:4])
    dma, regular = pltpu.SemaphoreType.DMA, pltpu.SemaphoreType.REGULAR
    scratch = dict(
        t=pltpu.VMEM((42, text_rows, half), BF16),
        u=pltpu.VMEM((8, patch_rows, half), BF16),
        patches=pltpu.VMEM((patch_rows, depth), BF16),
        p1=pltpu.VMEM((pairs, couples * TEXT_PAD, 2 * TEXT_PAD), BF16),
        p2=pltpu.VMEM((pairs, couples * TEXT_PAD, 2 * PATCH_PAD), BF16),
        z=pltpu.VMEM((text_rows, model_width), F32),
        hid=pltpu.VMEM((text_rows, model_width), F32),
        inv=pltpu.VMEM((2, text_rows, 1), F32),
        norms=pltpu.VMEM((8, model_width), F32),
        norm_grad=pltpu.VMEM((8, model_width), F32),
        pool=pltpu.VMEM((2, 16, model_width), F32),
        raw=pltpu.VMEM((2, 16, 2 * embed_half), F32),
        own_emb=pltpu.VMEM((16, 4 * embed_half), BF16),
        emb=pltpu.VMEM((2,) + dims + (16, 4 * embed_half), BF16),
        extra=pltpu.VMEM((2, 16, model_width), F32),
        chosen=pltpu.VMEM((pairs, 8, PATCH_PAD), F32),
        span=pltpu.VMEM((pairs, 8, TEXT_PAD), F32),
        regions=pltpu.VMEM((pairs, 8, model_width), F32),
        joined=pltpu.VMEM((pairs, length, model_width), BF16),
        text_stage=pltpu.VMEM((2, length, model_width), F32),
        patch_in=pltpu.VMEM((2, patch_count, depth), BF16),
        patch_stage=pltpu.VMEM((2, pairs // 2, patch_count, 256), F32),
        peer_in=pltpu.VMEM((PEER_RING,) + dims + (rows, half), BF16),
        arrive=pltpu.VMEM((ARRIVE_RING, units, rows, half), BF16),
        load_sem=dma((2,)),
        own_sem=dma((count + 1,)),
        g_send=dma((count + 1, send_slots(dims))),
        g_recv=dma((count + 1, gather_slots(dims))),
        gp_send=dma((count + 1,)),
        gp_recv=dma((count + 1,)),
        s_send=dma((ARRIVE_RING + 1, send_slots(dims))),
        s_recv=dma((ARRIVE_RING + 1, sum_slots(dims))),
        sp_send=dma((PEER_RING + 1,)),
        sp_recv=dma((PEER_RING + 1,)),
        h_send=dma((2,)),
        h_recv=dma((2,)),
        out_own=dma,
        out_send=dma,
        out_recv=dma,
        text_own=dma((pairs,)),
        text_send=dma((pairs,)),
        text_recv=dma((pairs,)),
        patch_sem=dma((2,)),
        credits=regular((ARRIVE_RING + 1, 6)),
        peer_credits=regular((PEER_RING + 1,)),
    )
    weights = [pltpu.VMEM((2,) + dims + shards[name].shape, BF16) for name in order]

    def kernel(*refs):
        refs = list(refs)

        def some(names):
            part = dict(zip(names, refs))
            del refs[: len(part)]
            return part

        table = some(inputs)
        table.update(norm_in=some(range(len(norm_shards))))
        table.update(shards=some(whole))
        table.update(some(outputs))
        table.update(results=some(order))
        table.update(some(scratch))
        table.update(w=some(order))
        fused_kernel(dims, sizes, table)

    results = pl.pallas_call(
        kernel,
        out_shape=[s for s, _ in outputs.values()] + result_shapes,
        in_specs=[spec for _, spec in inputs.values()] + [vmem] * len(norm_shards) + [anywhere] * len(whole),
        out_specs=[spec for _, spec in outputs.values()] + [vmem] * count,
        scratch_shapes=list(scratch.values()) + weights,
        compiler_params=pltpu.CompilerParams(
            collective_id=2, has_side_effects=True, vmem_limit_bytes=64 * 2**20
        ),
        name="layer",
    )(*[x for x, _ in inputs.values()], *[n.reshape(1, -1) for n in norm_shards], *whole.values())
    return finish(results, sizes, dims, model_width)


def finish_kernel(sizes, count, joined, text_grad, patch_grad, *refs):
    blocks, half, width = sizes.hidden_blocks, sizes.half, sizes.embed_half
    own, small = refs[:count], refs[SMALL]
    outs, (stage_joined, stage_text, stage_patch, in_sem, out_sem) = refs[count:-5], refs[-5:]
    pieces = []
    for src, stage, dst in ((joined, stage_joined, outs[0]), (text_grad, stage_text, outs[1])):
        pieces += [(src.at[k], stage.at[k], dst.at[k]) for k in range(2)]
    pieces += [(patch_grad.at[p], stage_patch.at[p], outs[2].at[p]) for p in range(sizes.pairs)]
    into = [pltpu.make_async_copy(src, stage, in_sem.at[k]) for k, (src, stage, _) in enumerate(pieces)]
    back = [pltpu.make_async_copy(stage, dst, out_sem.at[k]) for k, (_, stage, dst) in enumerate(pieces)]
    for copy in into:
        copy.start()
    for first, second in zip(into, back):
        first.wait()
        second.start()
    for k in range(2):
        outs[11][:, k * half : (k + 1) * half] = own[IMAGE][k]
        for j in range(2):
            outs[14 + j][:, k * width : (k + 1) * width] = small[k, :, j * width : (j + 1) * width]
    singles = (QUERY, KEY, VALUE, ATTN_OUT, CROSS_QUERY, CROSS_KEY, CROSS_VALUE, CROSS_OUT)
    for k, name in enumerate(singles):
        outs[3 + k][...] = own[name][...]
    for k in range(blocks):
        cols = slice(k * half, (k + 1) * half)
        outs[12][:, cols] = own[FFN + k][...]
        outs[13][:, cols] = own[FFN + blocks + k][...]
    rows = jnp.transpose(small[lax.axis_index("mp")][:, 2 * width :])
    for k in range(6):
        outs[16 + k][...] = rows[k : k + 1]
    for copy in back:
        copy.wait()


def finish(results, sizes, dims, model_width):
    anywhere, vmem = pl.BlockSpec(memory_space=pl.ANY), pl.BlockSpec(memory_space=pltpu.VMEM)
    own = results[3:]
    rows, half, width, blocks = own[QUERY].shape[0], sizes.half, sizes.embed_half, sizes.hidden_blocks
    shapes = [r.shape for r in results[:3]] + [(rows, half)] * 8
    shapes += [(own[IMAGE].shape[1], 2 * half)] + [(rows, blocks * half)] * 2 + [(rows, 2 * width)] * 2 + [(1, rows)] * 6
    types = [BF16] + [F32] * (len(shapes) - 1)
    outs = pl.pallas_call(
        functools.partial(finish_kernel, sizes, len(own)),
        out_shape=[jax.ShapeDtypeStruct(s, t) for s, t in zip(shapes, types)],
        in_specs=[anywhere] * 3 + [vmem] * len(own),
        out_specs=[anywhere] * 3 + [vmem] * 19,
        scratch_shapes=[pltpu.VMEM(r.shape, r.dtype) for r in results[:3]]
        + [pltpu.SemaphoreType.DMA((4 + sizes.pairs,))] * 2,
        compiler_params=pltpu.CompilerParams(vmem_limit_bytes=60 * 2**20),
        name="results",
    )(*results)
    whole = (2 * sizes.pairs, sizes.length, model_width)
    turned = (6, 10, 13)
    done = [outs[0].reshape(whole), outs[1].reshape(whole), *outs[2:16]]
    done = [x.T if k in turned else x for k, x in enumerate(done)]
    return (*done, *(x.reshape(-1) for x in outs[16:]))


def pad_rows(x, rows):
    return jnp.pad(x, ((0, rows - x.shape[0]), (0, 0)))


def body(
    text,
    patches,
    cotangent,
    region_counts,
    phrase_starts,
    phrase_lengths,
    box_patches,
    query_weight,
    key_weight,
    value_weight,
    attn_out_weight,
    cross_query_weight,
    cross_key_weight,
    cross_value_weight,
    cross_out_weight,
    image_weight,
    ffn_in_weight,
    ffn_out_weight,
    text_embed_weight,
    image_embed_weight,
    *norm_shards,
):
    dp = lax.axis_size("dp")
    dims = split_dims(dp)
    mp = lax.axis_index("mp")
    half_pairs, patch_count, _ = patches.shape
    length, model_width = text.shape[1:]
    half = query_weight.shape[1]
    rows = query_weight.shape[0]
    hidden_blocks = ffn_in_weight.shape[1] // half
    embed_half = text_embed_weight.shape[1] // 2
    image_rows_own = image_weight.shape[0]

    if rows % 16 == 0 and dims[0] % 2 == 0 and half % 128 == 0 and half == model_width // 2 and half_pairs % 2 == 0:
        return fused_body(
            text, patches, cotangent, region_counts, phrase_starts, phrase_lengths, box_patches,
            query_weight, key_weight, value_weight, attn_out_weight, cross_query_weight, cross_key_weight,
            cross_value_weight, cross_out_weight, image_weight, ffn_in_weight, ffn_out_weight,
            text_embed_weight, image_embed_weight, *norm_shards,
        )

    def own_half(x, size, dim):
        return lax.dynamic_slice_in_dim(x, mp * size, size, dim)

    text, cotangent = own_half(text, half_pairs, 0), own_half(cotangent, half_pairs, 0)
    region_counts, phrase_starts = own_half(region_counts, half_pairs, 0), own_half(phrase_starts, half_pairs, 0)
    phrase_lengths, box_patches = own_half(phrase_lengths, half_pairs, 0), own_half(box_patches, half_pairs, 0)

    padded = -(-rows // 16) * 16
    small = jnp.concatenate(
        [own_half(text_embed_weight, embed_half, 1), own_half(image_embed_weight, embed_half, 1)]
        + [jnp.pad(jnp.stack(norm_shards, 1), ((0, 0), (0, half - 2 * embed_half - len(norm_shards))))],
        1,
    )
    ffn_out_t = ffn_out_weight.T
    shards = [
        own_half(image_weight, half, 1),
        query_weight,
        key_weight,
        value_weight,
        attn_out_weight.T,
        small,
        cross_key_weight,
        cross_value_weight,
        cross_query_weight,
        cross_out_weight.T,
        *(ffn_in_weight[:, k * half : (k + 1) * half] for k in range(hidden_blocks)),
        *(ffn_out_t[:, k * half : (k + 1) * half] for k in range(hidden_blocks)),
    ]
    real = [s.shape[0] for s in shards]
    shards = [pad_rows(s, -(-s.shape[0] // 16) * 16) for s in shards]
    gathered = gather(shards, dims)

    def merge(g, n):
        g = g.reshape(2, dp, *g.shape[-2:])[:, :, :n]
        return g.reshape(2, dp * n, g.shape[-1])

    gathered = [merge(g, n) for g, n in zip(gathered, real)]

    def columns(g):
        return jnp.concatenate([g[0], g[1]], 1)

    def blocks(gs):
        return jnp.concatenate([g[0] for g in gs] + [g[1] for g in gs], 1)

    image_w, query_w, key_w, value_w, attn_out_t = (columns(g) for g in gathered[:5])
    embeds = gathered[5]
    text_embed32 = columns(embeds[:, :, :embed_half]).astype(F32)
    image_embed32 = columns(embeds[:, :, embed_half : 2 * embed_half]).astype(F32)
    norms = embeds[0, :, 2 * embed_half : 2 * embed_half + len(norm_shards)].astype(F32).T
    gain_one, bias_one, gain_two, bias_two, gain_three, bias_three = (norms[k] for k in range(6))
    cross_key_w, cross_value_w, cross_query_w, cross_out_t = (columns(g) for g in gathered[6:10])
    ffn_in_w = blocks(gathered[10 : 10 + hidden_blocks])
    ffn_out_tw = blocks(gathered[10 + hidden_blocks :])

    text_rows = text.reshape(half_pairs * length, model_width)
    patch_rows = patches.reshape(half_pairs * patch_count, -1)
    image_rows = matmul(patch_rows, image_w).astype(BF16)
    image32 = image_rows.astype(F32).reshape(half_pairs, patch_count, model_width)
    queries = split_heads(matmul(text_rows, query_w).astype(BF16), half_pairs)
    key_heads = split_heads(matmul(text_rows, key_w).astype(BF16), half_pairs)
    value_heads = split_heads(matmul(text_rows, value_w).astype(BF16), half_pairs)
    self_mixed, self_total = attend(queries, key_heads, value_heads)
    first = text_rows.astype(F32) + contract_cols(self_mixed, attn_out_t)
    hidden_one, normed_one, inv_one = layer_norm(first, gain_one, bias_one)
    low_one = hidden_one.astype(BF16)
    cross_queries = split_heads(matmul(low_one, cross_query_w).astype(BF16), half_pairs)
    cross_keys = split_heads(matmul(image_rows, cross_key_w).astype(BF16), half_pairs)
    cross_values = split_heads(matmul(image_rows, cross_value_w).astype(BF16), half_pairs)
    cross_mixed, cross_total = attend(cross_queries, cross_keys, cross_values)
    second = hidden_one + contract_cols(cross_mixed, cross_out_t)
    hidden_two, normed_two, inv_two = layer_norm(second, gain_two, bias_two)
    low_two = hidden_two.astype(BF16)
    inner = matmul(low_two, ffn_in_w)
    active = jax.nn.gelu(inner, approximate=False).astype(BF16)
    third = hidden_two + contract_cols(active, ffn_out_tw)
    output, normed_three, inv_three = layer_norm(third, gain_three, bias_three)
    output3 = output.reshape(half_pairs, length, model_width)
    joined = output3.astype(BF16)

    text_pool = jnp.mean(text.astype(F32), 1)
    image_pool = jnp.mean(image32, 1)
    grad_text_embed, grad_image_embed, text_extra, image_pool_grad = contrast(
        text_pool, image_pool, text_embed32, image_embed32
    )
    text_extra = (text_extra / length)[:, None, :]
    image_pool_grad = image_pool_grad / patch_count
    positions = jnp.arange(length, dtype=jnp.int32)
    slots = jnp.arange(phrase_starts.shape[1], dtype=jnp.int32)
    valid = (slots[None, :] < region_counts[:, None]).astype(F32)
    ends = phrase_starts + phrase_lengths
    inside = ((positions >= phrase_starts[..., None]) & (positions < ends[..., None])).astype(F32) * valid[..., None]
    span_weight = inside / phrase_lengths[..., None].astype(F32)
    chosen = (
        jnp.sum((box_patches[..., None] == jnp.arange(patch_count, dtype=jnp.int32)).astype(F32), axis=2)
        / box_patches.shape[2]
    )
    phrase = jnp.einsum("pbt,ptd->pbd", span_weight, output3, precision=HIGHEST)
    region = jnp.einsum("pbn,pnd->pbd", chosen, image32, precision=HIGHEST)
    mismatch = (phrase - region) * valid[..., None]
    box_text = jnp.einsum("pbt,pbd->ptd", span_weight, mismatch, precision=HIGHEST)
    box_image = -jnp.einsum("pbn,pbd->pnd", chosen, mismatch, precision=HIGHEST)
    image_extra = (box_image + image_pool_grad[:, None, :]).reshape(-1, model_width)

    upstream = cotangent.astype(F32).reshape(-1, model_width) + box_text.reshape(-1, model_width)
    grad_third, gain_three_grad, bias_three_grad = norm_back(upstream, normed_three, inv_three, gain_three)
    low_third = grad_third.astype(BF16)
    grad_ffn_out_t = contract_rows(low_third, active)
    dactive = matmul(low_third, ffn_out_tw)
    gelu_pull = jax.vjp(lambda values: jax.nn.gelu(values, approximate=False), inner)[1]
    dinner = gelu_pull(dactive)[0].astype(BF16)
    grad_ffn_in = contract_rows(low_two, dinner)
    grad_second = grad_third + contract_cols(dinner, ffn_in_w)
    grad_second, gain_two_grad, bias_two_grad = norm_back(grad_second, normed_two, inv_two, gain_two)
    low_second = grad_second.astype(BF16)
    grad_cross_out_t = contract_rows(low_second, cross_mixed)
    dcross = split_heads(matmul(low_second, cross_out_t).astype(BF16), half_pairs)
    dqueries, dkeys, dvalues = attend_back(cross_queries, cross_keys, cross_values, cross_total, dcross)
    grad_cross_query = contract_rows(low_one, dqueries)
    grad_first = grad_second + contract_cols(dqueries, cross_query_w)
    grad_cross_key = contract_rows(image_rows, dkeys)
    grad_cross_value = contract_rows(image_rows, dvalues)
    dimage = contract_cols(dkeys, cross_key_w) + contract_cols(dvalues, cross_value_w) + image_extra
    low_image = dimage.astype(BF16)
    grad_image = contract_rows(patch_rows, low_image)
    patch_grad = contract_cols(low_image, image_w).reshape(patches.shape)
    grad_first, gain_one_grad, bias_one_grad = norm_back(grad_first, normed_one, inv_one, gain_one)
    low_first = grad_first.astype(BF16)
    grad_attn_out_t = contract_rows(low_first, self_mixed)
    dself = split_heads(matmul(low_first, attn_out_t).astype(BF16), half_pairs)
    dqueries, dkeys, dvalues = attend_back(queries, key_heads, value_heads, self_total, dself)
    grad_query = contract_rows(text_rows, dqueries)
    grad_key = contract_rows(text_rows, dkeys)
    grad_value = contract_rows(text_rows, dvalues)
    dtext = contract_cols(dqueries, query_w) + contract_cols(dkeys, key_w) + contract_cols(dvalues, value_w)
    text_grad = (grad_first + dtext).reshape(half_pairs, length, model_width) + text_extra

    def halves(g):
        g = g.astype(BF16)
        return jnp.stack([g[:, :half], g[:, half:]], 0)

    def hidden_halves(g):
        g = g.astype(BF16)
        return [
            jnp.stack([g[:, k * half : (k + 1) * half], g[:, (hidden_blocks + k) * half : (hidden_blocks + k + 1) * half]])
            for k in range(hidden_blocks)
        ]

    norm_grads = jnp.stack(
        [gain_one_grad, bias_one_grad, gain_two_grad, bias_two_grad, gain_three_grad, bias_three_grad], 1
    ).astype(BF16)
    norm_grads = jnp.pad(norm_grads, ((0, 0), (0, half - 2 * embed_half - len(norm_shards))))
    text_half, image_half = grad_text_embed.astype(BF16), grad_image_embed.astype(BF16)
    small_grads = jnp.stack(
        [
            jnp.concatenate(
                [text_half[:, k * embed_half : (k + 1) * embed_half], image_half[:, k * embed_half : (k + 1) * embed_half], norm_grads], 1
            )
            for k in range(2)
        ]
    )
    grads = [
        *hidden_halves(grad_ffn_out_t),
        *hidden_halves(grad_ffn_in),
        halves(grad_cross_out_t),
        halves(grad_cross_query),
        halves(grad_cross_key),
        halves(grad_cross_value),
        halves(grad_image),
        halves(grad_attn_out_t),
        halves(grad_query),
        halves(grad_key),
        halves(grad_value),
        small_grads,
    ]
    shared = (2 * hidden_blocks + 4, len(grads) - 1)

    def cut(g):
        n = g.shape[1] // dp
        g = g.reshape(2, dp, n, g.shape[-1])
        g = jnp.pad(g, ((0, 0), (0, 0), (0, -(-n // 16) * 16 - n), (0, 0)))
        return g.reshape(2, *dims, *g.shape[-2:])

    results = scatter([cut(g) for g in grads], shared, (joined, text_grad), dims)
    joined_all, text_grad_all = (r.reshape(2 * half_pairs, length, model_width) for r in results[len(grads) :])
    sums = [r[..., :n, :] for r, n in zip(results, [g.shape[1] // dp for g in grads])]
    ffn_out_own = jnp.concatenate(sums[:hidden_blocks], 1).T
    ffn_in_own = jnp.concatenate(sums[hidden_blocks : 2 * hidden_blocks], 1)
    cross_out_own, cross_query_own, cross_key_own, cross_value_own, image_own, attn_out_own, query_own, key_own, value_own, small_own = sums[2 * hidden_blocks :]
    own_norm = lax.dynamic_index_in_dim(small_own, mp, 0, keepdims=False)[:, 2 * embed_half :]
    return (
        joined_all,
        text_grad_all,
        patch_grad,
        query_own,
        key_own,
        value_own,
        attn_out_own.T,
        cross_query_own,
        cross_key_own,
        cross_value_own,
        cross_out_own.T,
        jnp.concatenate([image_own[0], image_own[1]], 1),
        ffn_in_own,
        ffn_out_own,
        jnp.concatenate([small_own[0, :, :embed_half], small_own[1, :, :embed_half]], 1),
        jnp.concatenate([small_own[0, :, embed_half : 2 * embed_half], small_own[1, :, embed_half : 2 * embed_half]], 1),
        own_norm[:, 0],
        own_norm[:, 1],
        own_norm[:, 2],
        own_norm[:, 3],
        own_norm[:, 4],
        own_norm[:, 5],
    )


def solution(mesh):
    pairs, weight, turned, single = P("dp", None, None), P("dp", "mp"), P("mp", "dp"), P("dp", None)
    weights = (weight, weight, weight, turned, weight, weight, weight, turned, single, weight, turned, single, single)
    norms = (P("dp"),) * 6
    halves = P(("dp", "mp"), None, None)
    in_specs = (pairs, halves, pairs, P("dp"), single, single, pairs) + weights + norms
    out_specs = (pairs, pairs, halves) + weights + norms
    return jax.shard_map(body, mesh=mesh, in_specs=in_specs, out_specs=out_specs, check_vma=False)
```

```python
import functools
import math
import types

import jax
import jax.numpy as jnp
from jax import lax
from jax.experimental import pallas as pl
from jax.experimental.pallas import tpu as pltpu
from jax.sharding import PartitionSpec as P

HEAD_DIM = 64
EPS = 1e-06
TEMP_INVERSE = 20.0
GRAD_SCALE = 10.0
HIGHEST = lax.Precision.HIGHEST
MESH = pl.DeviceIdType.MESH
BF16 = jnp.bfloat16
F32 = jnp.float32


def split_dims(count):
    side = math.isqrt(count // 4) if count % 4 == 0 else 0
    if side and 4 * side * side == count:
        return (4, side, side)
    return (count, 1, 1)


class Place:
    def __init__(self, dims):
        self.dims = dims
        dp = lax.axis_index("dp")
        self.mp = lax.axis_index("mp")
        self.pos = (dp // (dims[1] * dims[2]), (dp // dims[2]) % dims[1], dp % dims[2])

    def at(self, axis, coord):
        spot = list(self.pos)
        spot[axis] = coord
        return ((spot[0] * self.dims[1] + spot[1]) * self.dims[2] + spot[2], self.mp)

    def peer(self):
        return (lax.axis_index("dp"), 1 - self.mp)


def block_of(place, order, stage, coord):
    index = [None] * 3
    for rank, axis in enumerate(order):
        index[axis] = slice(None) if rank < stage else (coord if rank == stage else place.pos[axis])
    return tuple(index)


def remote(src, dst, send_sem, recv_sem, device):
    return pltpu.make_async_remote_copy(
        src_ref=src,
        dst_ref=dst,
        send_sem=send_sem,
        recv_sem=recv_sem,
        device_id=device,
        device_id_type=MESH,
    )


def greet_lines(place):
    sem = pltpu.get_barrier_semaphore()

    def greet(device):
        pl.semaphore_signal(sem, inc=1, device_id=device, device_id_type=MESH)

    greet(place.peer())
    count = 1
    for axis in range(3):
        for away in range(1, place.dims[axis]):
            greet(place.at(axis, lax.rem(place.pos[axis] + away, place.dims[axis])))
            count += 1
    pl.semaphore_wait(sem, count)


def line_ways(length):
    return 2 if length > 2 else min(length - 1, 1)


def line_slots(length):
    return line_ways(length) * (length - 1)


def send_slot(dims, axis, way):
    return sum(line_ways(d) for d in dims[:axis]) + (way if dims[axis] > 2 else 0)


def send_slots(dims):
    return sum(line_ways(d) for d in dims)


def sum_slot(dims, axis, way, step):
    length = dims[axis]
    return sum(line_slots(d) for d in dims[:axis]) + (way * (length - 1) if length > 2 else 0) + step - 1


def sum_slots(dims):
    return sum(line_slots(d) for d in dims)


def gather_slots(dims):
    return sum(d - 1 for d in dims)


def gather_steps(place, order, buf, send_sem, recv_sem):
    sent = []
    for stage, axis in enumerate(order):
        length, pos = place.dims[axis], place.pos[axis]
        if length == 1:
            continue
        base = sum(d - 1 for d in place.dims[:axis])

        def copy(way, step, coord, to, stage=stage, axis=axis, pos=pos, base=base):
            ref = buf.at[block_of(place, order, stage, coord)]
            arrival = recv_sem.at[base + coord - (coord > to).astype(jnp.int32)]
            return remote(ref, ref, send_sem.at[send_slot(place.dims, axis, way)], arrival, place.at(axis, to))

        for step in range(1, length + 1):
            for way in (0, 1):
                coord = pos - (step - 1) if way == 0 else pos + (step - 1)
                to = pos + 1 if way == 0 else pos - 1
                here = (coord >= 0) if way == 0 else (coord < length)
                if step > 1:
                    pl.when(here)(lambda: copy(way, step - 1, coord, pos).wait_recv())
                if step < length:
                    more = jnp.logical_and(here, (to < length) if way == 0 else (to >= 0))

                    def send():
                        if step > 1:
                            copy(way, step, coord, to).wait_send()
                        copy(way, step, coord, to).start()

                    pl.when(more)(send)
                    if step == 1:
                        sent.append((more, functools.partial(copy, way, step, coord, to)))
            if step < length:
                yield
    return sent


def scatter_steps(place, order, acc, arrive, send_sem, recv_sem, result):
    sent = []
    last = [axis for axis in order if place.dims[axis] > 1][0]
    at = 0
    for stage in reversed(range(3)):
        axis = order[stage]
        length, pos = place.dims[axis], place.pos[axis]
        if length == 1:
            continue
        units = math.prod(place.dims[a] for a in order[:stage])
        shape = tuple(place.dims[a] for a in sorted(order[:stage]))

        def copy(way, step, coord, stage=stage, axis=axis, pos=pos, at=at, units=units, length=length, shape=shape):
            src = acc.at[block_of(place, order, stage, coord)]
            slot = at + ((way * (length - 1) if length > 2 else 0) + step - 1) * units
            dst = arrive.at[pl.ds(slot, units)].reshape(*shape, *arrive.shape[1:])
            leaves = send_sem.at[send_slot(place.dims, axis, way)]
            arrives = recv_sem.at[sum_slot(place.dims, axis, way, step)]
            device = place.at(axis, pos + 1 if way == 0 else pos - 1)
            return remote(src, dst, leaves, arrives, device), dst

        for step in range(length - 1, 0, -1):
            for way in (0, 1):
                coord = pos + step if way == 0 else pos - step
                has = (coord < length) if way == 0 else (coord >= 0)
                if step < length - 1:
                    farther = coord + 1 if way == 0 else coord - 1
                    before = (farther < length) if way == 0 else (farther >= 0)
                    pl.when(before)(lambda: copy(way, step, coord)[0].wait_send())
                pl.when(has)(lambda: copy(way, step, coord)[0].start())
                if step == 1:
                    sent.append((has, functools.partial(lambda move, *a: move(*a)[0], copy, way, step, coord)))
            yield
            for way in (0, 1):
                coord = pos - 1 + step if way == 0 else pos + 1 - step
                if way == 0:
                    comes = jnp.logical_and(pos > 0, coord < length)
                else:
                    comes = jnp.logical_and(pos < length - 1, coord >= 0)

                def take():
                    move, ref = copy(way, step, coord)
                    move.wait_recv()
                    index = block_of(place, order, stage, coord)
                    if axis == last and step == 1:
                        total = acc[index].astype(F32) + ref[...].astype(F32)
                        result[...] = total
                        acc[index] = total.astype(BF16)
                    else:
                        acc[index] = acc[index] + ref[...]

                pl.when(comes)(take)
        at += line_slots(length) * units
    return sent


def arrive_units(dims, order):
    units = 0
    for stage in range(3):
        if dims[order[stage]] > 1:
            length = dims[order[stage]]
            units += (2 if length > 2 else 1) * (length - 1) * math.prod(dims[a] for a in order[:stage])
    return units


def in_turn(plan):
    events = sorted((time, which, step) for which, (times, _) in enumerate(plan) for step, time in enumerate(times))
    results = [None] * len(plan)
    for _, which, _ in events:
        if results[which] is None:
            try:
                next(plan[which][1])
            except StopIteration as stop:
                results[which] = stop.value
    assert all(r is not None for r in results)
    return results


def wait_sent(sent):
    for cond, make in sent:
        if cond is None:
            make().wait_send()
        else:
            pl.when(cond)(lambda: make().wait_send())


ORDERS = ((2, 0, 1), (1, 0, 2), (0, 2, 1), (2, 0, 1), (1, 0, 2), (0, 1, 2))


def step_times(dims, order, start, back=False):
    times = [0.0]
    units = 1
    for axis in order:
        for _ in range(dims[axis] - 1):
            times.append(times[-1] + 1.6 * units + 3.0)
        units *= dims[axis]
    times.append(times[-1] + 4.0)
    if back:
        times = [times[-1] - t for t in reversed(times)]
    return [start + t for t in times] + [start + times[-1] + 4.0, start + times[-1] + 8.0]


def gather_kernel(dims, count, *refs):
    ins, outs = refs[:count], refs[count : 2 * count]
    send_sem, recv_sem, own_sem, peer_send, peer_recv = refs[2 * count :]
    place = Place(dims)
    own = [
        pltpu.make_async_copy(ins[c], outs[c].at[(place.mp,) + place.pos], own_sem.at[c]) for c in range(count)
    ]
    for copy in own:
        copy.start()
    greet_lines(place)

    def chunk(c, order):
        own[c].wait()
        mine, other = outs[c].at[place.mp], outs[c].at[1 - place.mp]
        sent = yield from gather_steps(place, order, mine, send_sem.at[c], recv_sem.at[c])

        def copy(ref):
            return remote(ref, ref, peer_send.at[c], peer_recv.at[c], place.peer())

        copy(mine).start()
        yield
        copy(other).wait_recv()
        return sent + [(None, lambda: copy(mine))]

    plan = []
    for c in range(count):
        order = ORDERS[c % len(ORDERS)]
        plan.append((step_times(dims, order, 3.9 * c), chunk(c, order)))
    for sent in in_turn(plan):
        wait_sent(sent)


def gather(shards, dims):
    count = len(shards)
    return pl.pallas_call(
        functools.partial(gather_kernel, dims, count),
        out_shape=[jax.ShapeDtypeStruct((2,) + dims + s.shape, BF16) for s in shards],
        in_specs=[pl.BlockSpec(memory_space=pl.ANY)] * count,
        out_specs=[pl.BlockSpec(memory_space=pl.ANY)] * count,
        scratch_shapes=[
            pltpu.SemaphoreType.DMA((count, send_slots(dims))),
            pltpu.SemaphoreType.DMA((count, gather_slots(dims))),
        ]
        + [pltpu.SemaphoreType.DMA((count,))] * 3,
        compiler_params=pltpu.CompilerParams(collective_id=0, has_side_effects=True),
        name="gather_weights",
    )(*shards)


def scatter_kernel(dims, count, shared, extra, *refs):
    ins, pieces = refs[:count], refs[count : count + extra]
    refs = refs[count + extra :]
    outs, wholes = refs[:count], refs[count : count + extra]
    refs = refs[count + extra :]
    acc, peer_in, arrive = refs[:count], refs[count : 2 * count], refs[2 * count : 3 * count]
    send_sem, recv_sem, own_sem, peer_send, peer_recv, end_send, end_recv, ex_own, ex_send, ex_recv = refs[3 * count :]
    place = Place(dims)
    own = [pltpu.make_async_copy(ins[c].at[place.mp], acc[c], own_sem.at[c]) for c in range(count)]
    for copy in own:
        copy.start()
    keep = [pltpu.make_async_copy(pieces[e], wholes[e].at[place.mp], ex_own.at[e]) for e in range(extra)]
    for copy in keep:
        copy.start()
    greet_lines(place)
    give = [
        remote(pieces[e], wholes[e].at[place.mp], ex_send.at[e], ex_recv.at[e], place.peer()) for e in range(extra)
    ]

    def chunk(c, order):
        def copy():
            return remote(ins[c].at[1 - place.mp], peer_in[c], peer_send.at[c], peer_recv.at[c], place.peer())

        copy().start()
        yield
        own[c].wait()
        copy().wait_recv()
        acc[c][...] = acc[c][...] + peer_in[c][...]
        result = outs[c].at[place.mp] if c in shared else outs[c]
        sent = yield from scatter_steps(
            place, order, acc[c], arrive[c], send_sem.at[c], recv_sem.at[c], result
        )
        sent.append((None, copy))
        if c in shared:

            def hand(half):
                ref = outs[c].at[half]
                return remote(ref, ref, end_send.at[c], end_recv.at[c], place.peer())

            hand(place.mp).start()
            yield
            hand(1 - place.mp).wait_recv()
            sent.append((None, lambda: hand(place.mp)))
        return sent

    plan = []
    for c in range(count):
        order = ORDERS[c % len(ORDERS)]
        plan.append((step_times(dims, order, 3.9 * c, True), chunk(c, order)))
    for copy in give:
        copy.start()
    for sent in in_turn(plan):
        wait_sent(sent)
    for copy in keep:
        copy.wait()
    for copy in give:
        copy.wait()


def scatter(grads, shared, pieces, dims):
    count, extra = len(grads), len(pieces)
    shapes = [
        jax.ShapeDtypeStruct(((2,) if c in shared else ()) + g.shape[-2:], F32) for c, g in enumerate(grads)
    ]
    wholes = [jax.ShapeDtypeStruct((2,) + p.shape, p.dtype) for p in pieces]
    return pl.pallas_call(
        functools.partial(scatter_kernel, dims, count, shared, extra),
        out_shape=shapes + wholes,
        in_specs=[pl.BlockSpec(memory_space=pl.ANY)] * (count + extra),
        out_specs=[pl.BlockSpec(memory_space=pltpu.VMEM)] * count + [pl.BlockSpec(memory_space=pl.ANY)] * extra,
        scratch_shapes=[pltpu.VMEM(g.shape[1:], BF16) for g in grads] * 2
        + [
            pltpu.VMEM((arrive_units(dims, ORDERS[c % len(ORDERS)]),) + g.shape[-2:], BF16)
            for c, g in enumerate(grads)
        ]
        + [pltpu.SemaphoreType.DMA((count, send_slots(dims))), pltpu.SemaphoreType.DMA((count, sum_slots(dims)))]
        + [pltpu.SemaphoreType.DMA((count,))] * 5
        + [pltpu.SemaphoreType.DMA((extra,))] * 3,
        compiler_params=pltpu.CompilerParams(
            collective_id=1, has_side_effects=True, vmem_limit_bytes=60 * 2**20
        ),
        name="scatter_gradients",
    )(*grads, *pieces)


def matmul(left, right):
    return jnp.dot(left, right, preferred_element_type=F32)


def contract_rows(left, right):
    return lax.dot_general(left, right, (((0,), (0,)), ((), ())), preferred_element_type=F32)


def contract_cols(left, right):
    return lax.dot_general(left, right, (((1,), (1,)), ((), ())), preferred_element_type=F32)


def layer_norm(inputs, gain, shift):
    centred = inputs - jnp.mean(inputs, -1, keepdims=True)
    inv_std = lax.rsqrt(jnp.mean(centred * centred, -1, keepdims=True) + EPS)
    normed = centred * inv_std
    return (normed * gain + shift, normed, inv_std)


def norm_back(upstream, normed, inv_std, gain):
    scaled = upstream * gain
    inner_mean = jnp.mean(scaled * normed, -1, keepdims=True)
    result = inv_std * (scaled - jnp.mean(scaled, -1, keepdims=True) - normed * inner_mean)
    return (result, jnp.sum(upstream * normed, 0), jnp.sum(upstream, 0))


def split_heads(flat, pair_count):
    return flat.reshape(pair_count, -1, flat.shape[-1] // HEAD_DIM, HEAD_DIM)


def attend(queries, key_heads, value_heads):
    factor = 1.0 / math.sqrt(HEAD_DIM)
    scores = jnp.einsum("pqhd,pkhd->phqk", queries, key_heads, preferred_element_type=F32) * factor
    row_max = jnp.max(scores, -1, keepdims=True)
    expd = jnp.exp(scores - row_max)
    row_sum = jnp.sum(expd, -1, keepdims=True)
    probs = (expd / row_sum).astype(BF16)
    mixed = jnp.einsum("phqk,pkhd->pqhd", probs, value_heads, preferred_element_type=F32)
    flat_rows = queries.shape[0] * queries.shape[1]
    return (mixed.astype(BF16).reshape(flat_rows, -1), row_max + jnp.log(row_sum))


def attend_back(queries, key_heads, value_heads, log_total, upstream):
    factor = 1.0 / math.sqrt(HEAD_DIM)
    scores = jnp.einsum("pqhd,pkhd->phqk", queries, key_heads, preferred_element_type=F32) * factor
    probs = jnp.exp(scores - log_total)
    dprobs = jnp.einsum("pqhd,pkhd->phqk", upstream, value_heads, preferred_element_type=F32)
    dscores = (probs * (dprobs - jnp.sum(dprobs * probs, -1, keepdims=True))).astype(BF16)
    dqueries = jnp.einsum("phqk,pkhd->pqhd", dscores, key_heads, preferred_element_type=F32) * factor
    dkeys = jnp.einsum("phqk,pqhd->pkhd", dscores, queries, preferred_element_type=F32) * factor
    dvalues = jnp.einsum("phqk,pqhd->pkhd", probs.astype(BF16), upstream, preferred_element_type=F32)
    return tuple(t.astype(BF16).reshape(-1, t.shape[2] * t.shape[3]) for t in (dqueries, dkeys, dvalues))


def unit_back(raw, inv_norm, upstream):
    cubed = inv_norm * inv_norm * inv_norm
    return inv_norm * upstream - raw * cubed * jnp.sum(raw * upstream, -1, keepdims=True)


def contrast(text_pool, image_pool, text_embed32, image_embed32):
    text_raw = jnp.dot(text_pool, text_embed32, precision=HIGHEST)
    text_inv = lax.rsqrt(jnp.sum(text_raw * text_raw, -1, keepdims=True) + EPS)
    image_raw = jnp.dot(image_pool, image_embed32, precision=HIGHEST)
    image_inv = lax.rsqrt(jnp.sum(image_raw * image_raw, -1, keepdims=True) + EPS)
    both = jnp.concatenate([(text_raw * text_inv).astype(BF16), (image_raw * image_inv).astype(BF16)], 1)
    width = text_raw.shape[1]
    everyone = lax.all_gather(both, ("dp", "mp"), axis=0, tiled=True)
    text_all, image_all = everyone[:, :width], everyone[:, width:]
    logits = contract_cols(text_all, image_all) * TEMP_INVERSE
    weights = jnp.exp(logits - jax.nn.logsumexp(logits, axis=1, keepdims=True)) + jnp.exp(
        logits - jax.nn.logsumexp(logits, axis=0, keepdims=True)
    )
    weights = weights - 2.0 * jnp.eye(logits.shape[0], dtype=F32)
    count = text_pool.shape[0]
    start = (lax.axis_index("dp") * 2 + lax.axis_index("mp")) * count
    rows = lax.dynamic_slice_in_dim(weights, start, count, 0)
    columns = lax.dynamic_slice_in_dim(weights, start, count, 1)
    dtext = GRAD_SCALE * jnp.dot(rows, image_all.astype(F32), precision=HIGHEST)
    dimage = GRAD_SCALE * jnp.dot(columns.T, text_all.astype(F32), precision=HIGHEST)
    dtext_raw = unit_back(text_raw, text_inv, dtext)
    dimage_raw = unit_back(image_raw, image_inv, dimage)
    return (
        jnp.dot(text_pool.T, dtext_raw, precision=HIGHEST),
        jnp.dot(image_pool.T, dimage_raw, precision=HIGHEST),
        jnp.dot(dtext_raw, text_embed32.T, precision=HIGHEST),
        jnp.dot(dimage_raw, image_embed32.T, precision=HIGHEST),
    )


FACTOR = 1.0 / math.sqrt(HEAD_DIM)
LOWEST = -1e30
TEXT_PAD = 64
PATCH_PAD = 160
PEER_RING = 3
ARRIVE_RING = 11


def nn(a, b):
    return lax.dot_general(a, b, (((1,), (0,)), ((), ())), preferred_element_type=F32)


def nt(a, b):
    return lax.dot_general(a, b, (((1,), (1,)), ((), ())), preferred_element_type=F32)


def tn(a, b):
    return lax.dot_general(a, b, (((0,), (0,)), ((), ())), preferred_element_type=F32)


def exact(a, b, dims):
    return lax.dot_general(a, b, (dims, ((), ())), precision=HIGHEST, preferred_element_type=F32)


def terms(x):
    high = x.astype(BF16)
    return high, (x - high.astype(F32)).astype(BF16)


def near(a, b, dims):
    def dot(x, y):
        return lax.dot_general(x, y, (dims, ((), ())), preferred_element_type=F32)

    (a_high, a_low), (b_high, b_low) = terms(a), terms(b)
    return dot(a_high, b_high) + (dot(a_high, b_low) + dot(a_low, b_high))


class Blocks:
    def __init__(self):
        self.free, self.top = [], 0

    def take(self, count):
        spare = sorted(self.free)
        for at in spare:
            if all(at + k in spare for k in range(count)):
                for k in range(count):
                    self.free.remove(at + k)
                return at
        at, self.top = self.top, self.top + count
        return at

    def give(self, at, count):
        self.free += range(at, at + count)


def lane_masks(width, split):
    lane = lax.broadcasted_iota(jnp.int32, (1, width), 1)
    left = (lane < split).astype(F32)
    return left, 1.0 - left


def head_pair(x):
    left, right = lane_masks(128, 64)
    return jnp.concatenate([x * left.astype(BF16), x * right.astype(BF16)], 0)


def one_head_each(x):
    half = x.shape[0] // 2
    left = lax.broadcasted_iota(jnp.int32, (half, 128), 1) < 64
    return jnp.where(left, x[:half], x[half:])


def softmax_pair(scores, keys, real):
    lane = lax.broadcasted_iota(jnp.int32, scores.shape, 1)
    left = lane < keys
    within = jnp.where(left, lane, lane - keys)
    scores = jnp.where(within < real, scores * FACTOR, LOWEST)
    top0 = jnp.max(jnp.where(left, scores, LOWEST), 1, keepdims=True)
    top1 = jnp.max(jnp.where(left, LOWEST, scores), 1, keepdims=True)
    expd = jnp.exp(scores - jnp.where(left, top0, top1))
    sum0 = jnp.sum(jnp.where(left, expd, 0.0), 1, keepdims=True)
    sum1 = jnp.sum(jnp.where(left, 0.0, expd), 1, keepdims=True)
    return (expd * jnp.where(left, 1.0 / sum0, 1.0 / sum1)).astype(BF16)


def softmax_pair_back(probs, dprobs, keys):
    left = lax.broadcasted_iota(jnp.int32, dprobs.shape, 1) < keys
    probs = probs.astype(F32)
    both = probs * dprobs
    sum0 = jnp.sum(jnp.where(left, both, 0.0), 1, keepdims=True)
    sum1 = jnp.sum(jnp.where(left, 0.0, both), 1, keepdims=True)
    return (both - probs * jnp.where(left, sum0, sum1)).astype(BF16)


def norm_rows(x):
    centred = x - jnp.mean(x, -1, keepdims=True)
    inv_std = lax.rsqrt(jnp.mean(centred * centred, -1, keepdims=True) + EPS)
    return centred * inv_std, inv_std


class Layer:
    def __init__(self, dims, sizes, refs):
        self.dims, self.sizes = dims, sizes
        self.__dict__.update(refs)
        self.place = Place(dims)
        self.blocks, self.wide = Blocks(), Blocks()
        self.rows = sizes.pairs * TEXT_PAD
        self.patch_rows = sizes.pairs * PATCH_PAD
        self.half = sizes.half
        self.da = None


    def weight(self, slot, h):
        w = self.w[slot][h]
        return w.reshape(-1, w.shape[-1])

    def put_grad(self, slot, h, f, value):
        cut = self.dims[0] // 2
        shape = self.w[slot].shape[2:]
        self.w[slot][h, f * cut : (f + 1) * cut] = value.astype(BF16).reshape(cut, *shape)

    def project(self, at, slot, h):
        w = self.weight(slot, h)
        return nn(self.t[at], w[: self.half]) + nn(self.t[at + 1], w[self.half :])

    def two(self, fn):
        for h in range(2):
            fn(h)

    def text_loop(self, fn):
        def step(p, carry):
            fn(p, pl.ds(pl.multiple_of(p * TEXT_PAD, TEXT_PAD), TEXT_PAD))
            return carry

        lax.fori_loop(0, self.sizes.pairs, step, 0)

    def read_rows(self, at, rows):
        return jnp.concatenate([self.t[at, rows, :], self.t[at + 1, rows, :]], 1)

    def write_rows(self, at, rows, value):
        self.t[at, rows, :] = value[:, : self.half].astype(BF16)
        self.t[at + 1, rows, :] = value[:, self.half :].astype(BF16)


    def own_pairs(self, ref, sem):
        return pltpu.make_async_copy(
            ref.at[pl.ds(self.place.mp * self.sizes.pairs, self.sizes.pairs)], self.joined, sem
        )

    def load(self):
        self.x, self.cot = self.blocks.take(2), self.blocks.take(2)
        for p in range(2):
            self.patch_load(p).start()
        self.own_pairs(self.text_in, self.load_sem.at[0]).start()

    def unpack(self, at):
        gap = jnp.zeros((TEXT_PAD - self.sizes.length, 2 * self.half), F32)
        for p in range(self.sizes.pairs):
            value = jnp.concatenate([self.joined[p].astype(F32), gap], 0)
            self.write_rows(at, pl.ds(p * TEXT_PAD, TEXT_PAD), value)

    def take_text(self):
        self.own_pairs(self.text_in, self.load_sem.at[0]).wait()
        self.unpack(self.x)
        self.own_pairs(self.cot_in, self.load_sem.at[1]).start()

    def patch_load(self, p):
        return pltpu.make_async_copy(self.patches_in.at[p], self.patch_in.at[p % 2], self.patch_sem.at[p % 2])

    def take_patches(self):
        gap = jnp.zeros((PATCH_PAD - self.sizes.patch_count, self.patches.shape[1]), F32)
        for p in range(self.sizes.pairs):
            self.patch_load(p).wait()
            value = jnp.concatenate([self.patch_in[p % 2].astype(F32), gap], 0)
            self.patches[p * PATCH_PAD : (p + 1) * PATCH_PAD, :] = value.astype(BF16)
            if p + 2 < self.sizes.pairs:
                self.patch_load(p + 2).start()

    def take_cotangent(self):
        self.own_pairs(self.cot_in, self.load_sem.at[1]).wait()
        self.unpack(self.cot)

    def own_copies(self, c, name):
        dst = self.w[name].at[(self.place.mp,) + self.place.pos]
        blocks, width = self.sizes.hidden_blocks, self.sizes.embed_half

        def copy(src, dst, sem):
            return pltpu.make_async_copy(src, dst, self.own_sem.at[sem])

        if name == IMAGE:
            return [copy(self.shards[name].at[:, pl.ds(self.place.mp * self.half, self.half)], dst, c)]
        if name == SMALL:
            cols = pl.ds(self.place.mp * width, width)
            refs = self.text_embed, self.image_embed
            spare = FFN + 2 * blocks
            return [
                copy(ref.at[:, cols], dst.at[:, pl.ds(k * width, width)], c if k == 0 else spare)
                for k, ref in enumerate(refs)
            ]
        if name >= FFN:
            ref = self.ffn_in_all if name < FFN + blocks else self.ffn_out_all
            return [copy(ref.at[:, pl.ds((name - FFN) % blocks * self.half, self.half)], dst, c)]
        return [copy(self.shards[name], dst, c)]

    def place_norms(self):
        rows = [ref[...].astype(F32) for ref in self.norm_in.values()]
        rows = jnp.concatenate(rows + [jnp.zeros((8 - len(rows), rows[0].shape[1]), F32)], 0).astype(BF16)
        width = 2 * self.sizes.embed_half
        lane = lax.broadcasted_iota(jnp.int32, (rows.shape[0], self.half - width), 1)
        unit = (lane == lax.broadcasted_iota(jnp.int32, lane.shape, 0)).astype(F32).astype(BF16)
        ref = self.w[SMALL].at[(self.place.mp,) + self.place.pos]
        ref[:, width:] = tn(rows, unit).astype(BF16)

    def image_features(self):
        self.im = self.wide.take(2)
        block = self.patch_rows // 3

        def step(i, carry):
            rows = pl.ds(pl.multiple_of(i * block, block), block)
            left = self.patches[rows, :]
            for h in range(2):
                self.u[self.im + h, rows, :] = nn(left, self.weight(IMAGE, h)).astype(BF16)
            return carry

        lax.fori_loop(0, 3, step, 0)

    def self_projections(self):
        self.q = self.blocks.take(6)
        for k, slot in enumerate((QUERY, KEY, VALUE)):
            self.two(lambda h: self.t.__setitem__(self.q + 2 * k + h, self.project(self.x, slot, h).astype(BF16)))

    def couples(self):
        return [(h, slice(128 * j, 128 * j + 128)) for h in range(2) for j in range(self.half // 128)]

    def put_couples(self, ref, at, rows, values):
        each = len(values) // 2
        for h in range(2):
            ref[at + h, rows, :] = jnp.concatenate(values[h * each : (h + 1) * each], 1)

    def attention(self, p, rows, queries, keys, values, saved, key_pad, real, out):
        scores = jnp.concatenate([nt(q, head_pair(k)) for q, k in zip(queries, keys)], 0)
        probs = softmax_pair(scores, key_pad, real)
        saved[p] = probs
        mixed = [
            nn(probs[TEXT_PAD * i : TEXT_PAD * (i + 1)], head_pair(v)).astype(BF16) for i, v in enumerate(values)
        ]
        self.put_couples(self.t, out, rows, mixed)

    def attention_back(self, p, queries, keys, values, upstream, saved, key_pad):
        probs = saved[p]
        dprobs = jnp.concatenate([nt(d, head_pair(v)) for d, v in zip(upstream, values)], 0)
        dscores = softmax_pair_back(probs, dprobs, key_pad)
        part = [slice(TEXT_PAD * i, TEXT_PAD * (i + 1)) for i in range(len(queries))]
        dqueries = [(nn(dscores[r], head_pair(k)) * FACTOR).astype(BF16) for r, k in zip(part, keys)]
        dkeys = [(one_head_each(tn(dscores[r], q)) * FACTOR).astype(BF16) for r, q in zip(part, queries)]
        dvalues = [one_head_each(tn(probs[r], d)).astype(BF16) for r, d in zip(part, upstream)]
        return dqueries, dkeys, dvalues

    def self_attention(self):
        self.a1 = self.blocks.take(2)

        def pair(p, rows):
            q, k, v = ([self.t[self.q + 2 * m + h, rows, lanes] for h, lanes in self.couples()] for m in range(3))
            self.attention(p, rows, q, k, v, self.p1, TEXT_PAD, self.sizes.length, self.a1)

        self.text_loop(pair)

    def norm_params(self):
        cols = self.weight(SMALL, 0)[:, 2 * self.sizes.embed_half :].astype(F32)
        self.norms[...] = jnp.transpose(cols)[: self.norms.shape[0]]

    def after_branch(self, at, slot, k):
        self.z[...] = nt(self.t[at], self.weight(slot, 0)) + nt(self.t[at + 1], self.weight(slot, 1))
        normed_at, low_at = self.blocks.take(2), self.blocks.take(2)

        def rows_step(p, rows):
            residual = self.read_rows(self.x, rows).astype(F32) if k == 0 else self.hid[rows, :]
            normed, inv_std = norm_rows(residual + self.z[rows, :])
            hidden = normed * self.norms[2 * k : 2 * k + 1, :] + self.norms[2 * k + 1 : 2 * k + 2, :]
            self.hid[rows, :] = hidden
            self.inv[k, rows, :] = inv_std
            self.write_rows(normed_at, rows, normed)
            self.write_rows(low_at, rows, hidden)

        self.text_loop(rows_step)
        return normed_at, low_at

    def turned(self, at):
        out = self.blocks.take(2)
        for h in range(2):
            self.t[out + h] = jnp.transpose(self.t[at + h])
        return out

    def after_self(self):
        self.n1, low = self.after_branch(self.a1, ATTN_OUT, 0)
        self.low1, self.low1_t = low, self.turned(low)

    def cross_keys(self, slot):
        at = self.wide.take(2)
        block = self.patch_rows // 3

        def step(i, carry):
            rows = pl.ds(pl.multiple_of(i * block, block), block)
            for h in range(2):
                w = self.weight(slot, h)
                self.u[at + h, rows, :] = (
                    nn(self.u[self.im, rows, :], w[: self.half]) + nn(self.u[self.im + 1, rows, :], w[self.half :])
                ).astype(BF16)
            return carry

        lax.fori_loop(0, 3, step, 0)
        return at

    def make_keys(self):
        self.k2 = self.cross_keys(CROSS_KEY)

    def make_values(self):
        self.v2 = self.cross_keys(CROSS_VALUE)

    def cross_query(self):
        self.q2 = self.blocks.take(2)
        self.two(lambda h: self.t.__setitem__(self.q2 + h, self.project(self.low1, CROSS_QUERY, h).astype(BF16)))
        self.blocks.give(self.low1, 2)

    def patch_rows_of(self, p):
        return pl.ds(pl.multiple_of(p * PATCH_PAD, PATCH_PAD), PATCH_PAD)

    def cross_attention(self):
        self.a2 = self.blocks.take(2)

        def pair(p, rows):
            keys = self.patch_rows_of(p)
            q = [self.t[self.q2 + h, rows, lanes] for h, lanes in self.couples()]
            k, v = ([self.u[at + h, keys, lanes] for h, lanes in self.couples()] for at in (self.k2, self.v2))
            self.attention(p, rows, q, k, v, self.p2, PATCH_PAD, self.sizes.patch_count, self.a2)

        self.text_loop(pair)

    def after_cross(self):
        self.n2, low = self.after_branch(self.a2, CROSS_OUT, 1)
        self.low2, self.low2_t = low, self.turned(low)
        self.g, self.dg = self.blocks.take(2 * self.sizes.hidden_blocks), self.blocks.take(2 * self.sizes.hidden_blocks)

    def ffn_in(self, k):
        def half(h, carry):
            inner = self.project(self.low2, FFN + k, h)
            cdf = 0.5 * (1.0 + lax.erf(inner * math.sqrt(0.5)))
            pdf = jnp.exp(-0.5 * inner * inner) * (1.0 / math.sqrt(2.0 * math.pi))
            self.t[self.g + 2 * k + h] = (inner * cdf).astype(BF16)
            self.t[self.dg + 2 * k + h] = (cdf + inner * pdf).astype(BF16)
            return carry

        lax.fori_loop(0, 2, half, 0)
        if k == self.sizes.hidden_blocks - 1:
            self.blocks.give(self.low2, 2)

    def ffn_out(self, k):
        def half(h, carry):
            self.hid[...] += nt(self.t[self.g + 2 * k + h], self.weight(FFN + self.sizes.hidden_blocks + k, h))
            return carry

        lax.fori_loop(0, 2, half, 0)


    def pools(self):
        pairs, length, patch_count = self.sizes.pairs, self.sizes.length, self.sizes.patch_count
        self.pool[...] = jnp.zeros_like(self.pool)
        for p in range(pairs):
            rows = pl.ds(p * TEXT_PAD, TEXT_PAD)
            self.pool[0, p : p + 1, :] = jnp.sum(self.read_rows(self.x, rows).astype(F32), 0, keepdims=True) * (1.0 / length)
            keys = pl.ds(p * PATCH_PAD, PATCH_PAD)
            for h in range(2):
                self.pool[1, p : p + 1, h * self.half : (h + 1) * self.half] = jnp.sum(
                    self.u[self.im + h, keys, :].astype(F32), 0, keepdims=True
                ) * (1.0 / patch_count)

    def embed_weight(self, which, h):
        width = self.sizes.embed_half
        return self.weight(SMALL, h)[:, which * width : (which + 1) * width].astype(F32)

    def embed(self):
        width = self.sizes.embed_half
        for which in range(2):
            for h in range(2):
                self.raw[which, :, h * width : (h + 1) * width] = exact(
                    self.pool[which], self.embed_weight(which, h), ((1,), (0,))
                )
            raw = self.raw[which]
            inv = lax.rsqrt(jnp.sum(raw * raw, -1, keepdims=True) + EPS)
            self.own_emb[:, which * 2 * width : (which + 1) * 2 * width] = (raw * inv).astype(BF16)

    def contrast(self):
        width, pairs = self.sizes.embed_half, self.sizes.pairs
        everyone = self.emb[...].reshape(-1, 4 * width)
        count = everyone.shape[0]
        both = everyone[:, : 2 * width], everyone[:, 2 * width :]
        own = self.own_emb[...][:, : 2 * width], self.own_emb[...][:, 2 * width :]
        spot = self.place.pos
        me = self.place.mp * (count // 2) + ((spot[0] * self.dims[1] + spot[1]) * self.dims[2] + spot[2]) * 16
        real_row = (lax.broadcasted_iota(jnp.int32, (1, count), 1) % 16 < pairs).astype(F32)
        real_col = (lax.broadcasted_iota(jnp.int32, (count, 1), 0) % 16 < pairs).astype(F32)
        own_row = (lax.broadcasted_iota(jnp.int32, (16, 1), 0) < pairs).astype(F32)
        match = (
            lax.broadcasted_iota(jnp.int32, (16, count), 1) == lax.broadcasted_iota(jnp.int32, (16, count), 0) + me
        ).astype(F32)
        for which in range(2):
            mine, others = own[which], both[1 - which]
            column_sum = jnp.zeros((1, count), F32)
            for at in range(0, count, 128):
                cross = nt(both[which][at : at + 128], others) * TEMP_INVERSE - TEMP_INVERSE
                column_sum = column_sum + jnp.sum(jnp.exp(cross) * real_col[at : at + 128], 0, keepdims=True)
            logits = nt(mine, others) * TEMP_INVERSE - TEMP_INVERSE
            expd = jnp.exp(logits) * (real_row * own_row)
            row_sum = jnp.sum(expd, 1, keepdims=True) + (1.0 - own_row)
            pull = expd * (1.0 / row_sum) + expd * (1.0 / column_sum) - 2.0 * match * own_row
            upstream = GRAD_SCALE * exact(pull, others.astype(F32), ((1,), (0,)))
            raw = self.raw[which]
            inv = lax.rsqrt(jnp.sum(raw * raw, -1, keepdims=True) + EPS)
            draw = unit_back(raw, inv, upstream)
            scale = 1.0 / (self.sizes.length if which == 0 else self.sizes.patch_count)
            extra = exact(draw[:, :width], self.embed_weight(which, 0), ((1,), (1,))) + exact(
                draw[:, width:], self.embed_weight(which, 1), ((1,), (1,))
            )
            self.extra[which] = extra * scale
            for h in range(2):
                value = exact(self.pool[which], draw[:, h * width : (h + 1) * width], ((0,), (0,)))
                self.put_small(h, which * width, value)


    def region(self):
        pairs, length, patch_count = self.sizes.pairs, self.sizes.length, self.sizes.patch_count
        boxes, listed = self.picks.shape[1:]
        self.chosen[...] = jnp.zeros_like(self.chosen)
        self.span[...] = jnp.zeros_like(self.span)
        for p in range(pairs):
            me = self.place.mp * pairs + p

            def column(ref):
                lane = lax.broadcasted_iota(jnp.int32, ref.shape, 1)
                return jnp.sum(jnp.where(lane == me, ref[...].astype(F32), 0.0), 1, keepdims=True)

            counts, starts, lengths = column(self.counts), column(self.starts), column(self.lengths)
            picks = self.picks[me]
            spot = lax.broadcasted_iota(jnp.int32, (boxes, PATCH_PAD), 1)
            listing = jnp.zeros((boxes, PATCH_PAD), F32)
            for k in range(listed):
                listing = listing + (picks[:, k : k + 1] == spot).astype(F32)
            valid = lax.broadcasted_iota(jnp.int32, (boxes, 1), 0).astype(F32) < counts
            self.chosen[p, :boxes, :] = jnp.where(valid, listing * (1.0 / listed), 0.0)
            token = lax.broadcasted_iota(jnp.int32, (boxes, TEXT_PAD), 1).astype(F32)
            inside = (token >= starts) & (token < starts + lengths) & valid
            self.span[p, :boxes, :] = jnp.where(inside, 1.0 / lengths, 0.0)
            keys = pl.ds(p * PATCH_PAD, PATCH_PAD)
            for h in range(2):
                self.regions[p, :, h * self.half : (h + 1) * self.half] = nn(
                    self.chosen[p].astype(BF16), self.u[self.im + h, keys, :]
                )


    def norm_back(self, k, upstream, normed, inv_std, rows):
        scaled = upstream * self.norms[2 * k : 2 * k + 1, :]
        inner = jnp.mean(scaled * normed, -1, keepdims=True)
        self.norm_grad[2 * k : 2 * k + 1, :] += jnp.sum(upstream * normed, 0, keepdims=True)
        self.norm_grad[2 * k + 1 : 2 * k + 2, :] += jnp.sum(upstream, 0, keepdims=True)
        result = inv_std * (scaled - jnp.mean(scaled, -1, keepdims=True) - normed * inner)
        self.z[rows, :] = result
        self.write_rows(self.db, rows, result)

    def output_and_back(self):
        self.db = self.blocks.take(2)
        self.norm_grad[...] = jnp.zeros_like(self.norm_grad)

        def pair(p, rows):
            normed, inv_std = norm_rows(self.hid[rows, :])
            output = normed * self.norms[4:5, :] + self.norms[5:6, :]
            self.joined[p] = output[: self.sizes.length].astype(BF16)
            mismatch = near(self.span[p], output, ((1,), (0,))) - self.regions[p]
            self.regions[p] = mismatch
            upstream = self.read_rows(self.cot, rows).astype(F32) + near(self.span[p], mismatch, ((0,), (0,)))
            self.norm_back(2, upstream, normed, inv_std, rows)

        self.text_loop(pair)
        self.blocks.give(self.cot, 2)
        self.db_t = self.turned(self.db)

    def grads(self, slot, h, left_t, right):
        for f in range(2):
            self.put_grad(slot, h, f, nn(self.t[left_t + f], right))

    def ffn_out_back(self, k):
        slot = FFN + self.sizes.hidden_blocks + k

        def half(h, carry):
            at = 2 * k + h
            dactive = self.project(self.db, slot, h)
            self.t[self.dg + at] = (dactive * self.t[self.dg + at].astype(F32)).astype(BF16)
            self.grads(slot, h, self.db_t, self.t[self.g + at])
            return carry

        lax.fori_loop(0, 2, half, 0)
        self.blocks.give(self.g + 2 * k, 2)

    def ffn_in_back(self, k):
        slot = FFN + k

        def half(h, carry):
            dinner = self.t[self.dg + 2 * k + h]
            self.z[...] += nt(dinner, self.weight(slot, h))
            self.grads(slot, h, self.low2_t, dinner)
            return carry

        lax.fori_loop(0, 2, half, 0)

    def back_through_norm(self, k):
        normed_at = (self.n1, self.n2)[k]

        def step(p, rows):
            self.norm_back(k, self.z[rows, :], self.read_rows(normed_at, rows).astype(F32), self.inv[k, rows, :], rows)

        self.text_loop(step)
        for h in range(2):
            self.t[self.db_t + h] = jnp.transpose(self.t[self.db + h])

    def branch_back(self, slot, at):
        if self.da is None:
            self.da = self.blocks.take(2)

        def half(h, carry):
            self.t[self.da + h] = self.project(self.db, slot, h).astype(BF16)
            self.grads(slot, h, self.db_t, self.t[at + h])
            return carry

        lax.fori_loop(0, 2, half, 0)

    def cross_attention_back(self):
        def pair(p, rows):
            keys = self.patch_rows_of(p)
            q, d = ([self.t[at + h, rows, lanes] for h, lanes in self.couples()] for at in (self.q2, self.da))
            k, v = ([self.u[at + h, keys, lanes] for h, lanes in self.couples()] for at in (self.k2, self.v2))
            dq, dk, dv = self.attention_back(p, q, k, v, d, self.p2, PATCH_PAD)
            self.put_couples(self.t, self.q2, rows, dq)
            self.put_couples(self.u, self.k2, keys, dk)
            self.put_couples(self.u, self.v2, keys, dv)

        self.text_loop(pair)

    def cross_query_back(self):
        def half(h, carry):
            dq = self.t[self.q2 + h]
            self.z[...] += nt(dq, self.weight(CROSS_QUERY, h))
            self.grads(CROSS_QUERY, h, self.low1_t, dq)
            return carry

        lax.fori_loop(0, 2, half, 0)

    def image_back(self):
        self.dim = self.wide.take(2)
        group = self.sizes.pairs // 2
        block = group * PATCH_PAD

        def step(i, carry):
            rows = pl.ds(pl.multiple_of(i * block, block), block)
            parts = [self.u[at + h, rows, :] for at in (self.k2, self.v2) for h in range(2)]
            for half in range(2):
                cols = slice(half * self.half, (half + 1) * self.half)
                weights = [self.weight(slot, h)[cols] for slot in (CROSS_KEY, CROSS_VALUE) for h in range(2)]
                total = sum(nt(part, weight) for part, weight in zip(parts, weights))
                for k in range(group):
                    p = group * i + k
                    value = total[k * PATCH_PAD : (k + 1) * PATCH_PAD]
                    value = value - sum(tn(self.chosen[p].astype(BF16), m) for m in terms(self.regions[p, :, cols]))
                    value = value + self.extra[1, pl.ds(p, 1), cols]
                    self.u[self.dim + half, self.patch_rows_of(p), :] = value.astype(BF16)
            return carry

        lax.fori_loop(0, 2, step, 0)

    def cross_key_back(self, slot, at):
        for f in range(2):

            def half(h, carry):
                self.put_grad(slot, h, f, tn(self.u[self.im + f], self.u[at + h]))
                return carry

            lax.fori_loop(0, 2, half, 0)

    def patch_back(self):
        group, patch_count = self.sizes.pairs // 2, self.sizes.patch_count
        width = self.patch_stage.shape[-1]
        steps = [(n, g) for n in range(self.patches.shape[1] // width) for g in range(2)]

        def out(i):
            n, g = steps[i]
            dst = self.patch_grad.at[pl.ds(g * group, group), :, pl.ds(n * width, width)]
            return pltpu.make_async_copy(self.patch_stage.at[i % 2], dst, self.patch_sem.at[i % 2])

        for i, (n, g) in enumerate(steps):
            if i >= 2:
                out(i - 2).wait()
            rows, cols = pl.ds(g * group * PATCH_PAD, group * PATCH_PAD), slice(n * width, (n + 1) * width)
            value = nt(self.u[self.dim, rows, :], self.weight(IMAGE, 0)[cols])
            value = value + nt(self.u[self.dim + 1, rows, :], self.weight(IMAGE, 1)[cols])
            for k in range(group):
                self.patch_stage[i % 2, k] = value[k * PATCH_PAD : k * PATCH_PAD + patch_count]
            out(i).start()
        for i in range(len(steps) - 2, len(steps)):
            out(i).wait()

    def image_weight_back(self):
        cut = self.dims[0] // 2
        shape = self.w[IMAGE].shape[2:]
        half_depth = self.patches.shape[1] // 2
        for f in range(2):

            def half(h, carry):
                value = tn(self.patches[:, f * half_depth : (f + 1) * half_depth], self.u[self.dim + h])
                self.w[IMAGE][h, f * cut : (f + 1) * cut] = value.astype(BF16).reshape(cut, *shape)
                return carry

            lax.fori_loop(0, 2, half, 0)

    def put_small(self, h, start, value):
        ref = self.w[SMALL]
        ref[h, :, :, :, :, start : start + value.shape[1]] = value.astype(BF16).reshape(
            *ref.shape[1:-1], value.shape[1]
        )

    def small_grads(self):
        rows = jnp.concatenate([self.norm_grad[...], jnp.zeros((128 - self.norm_grad.shape[0], 2 * self.half), F32)], 0)
        columns = jnp.transpose(rows)
        for h in range(2):
            self.put_small(h, 2 * self.sizes.embed_half, columns)

    def self_attention_back(self):
        def pair(p, rows):
            q, k, v = ([self.t[self.q + 2 * m + h, rows, lanes] for h, lanes in self.couples()] for m in range(3))
            d = [self.t[self.da + h, rows, lanes] for h, lanes in self.couples()]
            for m, values in enumerate(self.attention_back(p, q, k, v, d, self.p1, TEXT_PAD)):
                self.put_couples(self.t, self.q + 2 * m, rows, values)

        self.text_loop(pair)
        for h in range(2):
            self.t[self.db_t + h] = jnp.transpose(self.t[self.x + h])

    def self_projection_back(self, k):
        slot = (QUERY, KEY, VALUE)[k]

        def half(h, carry):
            d = self.t[self.q + 2 * k + h]
            self.z[...] += nt(d, self.weight(slot, h))
            self.grads(slot, h, self.db_t, d)
            return carry

        lax.fori_loop(0, 2, half, 0)

    def text_out(self):
        def moves(p):
            src, dst = self.text_stage.at[p % 2], self.text_out_ref.at[self.place.mp, p]
            own = pltpu.make_async_copy(src, dst, self.text_own.at[p])
            return own, remote(src, dst, self.text_send.at[p], self.text_recv.at[p], self.place.peer())

        def done(p):
            own, give = moves(p)
            own.wait()
            give.wait_send()

        pairs = self.sizes.pairs
        for p in range(pairs):
            if p >= 2:
                done(p - 2)
            rows = pl.ds(p * TEXT_PAD, TEXT_PAD)
            value = self.z[rows, :] + self.extra[0, p : p + 1, :]
            self.text_stage[p % 2] = value[: self.sizes.length]
            for move in moves(p):
                move.start()

        def end():
            for p in range(max(pairs - 2, 0), pairs):
                done(p)
            for p in range(pairs):
                moves(p)[1].wait_recv()

        self.ends.append(end)


    def gather_to_peer(self, c, name, order, buf):
        mine, other = buf.at[self.place.mp], buf.at[1 - self.place.mp]
        sent = yield from gather_steps(self.place, order, mine, self.g_send.at[c], self.g_recv.at[c])

        def copy(ref):
            return remote(ref, ref, self.gp_send.at[c], self.gp_recv.at[c], self.place.peer())

        copy(mine).start()
        yield
        copy(other).wait_recv()
        self.sending[name] = sent + [(None, lambda: copy(mine))]

    def gather(self, c, name, order):
        buf = self.w[name]
        for copy in self.own_copies(c, name):
            copy.start()
        if name == SMALL:
            self.place_norms()
        yield
        for copy in self.own_copies(c, name):
            copy.wait()
        yield from self.gather_to_peer(c, name, order, buf)

    def gather_embeddings(self, c, order):
        self.emb[(self.place.mp,) + self.place.pos] = self.own_emb[...]
        yield from self.gather_to_peer(c, EMBEDDINGS, order, self.emb)

    def settle(self, names):
        for name in names:
            wait_sent(self.sending.pop(name))

    def credit(self, slot, give):
        place = self.place

        def act(index, device):
            sem = self.credits.at[slot, index]
            if give:
                pl.semaphore_signal(sem, inc=1, device_id=device, device_id_type=MESH)
            else:
                pl.semaphore_wait(sem, 1)

        for axis in range(3):
            length, pos = place.dims[axis], place.pos[axis]
            if length > 1:
                pl.when(pos > 0)(lambda: act(2 * axis + (1 if give else 0), place.at(axis, pos - 1)))
                pl.when(pos < length - 1)(lambda: act(2 * axis + (0 if give else 1), place.at(axis, pos + 1)))

    def peer_credit(self, slot, give):
        sem = self.peer_credits.at[slot]
        if give:
            pl.semaphore_signal(sem, inc=1, device_id=self.place.peer(), device_id_type=MESH)
        else:
            pl.semaphore_wait(sem, 1)

    def image_credit(self):
        self.credit(ARRIVE_RING, True)
        self.peer_credit(PEER_RING, True)

    def spare(self, at, units, rows):
        blocks = self.u.at[pl.ds(at, 2)].reshape(-1, rows, self.half)
        return blocks.at[pl.ds(0, units)]

    def scatter(self, c, turn, name, order, total):
        buf, ringed = self.w[name], name != IMAGE
        mine, other = buf.at[self.place.mp], buf.at[1 - self.place.mp]
        if ringed:
            peer_slot, slot = turn % PEER_RING, turn % ARRIVE_RING
            peer_in, arrive = self.peer_in.at[peer_slot], self.arrive.at[slot]
        else:
            peer_slot, slot = PEER_RING, ARRIVE_RING
            peer_in = self.spare(0, math.prod(self.dims), buf.shape[-2]).reshape(*buf.shape[1:])
            arrive = self.spare(2, arrive_units(self.dims, order), buf.shape[-2])

        def copy():
            return remote(other, peer_in, self.sp_send.at[peer_slot], self.sp_recv.at[peer_slot], self.place.peer())

        if not ringed or turn >= PEER_RING:
            self.peer_credit(peer_slot, False)
        wait_sent(self.peer_sent.pop(peer_slot, ()))
        copy().start()
        self.peer_sent[peer_slot] = [(None, copy)]
        yield
        copy().wait_recv()
        mine[...] = mine[...] + peer_in[...]
        if ringed and turn + PEER_RING < total:
            self.peer_credit(peer_slot, True)
        if not ringed or turn >= ARRIVE_RING:
            self.credit(slot, False)
        wait_sent(self.ring_sent.pop(slot, ()))
        result = self.results[name]
        target = result.at[self.place.mp] if len(result.shape) == 3 else result
        sent = yield from scatter_steps(
            self.place, order, mine, arrive, self.s_send.at[slot], self.s_recv.at[slot], target
        )
        if ringed and turn + ARRIVE_RING < total:
            self.credit(slot, True)
        self.ring_sent[slot] = sent
        if len(result.shape) == 3:

            def hand(half):
                ref = result.at[half]
                return remote(ref, ref, self.h_send.at[int(name == IMAGE)], self.h_recv.at[int(name == IMAGE)], self.place.peer())

            hand(self.place.mp).start()
            yield
            hand(1 - self.place.mp).wait_recv()
            self.sent.append((None, lambda: hand(self.place.mp)))

    def joined_over(self):
        stage, whole = self.joined, self.joined_out
        own = pltpu.make_async_copy(stage, whole.at[self.place.mp], self.out_own)
        give = remote(stage, whole.at[self.place.mp], self.out_send, self.out_recv, self.place.peer())
        own.start()
        give.start()
        self.ends += [own.wait, give.wait]


IMAGE, QUERY, KEY, VALUE, SMALL, ATTN_OUT, CROSS_KEY, CROSS_VALUE, CROSS_QUERY, CROSS_OUT, FFN = range(11)
EMBEDDINGS = -1


def grad_order(hidden_blocks):
    ffn = (*range(FFN + hidden_blocks, FFN + 2 * hidden_blocks), *range(FFN, FFN + hidden_blocks))
    return ffn + (CROSS_OUT, CROSS_QUERY, CROSS_KEY, CROSS_VALUE, IMAGE, ATTN_OUT, SMALL, QUERY, KEY, VALUE)


class Timeline:
    def __init__(self):
        self.events = []

    def add(self, time, fn):
        self.events.append((time, len(self.events), fn))

    def add_steps(self, times, steps):
        last = [False]

        def advance():
            if not last[0]:
                try:
                    next(steps)
                except StopIteration:
                    last[0] = True

        for time in times:
            self.add(time, advance)

    def run(self):
        for _, _, fn in sorted(self.events, key=lambda e: e[:2]):
            fn()


CHUNK = 3.9
KINDS = ((2, 0, 1), (1, 0, 2), (0, 2, 1), (0, 1, 2), (2, 1, 0), (1, 2, 0))

GATHER_KINDS = (2, 1, 2, 1, 3, 2, 1, 0, 0, 3, 2, 1, 0, 1, 2, 3, 0, 1)
GATHER_START = (0.0, 35.78, 9.14, 7.29, 8.49, 34.08, 32.19, 18.67, 13.4, 23.56, 64.34, 62.53, 73.03, 62.92, 87.05, 47.64, 73.57, 73.11)
GATHER_STEPS = (
    (0.0, 9.86, 19.46, 20.54, 44.84, 69.22, 77.55),
    (0.0, 9.5, 18.16, 25.51, 36.27, 56.29, 63.23),
    (0.0, 4.91, 13.38, 28.77, 37.2, 65.33, 87.19),
    (0.0, 20.6, 34.85, 38.31, 50.92, 77.49, 86.82),
    (0.0, 2.0, 14.0, 20.51, 31.8, 45.01, 50.55),
    (0.0, 10.96, 15.65, 18.67, 37.8, 45.42, 88.59),
    (0.0, 36.34, 39.98, 42.92, 45.73, 67.89, 69.96),
    (0.0, 12.35, 52.03, 62.19, 68.96, 91.36, 91.73),
    (0.0, 48.13, 60.52, 77.82, 83.43, 113.81, 119.75),
    (0.0, 26.68, 32.47, 48.62, 62.07, 91.48, 127.96),
    (0.0, 12.23, 15.22, 26.74, 57.19, 75.56, 109.53),
    (0.0, 20.34, 32.76, 43.48, 47.67, 108.99, 138.63),
    (0.0, 20.85, 35.36, 60.72, 72.87, 115.45, 141.33),
    (0.0, 26.1, 44.43, 60.04, 73.87, 147.49, 156.02),
    (0.0, 9.02, 14.88, 21.06, 39.31, 105.07, 131.21),
    (0.0, 6.63, 26.12, 35.19, 66.26, 164.18, 194.81),
    (0.0, 37.17, 73.98, 78.09, 99.34, 152.56, 170.68),
    (0.0, 30.29, 50.44, 98.38, 99.94, 169.35, 241.95),
)
EMBED_STEPS = (0.0, 8.91, 16.59, 27.36, 29.51, 45.31, 65.65)
SCATTER_KINDS = (0, 1, 0, 1, 3, 2, 3, 2, 1, 3, 0, 0, 1, 2, 1, 2, 2, 3)
SCATTER_GAPS = (191.0, 0.0, 5.73, 2.04, 0.46, 0.0, 7.0, 4.69, 0.0, 4.57, 0.08, 3.68, 7.84, 0.0, 3.15, 0.0, 21.45, 10.42)
SCATTER_STEPS = (
    (0.0, 4.04, 12.95, 23.87, 32.6, 36.14, 42.79),
    (0.0, 3.0, 16.04, 20.81, 25.89, 31.51, 36.95),
    (0.0, 1.97, 9.58, 17.57, 26.02, 34.36, 45.87),
    (0.0, 1.34, 11.81, 18.03, 25.35, 32.29, 46.72),
    (0.0, 5.46, 23.87, 29.46, 35.73, 45.62, 73.83),
    (0.0, 4.56, 17.74, 24.03, 29.36, 35.29, 63.7),
    (0.0, 5.03, 14.62, 19.72, 24.8, 28.81, 109.64),
    (0.0, 2.85, 10.48, 21.98, 25.03, 54.32, 92.15),
    (0.0, 6.97, 13.67, 20.43, 25.72, 77.02, 206.52),
    (0.0, 12.41, 21.43, 58.18, 71.76, 81.1, 168.25),
    (0.0, 3.91, 15.0, 16.25, 21.35, 24.72, 121.97),
    (0.0, 8.0, 14.81, 21.25, 76.96, 144.83, 236.56),
    (0.0, 2.83, 11.79, 24.73, 61.73, 150.58, 197.54),
    (0.0, 2.49, 11.12, 55.01, 102.76, 109.24, 203.32),
    (0.0, 3.22, 41.46, 48.01, 73.25, 126.87, 208.6),
    (0.0, 3.06, 48.3, 102.56, 113.82, 171.84, 210.86),
    (0.0, 19.43, 79.99, 83.8, 142.14, 167.44, 256.6),
    (0.0, 1.16, 68.62, 72.95, 111.24, 153.3, 212.93),
)
PACE = 1.058


class Plan:
    def __init__(self, dims, count):
        self.dims = dims
        self.tabled = dims == (4, 2, 2) and count == len(GATHER_START)
        self.gather_kinds = GATHER_KINDS if self.tabled else [k % 2 for k in range(count)]
        self.scatter_kinds = SCATTER_KINDS if self.tabled else [k % 2 for k in range(count)]
        self.gaps = SCATTER_GAPS if self.tabled else [CHUNK] * count
        self.pace = PACE if self.tabled else 1.0

    def steps(self, order, back):
        units = [math.prod(self.dims[a] for a in order[:k]) for k in range(3) for _ in range(self.dims[order[k]] - 1)]
        times = [0.0, 3.0] if back else [0.0]
        for unit in reversed(units) if back else units:
            times.append(times[-1] + 1.6 * unit + 3.0)
        return times if back else times + [times[-1] + 4.0]

    def gather(self, c):
        kind = self.gather_kinds[c]
        if self.tabled:
            return KINDS[kind], [GATHER_START[c] + t for t in GATHER_STEPS[c]]
        return KINDS[kind], [CHUNK * c + t for t in self.steps(KINDS[kind], False)]

    def scatter(self, c):
        kind = self.scatter_kinds[c]
        return KINDS[kind], SCATTER_STEPS[c] if self.tabled else self.steps(KINDS[kind], True)

    def embeddings(self, start):
        order = (2, 1, 0)
        return order, [start + t for t in (EMBED_STEPS if self.tabled else self.steps(order, False))]


def fused_kernel(dims, sizes, refs):
    layer = Layer(dims, sizes, refs)
    blocks = sizes.hidden_blocks
    layer.sent, layer.ends, layer.sending, layer.ring_sent, layer.peer_sent = [], [], {}, {}, {}
    timeline = Timeline()

    layer.load()
    layer.own_emb[...] = jnp.zeros_like(layer.own_emb)
    ready = {}
    plan = Plan(dims, FFN + 2 * blocks)
    for c, name in enumerate(range(FFN + 2 * blocks)):
        order, times = plan.gather(c)
        timeline.add_steps([-1.0] + times, layer.gather(c, name, order))
        ready[name] = times[-1]
    timeline.add(-0.5, lambda: greet_lines(layer.place))

    clock = [0.0]

    def compute(fn, cost, *needs):
        clock[0] = max([clock[0] + 0.001] + [ready[n] + 0.01 for n in needs])
        timeline.add(clock[0], fn)
        clock[0] += cost * plan.pace
        return clock[0]

    compute(layer.take_patches, 3.0)
    compute(layer.take_text, 0.5)
    compute(layer.image_features, 1.6, IMAGE)
    compute(layer.region, 0.8)
    compute(layer.take_cotangent, 0.5)
    compute(layer.self_projections, 2.0, QUERY, KEY, VALUE)
    compute(layer.self_attention, 4.0)
    compute(layer.norm_params, 0.2, SMALL)
    compute(layer.pools, 0.3)
    start = compute(layer.embed, 0.3)
    order, times = plan.embeddings(start)
    timeline.add_steps(times, layer.gather_embeddings(len(ready), order))
    ready[EMBEDDINGS] = times[-1]
    compute(layer.after_self, 2.7, ATTN_OUT)
    compute(layer.make_keys, 2.3, CROSS_KEY)
    compute(layer.make_values, 2.3, CROSS_VALUE)
    compute(layer.cross_query, 0.6, CROSS_QUERY)
    compute(layer.cross_attention, 4.5)
    compute(layer.after_cross, 2.0, CROSS_OUT)
    compute(lambda: layer.settle([SMALL]), 0.0, EMBEDDINGS)
    compute(layer.contrast, 4.0)
    for k in range(blocks):
        compute(functools.partial(layer.ffn_in, k), 1.6, FFN + k)
    for k in range(blocks):
        compute(functools.partial(layer.ffn_out, k), 1.0, FFN + blocks + k)

    done = {}
    compute(layer.output_and_back, 4.0)
    compute(lambda: layer.settle(list(layer.sending)), 0.0)
    compute(layer.joined_over, 0.1)
    for k in range(blocks):
        done[FFN + blocks + k] = compute(functools.partial(layer.ffn_out_back, k), 2.2)
    for k in range(blocks):
        done[FFN + k] = compute(functools.partial(layer.ffn_in_back, k), 1.9)
    compute(functools.partial(layer.back_through_norm, 1), 1.8)
    done[CROSS_OUT] = compute(lambda: layer.branch_back(CROSS_OUT, layer.a2), 1.8)
    compute(layer.cross_attention_back, 5.0)
    done[CROSS_QUERY] = compute(layer.cross_query_back, 1.5)
    compute(layer.image_back, 5.0)
    done[CROSS_KEY] = compute(lambda: layer.cross_key_back(CROSS_KEY, layer.k2), 2.4)
    done[CROSS_VALUE] = compute(lambda: layer.cross_key_back(CROSS_VALUE, layer.v2), 2.4)
    compute(layer.patch_back, 5.5)
    done[IMAGE] = compute(layer.image_weight_back, 2.3)
    compute(layer.image_credit, 0.1)
    compute(functools.partial(layer.back_through_norm, 0), 1.8)
    done[ATTN_OUT] = compute(lambda: layer.branch_back(ATTN_OUT, layer.a1), 1.8)
    done[SMALL] = compute(layer.small_grads, 0.5)
    compute(layer.self_attention_back, 5.0)
    for k, name in enumerate((QUERY, KEY, VALUE)):
        done[name] = compute(functools.partial(layer.self_projection_back, k), 1.5)
    compute(layer.text_out, 2.0)

    start, ends, peer_ends = 0.0, [], []
    for c, name in enumerate(grad_order(blocks)):
        order, steps = plan.scatter(c)
        start = max(start + plan.gaps[c], done[name])
        if name != IMAGE and len(ends) >= PEER_RING:
            start = max(start, peer_ends[len(ends) - PEER_RING] + 0.1)
        if name != IMAGE and len(ends) >= ARRIVE_RING:
            start = max(start, ends[len(ends) - ARRIVE_RING] + 0.1 - steps[1])
        times = [start + 0.02 + t for t in steps]
        if name in (IMAGE, SMALL):
            times.append(times[-1] + 3.0)
        timeline.add_steps(times, layer.scatter(c, len(ends), name, order, sizes.ring_total))
        if name != IMAGE:
            peer_ends.append(times[1])
            ends.append(times[len(steps) - 1])
    timeline.run()
    assert not layer.sending
    for end in layer.ends:
        end()
    for sent in (layer.sent, *layer.ring_sent.values(), *layer.peer_sent.values()):
        wait_sent(sent)
    assert layer.blocks.top <= layer.t.shape[0], layer.blocks.top
    assert layer.wide.top <= layer.u.shape[0], layer.wide.top


def fused_body(
    text,
    patches,
    cotangent,
    region_counts,
    phrase_starts,
    phrase_lengths,
    box_patches,
    query_weight,
    key_weight,
    value_weight,
    attn_out_weight,
    cross_query_weight,
    cross_key_weight,
    cross_value_weight,
    cross_out_weight,
    image_weight,
    ffn_in_weight,
    ffn_out_weight,
    text_embed_weight,
    image_embed_weight,
    *norm_shards,
):
    dims = split_dims(lax.axis_size("dp"))
    mp = lax.axis_index("mp")
    pairs, patch_count, depth = patches.shape
    length, model_width = text.shape[1:]
    half = query_weight.shape[1]
    rows = query_weight.shape[0]
    hidden_blocks = ffn_in_weight.shape[1] // half
    embed_half = text_embed_weight.shape[1] // 2

    slot = jax.ShapeDtypeStruct((rows, half), BF16)
    shards = {name: slot for name in range(FFN + 2 * hidden_blocks)}
    shards[IMAGE] = jax.ShapeDtypeStruct((image_weight.shape[0], half), BF16)
    whole = {
        IMAGE: image_weight,
        QUERY: query_weight,
        KEY: key_weight,
        VALUE: value_weight,
        ATTN_OUT: attn_out_weight.T,
        CROSS_KEY: cross_key_weight,
        CROSS_VALUE: cross_value_weight,
        CROSS_QUERY: cross_query_weight,
        CROSS_OUT: cross_out_weight.T,
    }
    order = range(FFN + 2 * hidden_blocks)
    sizes = types.SimpleNamespace(
        pairs=pairs,
        length=length,
        patch_count=patch_count,
        half=half,
        hidden_blocks=hidden_blocks,
        embed_half=embed_half,
        ring_total=len(order) - 1,
    )
    count, text_rows, patch_rows = len(order), pairs * TEXT_PAD, pairs * PATCH_PAD
    couples = model_width // 128
    anywhere, vmem = pl.BlockSpec(memory_space=pl.ANY), pl.BlockSpec(memory_space=pltpu.VMEM)

    inputs = dict(
        text_in=(text, anywhere),
        cot_in=(cotangent, anywhere),
        patches_in=(patches, anywhere),
        ffn_in_all=(ffn_in_weight, anywhere),
        ffn_out_all=(ffn_out_weight.T, anywhere),
        text_embed=(text_embed_weight, anywhere),
        image_embed=(image_embed_weight, anywhere),
        counts=(region_counts.reshape(1, -1), vmem),
        starts=(phrase_starts.T, vmem),
        lengths=(phrase_lengths.T, vmem),
        picks=(box_patches, vmem),
    )
    outputs = dict(
        joined_out=(jax.ShapeDtypeStruct((2, pairs, length, model_width), BF16), anywhere),
        text_out_ref=(jax.ShapeDtypeStruct((2, pairs, length, model_width), F32), anywhere),
        patch_grad=(jax.ShapeDtypeStruct((pairs, patch_count, depth), F32), anywhere),
    )
    result_shapes = []
    for name in order:
        shape = shards[name].shape
        result_shapes.append(jax.ShapeDtypeStruct(((2,) if name in (IMAGE, SMALL) else ()) + shape, F32))
    units = max(arrive_units(dims, o) for o in KINDS[:4])
    dma, regular = pltpu.SemaphoreType.DMA, pltpu.SemaphoreType.REGULAR
    scratch = dict(
        t=pltpu.VMEM((42, text_rows, half), BF16),
        u=pltpu.VMEM((8, patch_rows, half), BF16),
        patches=pltpu.VMEM((patch_rows, depth), BF16),
        p1=pltpu.VMEM((pairs, couples * TEXT_PAD, 2 * TEXT_PAD), BF16),
        p2=pltpu.VMEM((pairs, couples * TEXT_PAD, 2 * PATCH_PAD), BF16),
        z=pltpu.VMEM((text_rows, model_width), F32),
        hid=pltpu.VMEM((text_rows, model_width), F32),
        inv=pltpu.VMEM((2, text_rows, 1), F32),
        norms=pltpu.VMEM((8, model_width), F32),
        norm_grad=pltpu.VMEM((8, model_width), F32),
        pool=pltpu.VMEM((2, 16, model_width), F32),
        raw=pltpu.VMEM((2, 16, 2 * embed_half), F32),
        own_emb=pltpu.VMEM((16, 4 * embed_half), BF16),
        emb=pltpu.VMEM((2,) + dims + (16, 4 * embed_half), BF16),
        extra=pltpu.VMEM((2, 16, model_width), F32),
        chosen=pltpu.VMEM((pairs, 8, PATCH_PAD), F32),
        span=pltpu.VMEM((pairs, 8, TEXT_PAD), F32),
        regions=pltpu.VMEM((pairs, 8, model_width), F32),
        joined=pltpu.VMEM((pairs, length, model_width), BF16),
        text_stage=pltpu.VMEM((2, length, model_width), F32),
        patch_in=pltpu.VMEM((2, patch_count, depth), BF16),
        patch_stage=pltpu.VMEM((2, pairs // 2, patch_count, 256), F32),
        peer_in=pltpu.VMEM((PEER_RING,) + dims + (rows, half), BF16),
        arrive=pltpu.VMEM((ARRIVE_RING, units, rows, half), BF16),
        load_sem=dma((2,)),
        own_sem=dma((count + 1,)),
        g_send=dma((count + 1, send_slots(dims))),
        g_recv=dma((count + 1, gather_slots(dims))),
        gp_send=dma((count + 1,)),
        gp_recv=dma((count + 1,)),
        s_send=dma((ARRIVE_RING + 1, send_slots(dims))),
        s_recv=dma((ARRIVE_RING + 1, sum_slots(dims))),
        sp_send=dma((PEER_RING + 1,)),
        sp_recv=dma((PEER_RING + 1,)),
        h_send=dma((2,)),
        h_recv=dma((2,)),
        out_own=dma,
        out_send=dma,
        out_recv=dma,
        text_own=dma((pairs,)),
        text_send=dma((pairs,)),
        text_recv=dma((pairs,)),
        patch_sem=dma((2,)),
        credits=regular((ARRIVE_RING + 1, 6)),
        peer_credits=regular((PEER_RING + 1,)),
    )
    weights = [pltpu.VMEM((2,) + dims + shards[name].shape, BF16) for name in order]

    def kernel(*refs):
        refs = list(refs)

        def some(names):
            part = dict(zip(names, refs))
            del refs[: len(part)]
            return part

        table = some(inputs)
        table.update(norm_in=some(range(len(norm_shards))))
        table.update(shards=some(whole))
        table.update(some(outputs))
        table.update(results=some(order))
        table.update(some(scratch))
        table.update(w=some(order))
        fused_kernel(dims, sizes, table)

    results = pl.pallas_call(
        kernel,
        out_shape=[s for s, _ in outputs.values()] + result_shapes,
        in_specs=[spec for _, spec in inputs.values()] + [vmem] * len(norm_shards) + [anywhere] * len(whole),
        out_specs=[spec for _, spec in outputs.values()] + [vmem] * count,
        scratch_shapes=list(scratch.values()) + weights,
        compiler_params=pltpu.CompilerParams(
            collective_id=2, has_side_effects=True, vmem_limit_bytes=64 * 2**20
        ),
        name="layer",
    )(*[x for x, _ in inputs.values()], *[n.reshape(1, -1) for n in norm_shards], *whole.values())
    return finish(results, sizes, dims, model_width)


def finish_kernel(sizes, count, joined, text_grad, patch_grad, *refs):
    blocks, half, width = sizes.hidden_blocks, sizes.half, sizes.embed_half
    own, outs = refs[:count], refs[count : count + 22]
    stage_joined, stage_text, stage_patch = refs[count + 22 : count + 25]
    stages, (in_sem, out_sem) = refs[count + 25 : -2], refs[-2:]
    small = stages[SMALL]
    pieces = []
    for src, stage, dst in ((joined, stage_joined, outs[0]), (text_grad, stage_text, outs[1])):
        pieces += [(src.at[k], stage.at[k], [(stage.at[k], dst.at[k])]) for k in range(2)]
    pieces += [
        (patch_grad.at[p], stage_patch.at[p], [(stage_patch.at[p], outs[2].at[p])]) for p in range(sizes.pairs)
    ]
    singles = (QUERY, KEY, VALUE, ATTN_OUT, CROSS_QUERY, CROSS_KEY, CROSS_VALUE, CROSS_OUT)
    for name in range(count):
        stage = stages[name]
        if name in singles:
            moves = [(stage, outs[3 + singles.index(name)])]
        elif name == IMAGE:
            moves = [(stage.at[k], outs[11].at[:, pl.ds(k * half, half)]) for k in range(2)]
        elif name == SMALL:
            moves = [
                (stage.at[k, :, pl.ds(j * width, width)], outs[14 + j].at[:, pl.ds(k * width, width)])
                for k in range(2)
                for j in range(2)
            ]
        else:
            out = outs[12] if name < FFN + blocks else outs[13]
            moves = [(stage, out.at[:, pl.ds((name - FFN) % blocks * half, half)])]
        pieces.append((own[name], stage, moves))
    into = [pltpu.make_async_copy(src, stage, in_sem.at[k]) for k, (src, stage, _) in enumerate(pieces)]
    for copy in into:
        copy.start()
    back = []
    for copy, (_, _, moves) in zip(into, pieces):
        copy.wait()
        for src, dst in moves:
            back.append(pltpu.make_async_copy(src, dst, out_sem.at[len(back)]))
            back[-1].start()
    rows = jnp.transpose(small[lax.axis_index("mp")][:, 2 * width :])
    for k in range(6):
        outs[16 + k][...] = rows[k : k + 1]
    for copy in back:
        copy.wait()


def finish(results, sizes, dims, model_width):
    anywhere, vmem = pl.BlockSpec(memory_space=pl.ANY), pl.BlockSpec(memory_space=pltpu.VMEM)
    own = results[3:]
    rows, half, width, blocks = own[QUERY].shape[0], sizes.half, sizes.embed_half, sizes.hidden_blocks
    shapes = [r.shape for r in results[:3]] + [(rows, half)] * 8
    shapes += [(own[IMAGE].shape[1], 2 * half)] + [(rows, blocks * half)] * 2 + [(rows, 2 * width)] * 2 + [(1, rows)] * 6
    types = [BF16] + [F32] * (len(shapes) - 1)
    outs = pl.pallas_call(
        functools.partial(finish_kernel, sizes, len(own)),
        out_shape=[jax.ShapeDtypeStruct(s, t) for s, t in zip(shapes, types)],
        in_specs=[anywhere] * len(results),
        out_specs=[anywhere] * 16 + [vmem] * 6,
        scratch_shapes=[pltpu.VMEM(r.shape, r.dtype) for r in results]
        + [
            pltpu.SemaphoreType.DMA((4 + sizes.pairs + len(own),)),
            pltpu.SemaphoreType.DMA((4 + sizes.pairs + len(own) + 4,)),
        ],
        compiler_params=pltpu.CompilerParams(vmem_limit_bytes=60 * 2**20),
        name="results",
    )(*results)
    whole = (2 * sizes.pairs, sizes.length, model_width)
    turned = (6, 10, 13)
    done = [outs[0].reshape(whole), outs[1].reshape(whole), *outs[2:16]]
    done = [x.T if k in turned else x for k, x in enumerate(done)]
    return (*done, *(x.reshape(-1) for x in outs[16:]))


def pad_rows(x, rows):
    return jnp.pad(x, ((0, rows - x.shape[0]), (0, 0)))


def body(
    text,
    patches,
    cotangent,
    region_counts,
    phrase_starts,
    phrase_lengths,
    box_patches,
    query_weight,
    key_weight,
    value_weight,
    attn_out_weight,
    cross_query_weight,
    cross_key_weight,
    cross_value_weight,
    cross_out_weight,
    image_weight,
    ffn_in_weight,
    ffn_out_weight,
    text_embed_weight,
    image_embed_weight,
    *norm_shards,
):
    dp = lax.axis_size("dp")
    dims = split_dims(dp)
    mp = lax.axis_index("mp")
    half_pairs, patch_count, _ = patches.shape
    length, model_width = text.shape[1:]
    half = query_weight.shape[1]
    rows = query_weight.shape[0]
    hidden_blocks = ffn_in_weight.shape[1] // half
    embed_half = text_embed_weight.shape[1] // 2
    image_rows_own = image_weight.shape[0]

    if rows % 16 == 0 and dims[0] % 2 == 0 and half % 128 == 0 and half == model_width // 2 and half_pairs % 2 == 0:
        return fused_body(
            text, patches, cotangent, region_counts, phrase_starts, phrase_lengths, box_patches,
            query_weight, key_weight, value_weight, attn_out_weight, cross_query_weight, cross_key_weight,
            cross_value_weight, cross_out_weight, image_weight, ffn_in_weight, ffn_out_weight,
            text_embed_weight, image_embed_weight, *norm_shards,
        )

    def own_half(x, size, dim):
        return lax.dynamic_slice_in_dim(x, mp * size, size, dim)

    text, cotangent = own_half(text, half_pairs, 0), own_half(cotangent, half_pairs, 0)
    region_counts, phrase_starts = own_half(region_counts, half_pairs, 0), own_half(phrase_starts, half_pairs, 0)
    phrase_lengths, box_patches = own_half(phrase_lengths, half_pairs, 0), own_half(box_patches, half_pairs, 0)

    padded = -(-rows // 16) * 16
    small = jnp.concatenate(
        [own_half(text_embed_weight, embed_half, 1), own_half(image_embed_weight, embed_half, 1)]
        + [jnp.pad(jnp.stack(norm_shards, 1), ((0, 0), (0, half - 2 * embed_half - len(norm_shards))))],
        1,
    )
    ffn_out_t = ffn_out_weight.T
    shards = [
        own_half(image_weight, half, 1),
        query_weight,
        key_weight,
        value_weight,
        attn_out_weight.T,
        small,
        cross_key_weight,
        cross_value_weight,
        cross_query_weight,
        cross_out_weight.T,
        *(ffn_in_weight[:, k * half : (k + 1) * half] for k in range(hidden_blocks)),
        *(ffn_out_t[:, k * half : (k + 1) * half] for k in range(hidden_blocks)),
    ]
    real = [s.shape[0] for s in shards]
    shards = [pad_rows(s, -(-s.shape[0] // 16) * 16) for s in shards]
    gathered = gather(shards, dims)

    def merge(g, n):
        g = g.reshape(2, dp, *g.shape[-2:])[:, :, :n]
        return g.reshape(2, dp * n, g.shape[-1])

    gathered = [merge(g, n) for g, n in zip(gathered, real)]

    def columns(g):
        return jnp.concatenate([g[0], g[1]], 1)

    def blocks(gs):
        return jnp.concatenate([g[0] for g in gs] + [g[1] for g in gs], 1)

    image_w, query_w, key_w, value_w, attn_out_t = (columns(g) for g in gathered[:5])
    embeds = gathered[5]
    text_embed32 = columns(embeds[:, :, :embed_half]).astype(F32)
    image_embed32 = columns(embeds[:, :, embed_half : 2 * embed_half]).astype(F32)
    norms = embeds[0, :, 2 * embed_half : 2 * embed_half + len(norm_shards)].astype(F32).T
    gain_one, bias_one, gain_two, bias_two, gain_three, bias_three = (norms[k] for k in range(6))
    cross_key_w, cross_value_w, cross_query_w, cross_out_t = (columns(g) for g in gathered[6:10])
    ffn_in_w = blocks(gathered[10 : 10 + hidden_blocks])
    ffn_out_tw = blocks(gathered[10 + hidden_blocks :])

    text_rows = text.reshape(half_pairs * length, model_width)
    patch_rows = patches.reshape(half_pairs * patch_count, -1)
    image_rows = matmul(patch_rows, image_w).astype(BF16)
    image32 = image_rows.astype(F32).reshape(half_pairs, patch_count, model_width)
    queries = split_heads(matmul(text_rows, query_w).astype(BF16), half_pairs)
    key_heads = split_heads(matmul(text_rows, key_w).astype(BF16), half_pairs)
    value_heads = split_heads(matmul(text_rows, value_w).astype(BF16), half_pairs)
    self_mixed, self_total = attend(queries, key_heads, value_heads)
    first = text_rows.astype(F32) + contract_cols(self_mixed, attn_out_t)
    hidden_one, normed_one, inv_one = layer_norm(first, gain_one, bias_one)
    low_one = hidden_one.astype(BF16)
    cross_queries = split_heads(matmul(low_one, cross_query_w).astype(BF16), half_pairs)
    cross_keys = split_heads(matmul(image_rows, cross_key_w).astype(BF16), half_pairs)
    cross_values = split_heads(matmul(image_rows, cross_value_w).astype(BF16), half_pairs)
    cross_mixed, cross_total = attend(cross_queries, cross_keys, cross_values)
    second = hidden_one + contract_cols(cross_mixed, cross_out_t)
    hidden_two, normed_two, inv_two = layer_norm(second, gain_two, bias_two)
    low_two = hidden_two.astype(BF16)
    inner = matmul(low_two, ffn_in_w)
    active = jax.nn.gelu(inner, approximate=False).astype(BF16)
    third = hidden_two + contract_cols(active, ffn_out_tw)
    output, normed_three, inv_three = layer_norm(third, gain_three, bias_three)
    output3 = output.reshape(half_pairs, length, model_width)
    joined = output3.astype(BF16)

    text_pool = jnp.mean(text.astype(F32), 1)
    image_pool = jnp.mean(image32, 1)
    grad_text_embed, grad_image_embed, text_extra, image_pool_grad = contrast(
        text_pool, image_pool, text_embed32, image_embed32
    )
    text_extra = (text_extra / length)[:, None, :]
    image_pool_grad = image_pool_grad / patch_count
    positions = jnp.arange(length, dtype=jnp.int32)
    slots = jnp.arange(phrase_starts.shape[1], dtype=jnp.int32)
    valid = (slots[None, :] < region_counts[:, None]).astype(F32)
    ends = phrase_starts + phrase_lengths
    inside = ((positions >= phrase_starts[..., None]) & (positions < ends[..., None])).astype(F32) * valid[..., None]
    span_weight = inside / phrase_lengths[..., None].astype(F32)
    chosen = (
        jnp.sum((box_patches[..., None] == jnp.arange(patch_count, dtype=jnp.int32)).astype(F32), axis=2)
        / box_patches.shape[2]
    )
    phrase = jnp.einsum("pbt,ptd->pbd", span_weight, output3, precision=HIGHEST)
    region = jnp.einsum("pbn,pnd->pbd", chosen, image32, precision=HIGHEST)
    mismatch = (phrase - region) * valid[..., None]
    box_text = jnp.einsum("pbt,pbd->ptd", span_weight, mismatch, precision=HIGHEST)
    box_image = -jnp.einsum("pbn,pbd->pnd", chosen, mismatch, precision=HIGHEST)
    image_extra = (box_image + image_pool_grad[:, None, :]).reshape(-1, model_width)

    upstream = cotangent.astype(F32).reshape(-1, model_width) + box_text.reshape(-1, model_width)
    grad_third, gain_three_grad, bias_three_grad = norm_back(upstream, normed_three, inv_three, gain_three)
    low_third = grad_third.astype(BF16)
    grad_ffn_out_t = contract_rows(low_third, active)
    dactive = matmul(low_third, ffn_out_tw)
    gelu_pull = jax.vjp(lambda values: jax.nn.gelu(values, approximate=False), inner)[1]
    dinner = gelu_pull(dactive)[0].astype(BF16)
    grad_ffn_in = contract_rows(low_two, dinner)
    grad_second = grad_third + contract_cols(dinner, ffn_in_w)
    grad_second, gain_two_grad, bias_two_grad = norm_back(grad_second, normed_two, inv_two, gain_two)
    low_second = grad_second.astype(BF16)
    grad_cross_out_t = contract_rows(low_second, cross_mixed)
    dcross = split_heads(matmul(low_second, cross_out_t).astype(BF16), half_pairs)
    dqueries, dkeys, dvalues = attend_back(cross_queries, cross_keys, cross_values, cross_total, dcross)
    grad_cross_query = contract_rows(low_one, dqueries)
    grad_first = grad_second + contract_cols(dqueries, cross_query_w)
    grad_cross_key = contract_rows(image_rows, dkeys)
    grad_cross_value = contract_rows(image_rows, dvalues)
    dimage = contract_cols(dkeys, cross_key_w) + contract_cols(dvalues, cross_value_w) + image_extra
    low_image = dimage.astype(BF16)
    grad_image = contract_rows(patch_rows, low_image)
    patch_grad = contract_cols(low_image, image_w).reshape(patches.shape)
    grad_first, gain_one_grad, bias_one_grad = norm_back(grad_first, normed_one, inv_one, gain_one)
    low_first = grad_first.astype(BF16)
    grad_attn_out_t = contract_rows(low_first, self_mixed)
    dself = split_heads(matmul(low_first, attn_out_t).astype(BF16), half_pairs)
    dqueries, dkeys, dvalues = attend_back(queries, key_heads, value_heads, self_total, dself)
    grad_query = contract_rows(text_rows, dqueries)
    grad_key = contract_rows(text_rows, dkeys)
    grad_value = contract_rows(text_rows, dvalues)
    dtext = contract_cols(dqueries, query_w) + contract_cols(dkeys, key_w) + contract_cols(dvalues, value_w)
    text_grad = (grad_first + dtext).reshape(half_pairs, length, model_width) + text_extra

    def halves(g):
        g = g.astype(BF16)
        return jnp.stack([g[:, :half], g[:, half:]], 0)

    def hidden_halves(g):
        g = g.astype(BF16)
        return [
            jnp.stack([g[:, k * half : (k + 1) * half], g[:, (hidden_blocks + k) * half : (hidden_blocks + k + 1) * half]])
            for k in range(hidden_blocks)
        ]

    norm_grads = jnp.stack(
        [gain_one_grad, bias_one_grad, gain_two_grad, bias_two_grad, gain_three_grad, bias_three_grad], 1
    ).astype(BF16)
    norm_grads = jnp.pad(norm_grads, ((0, 0), (0, half - 2 * embed_half - len(norm_shards))))
    text_half, image_half = grad_text_embed.astype(BF16), grad_image_embed.astype(BF16)
    small_grads = jnp.stack(
        [
            jnp.concatenate(
                [text_half[:, k * embed_half : (k + 1) * embed_half], image_half[:, k * embed_half : (k + 1) * embed_half], norm_grads], 1
            )
            for k in range(2)
        ]
    )
    grads = [
        *hidden_halves(grad_ffn_out_t),
        *hidden_halves(grad_ffn_in),
        halves(grad_cross_out_t),
        halves(grad_cross_query),
        halves(grad_cross_key),
        halves(grad_cross_value),
        halves(grad_image),
        halves(grad_attn_out_t),
        halves(grad_query),
        halves(grad_key),
        halves(grad_value),
        small_grads,
    ]
    shared = (2 * hidden_blocks + 4, len(grads) - 1)

    def cut(g):
        n = g.shape[1] // dp
        g = g.reshape(2, dp, n, g.shape[-1])
        g = jnp.pad(g, ((0, 0), (0, 0), (0, -(-n // 16) * 16 - n), (0, 0)))
        return g.reshape(2, *dims, *g.shape[-2:])

    results = scatter([cut(g) for g in grads], shared, (joined, text_grad), dims)
    joined_all, text_grad_all = (r.reshape(2 * half_pairs, length, model_width) for r in results[len(grads) :])
    sums = [r[..., :n, :] for r, n in zip(results, [g.shape[1] // dp for g in grads])]
    ffn_out_own = jnp.concatenate(sums[:hidden_blocks], 1).T
    ffn_in_own = jnp.concatenate(sums[hidden_blocks : 2 * hidden_blocks], 1)
    cross_out_own, cross_query_own, cross_key_own, cross_value_own, image_own, attn_out_own, query_own, key_own, value_own, small_own = sums[2 * hidden_blocks :]
    own_norm = lax.dynamic_index_in_dim(small_own, mp, 0, keepdims=False)[:, 2 * embed_half :]
    return (
        joined_all,
        text_grad_all,
        patch_grad,
        query_own,
        key_own,
        value_own,
        attn_out_own.T,
        cross_query_own,
        cross_key_own,
        cross_value_own,
        cross_out_own.T,
        jnp.concatenate([image_own[0], image_own[1]], 1),
        ffn_in_own,
        ffn_out_own,
        jnp.concatenate([small_own[0, :, :embed_half], small_own[1, :, :embed_half]], 1),
        jnp.concatenate([small_own[0, :, embed_half : 2 * embed_half], small_own[1, :, embed_half : 2 * embed_half]], 1),
        own_norm[:, 0],
        own_norm[:, 1],
        own_norm[:, 2],
        own_norm[:, 3],
        own_norm[:, 4],
        own_norm[:, 5],
    )


def solution(mesh):
    pairs, weight, turned, single = P("dp", None, None), P("dp", "mp"), P("mp", "dp"), P("dp", None)
    weights = (weight, weight, weight, turned, weight, weight, weight, turned, single, weight, turned, single, single)
    norms = (P("dp"),) * 6
    halves = P(("dp", "mp"), None, None)
    in_specs = (pairs, halves, pairs, P("dp"), single, single, pairs) + weights + norms
    out_specs = (pairs, pairs, halves) + weights + norms
    return jax.shard_map(body, mesh=mesh, in_specs=in_specs, out_specs=out_specs, check_vma=False)
```
